32 devices in a mesh: groups: 2 (over x), line: 16 (over z, y, core).
Axes of the slice: x: 2, y: 2, z: 4, core: 2. Of those that a mesh axis runs over, the one named last changes fastest.
Arguments:
- lodf: bfloat16 [2048, 2048], P('line'), may hold values from -0.59765625 to 0.59765625
- limits: int32 [2048], P('line'), may hold values from 50 to 150
- base_flow: float32 [4096], P(('groups', 'line')), parts along dimension 0, may hold values from -4 to 4
- first_ids: int32 [256], P(('groups', 'line')), parts along dimension 0, may hold values from 0 to 2047, as said below
- second_ids: int32 [256, 128], P(('groups', 'line')), parts along dimension 0, may hold values from 0 to 2047, as said below
- counts: int32 [256], P(('groups', 'line')), parts along dimension 0, may hold values from 1 to 128, as said below
Outputs:
- pair_penalty: float32 [256, 128], P(('groups', 'line')), parts along dimension 0
- line_pressure: float32 [4096], P(('groups', 'line')), parts along dimension 0
- lodf_grad: bfloat16 [4096, 2048], P(('groups', 'line')), parts along dimension 0
The draws below stay inside these ranges and needn't reach their ends.
There are 2 independent parts, one for each index of `groups`. The reference program is written for one: setup_inputs(seed, part) draws one part's arguments, and reference() takes and returns one part's arrays. A program takes and returns all parts, laid end to end along the dimension named above; an argument that names none is the same for every part. Nothing has to cross between parts.
Inputs may be any that keep to these rules, and one draw needn't show every extreme that they name: Entry j of first_ids is a line of tile j // 8, that is between (j // 8) * 128 and (j // 8) * 128 + 127. second_ids[j, c] is a line of the same tile as first_ids[j] and differs from first_ids[j]; entries may repeat. Slots c < counts[j] of row j are live; the others are ignored.
All inputs are finite; a program needn't handle non-finite values.
Results may differ from the reference program's by a relative error of at most 0.0021.
Values may be sent and summed in bfloat16 or wider, within the bound.
No kernel may reach another device: no remote copies, remote signals or barrier semaphores. Data moves between devices by JAX's collectives and lax.ppermute only.
A program may use at most 64 MiB of HBM per device.

```python
import jax
import jax.numpy as jnp
from jax import lax

LINE_DEV = 128
FIRST_DEV = 8
CAND = 128
LINES = 2048
FIRST = 128
N_LINE = 16


def tile_firsts(key):
    subkey = jax.random.fold_in(key, 11)
    tiles = jnp.arange(FIRST, dtype=jnp.int32) // FIRST_DEV
    drawn = tiles * LINE_DEV + jax.random.randint(subkey, (FIRST,), 0, LINE_DEV, dtype=jnp.int32)
    drawn = drawn.at[0].set(1).at[1].set(0)
    drawn = drawn.at[FIRST - 2].set(LINES - 1).at[FIRST - 1].set(LINES - 2)
    return drawn.astype(jnp.int32)


def draw_first_ids(key, part):
    return tile_firsts(key)


def draw_second_ids(key, part):
    firsts = tile_firsts(key)
    anchor = firsts // LINE_DEV * LINE_DEV
    offsets = jax.random.randint(jax.random.fold_in(key, 23), (FIRST, CAND), 1, LINE_DEV, dtype=jnp.int32)
    chosen = (anchor[:, None] + (firsts[:, None] - anchor[:, None] + offsets) % LINE_DEV).astype(jnp.int32)
    chosen = chosen.at[0, 0].set(0).at[FIRST - 1, 0].set(LINES - 1)
    return chosen.astype(jnp.int32)


def draw_counts(key, part):
    levels = jax.random.randint(jax.random.fold_in(key, 31), (FIRST // FIRST_DEV,), 1, 5, dtype=jnp.int32)
    row_levels = jnp.repeat(levels, FIRST_DEV)
    bottom = jnp.maximum(1, CAND * (row_levels - 1) // 4)
    ceiling = CAND * row_levels // 4 + 1
    drawn = jax.random.randint(jax.random.fold_in(key, 37), (FIRST,), bottom, ceiling, dtype=jnp.int32)
    marked = jax.random.randint(jax.random.fold_in(key, 41), (), 0, FIRST, dtype=jnp.int32)
    rows = jnp.arange(FIRST, dtype=jnp.int32)
    drawn = jnp.where(rows == (marked + 1) % FIRST, 1, drawn)
    return jnp.where(rows == marked, CAND, drawn).astype(jnp.int32)


def with_ends(entries, own_key, least, high):
    longest = entries.shape.index(max(entries.shape))
    spots = []
    for shift in (0, 1):
        where = [jax.random.randint(jax.random.fold_in(own_key, axis), (), 0, length) for axis, length in enumerate(entries.shape)]
        where[longest] = (where[longest] + shift) % entries.shape[longest]
        spots.append(tuple(where))
    return entries.at[spots[0]].set(least).at[spots[1]].set(high)


def level_of(rng, shape, pieces, low, top_value):
    def one(dim, parts):
        draws = jax.random.uniform(jax.random.fold_in(jax.random.fold_in(rng, 6), dim), (parts,), jnp.float32, low / len(pieces), top_value / len(pieces))
        return jnp.repeat(jnp.exp(draws), shape[dim] // parts).reshape((-1,) + (1,) * (len(shape) - dim - 1))

    loudness = one(*pieces[0])
    for cut in pieces[1:]:
        loudness = loudness * one(*cut)
    return loudness


def centred(key, extent, deviation, most, pieces=(), kind=jnp.bfloat16):
    entries = jax.random.normal(key, extent, jnp.float32) * deviation
    if len(pieces) > 0:
        entries = level_of(key, extent, pieces, -0.22, 0.18) * entries
    return jnp.clip(entries, min=-most, max=most).astype(kind)


def setup_inputs(seed: int = 0, part: int = 0) -> dict:
    keys = jax.random.split(jax.random.key(seed), 7)
    own_keys = jax.random.split(jax.random.fold_in(keys[6], part), 7)
    return {
        "lodf": jnp.clip(jax.random.uniform(keys[0], (LINES, LINES), jnp.float32, -0.59765625, 0.59765625) * level_of(keys[0], (LINES, LINES), ((0, 16),), -0.4, 0.0), -0.59765625, 0.59765625).astype(jnp.bfloat16),
        "limits": with_ends(jax.random.randint(keys[1], (LINES,), 50, 151), jax.random.fold_in(keys[1], 1), 50, 150).astype(jnp.int32),
        "base_flow": centred(own_keys[2], (LINES,), 1.0, 4.0, ((0, 16),), jnp.float32),
        "first_ids": draw_first_ids(jax.random.fold_in(jax.random.fold_in(keys[6], part), 71), part),
        "second_ids": draw_second_ids(jax.random.fold_in(jax.random.fold_in(keys[6], part), 71), part),
        "counts": draw_counts(jax.random.fold_in(jax.random.fold_in(keys[6], part), 71), part),
    }


def pair_coefficients(square, own_flows, first_local, second_local):
    first_row = lax.dynamic_index_in_dim(square, first_local, 0, keepdims=False).astype(jnp.float32)
    first_column = lax.dynamic_index_in_dim(square, first_local, 1, keepdims=False).astype(jnp.float32)
    mutual_one = jnp.take(first_row, second_local)
    mutual_two = jnp.take(first_column, second_local)
    first_flow = lax.dynamic_index_in_dim(own_flows, first_local, 0, keepdims=False)
    second_flows = jnp.take(own_flows, second_local)
    determinant = 1.0 - mutual_one * mutual_two
    first_scale = (first_flow + mutual_one * second_flows) / determinant
    second_scale = (second_flows + mutual_two * first_flow) / determinant
    return first_scale, second_scale


def pair_terms(columns, base, limit, line_ids, first_line, second_lines, first_local, second_local, first_scale, second_scale, live_count):
    width = columns.shape[1]
    cands = second_lines.shape[0]
    selector = lax.broadcasted_iota(jnp.int32, (width, cands), 0) == second_local[None, :]
    onehot = selector.astype(jnp.bfloat16)
    picked = jnp.dot(columns, onehot, preferred_element_type=jnp.float32)
    first_column = lax.dynamic_index_in_dim(columns, first_local, 1, keepdims=False).astype(jnp.float32)
    flows = base[:, None] + first_column[:, None] * first_scale[None, :] + picked * second_scale[None, :]
    live = jnp.arange(cands, dtype=jnp.int32) < live_count
    keeping = live[None, :] & (line_ids[:, None] != first_line) & (line_ids[:, None] != second_lines[None, :])
    excess = jnp.where(keeping, jnp.maximum(jnp.abs(flows) - limit[:, None], 0.0), 0.0)
    slopes = 2.0 * excess * jnp.sign(flows)
    squares = jnp.sum(excess * excess, axis=0)
    pressure = jnp.sum(slopes, axis=1)
    weighted = (slopes * second_scale[None, :]).astype(jnp.bfloat16)
    spread = lax.dot_general(weighted, onehot, (((1,), (1,)), ((), ())), preferred_element_type=jnp.float32)
    first_part = jnp.sum(slopes * first_scale[None, :], axis=1)
    column_mark = (jnp.arange(width, dtype=jnp.int32) == first_local).astype(jnp.float32)
    spread = spread + first_part[:, None] * column_mark[None, :]
    return squares, pressure, spread


def reference(lodf, limits, base_flow, first_ids, second_ids, counts):
    limit = 0.01 * limits.astype(jnp.float32)
    line_ids = jnp.arange(LINES, dtype=jnp.int32)

    def one_tile(pressure_total, tile_index):
        anchor = (tile_index * LINE_DEV).astype(jnp.int32)
        row_anchor = (tile_index * FIRST_DEV).astype(jnp.int32)
        zero_index = jnp.zeros((), jnp.int32)
        columns = lax.dynamic_slice(lodf, (zero_index, anchor), (LINES, LINE_DEV))
        square = lax.dynamic_slice(lodf, (anchor, anchor), (LINE_DEV, LINE_DEV))
        own_flows = lax.dynamic_slice(base_flow, (anchor,), (LINE_DEV,))
        heads = lax.dynamic_slice(first_ids, (row_anchor,), (FIRST_DEV,))
        seconds = lax.dynamic_slice(second_ids, (row_anchor, zero_index), (FIRST_DEV, CAND))
        lives = lax.dynamic_slice(counts, (row_anchor,), (FIRST_DEV,))
        first_scale, second_scale = jax.vmap(pair_coefficients, in_axes=(None, None, 0, 0))(square, own_flows, heads - anchor, seconds - anchor)

        def one_first(totals, items):
            pressure_sum, spread_sum = totals
            first_line, second_lines, live_count, scale_one, scale_two = items
            squares, pressure, spread = pair_terms(columns, base_flow, limit, line_ids, first_line, second_lines, first_line - anchor, second_lines - anchor, scale_one, scale_two, live_count)
            return (pressure_sum + pressure, spread_sum + spread), squares

        start_spread = jnp.zeros((LINES, LINE_DEV), jnp.float32)
        (pressure_total, spread_sum), squares = lax.scan(one_first, (pressure_total, start_spread), (heads, seconds, lives, first_scale, second_scale))
        return pressure_total, (squares, (spread_sum / CAND).astype(jnp.bfloat16))

    pressure_total, (squares, tiles) = lax.scan(one_tile, jnp.zeros((LINES,), jnp.float32), jnp.arange(N_LINE, dtype=jnp.int32))
    pair_penalty = squares.reshape(FIRST, CAND) / LINES
    line_pressure = pressure_total / (FIRST * CAND)
    lodf_grad = jnp.transpose(tiles, (1, 0, 2)).reshape(LINES, LINES)
    return (pair_penalty, line_pressure, lodf_grad)
```

```python
import functools

import jax
import jax.numpy as jnp
from jax import lax
from jax.experimental import pallas as pl
from jax.experimental.pallas import tpu as pltpu
from jax.sharding import PartitionSpec as P

F32 = jnp.float32
BF16 = jnp.bfloat16


def iota(shape, dim, dtype=jnp.int32):
    return lax.broadcasted_iota(jnp.int32, shape, dim).astype(dtype)


def split3(x):
    top = x.astype(BF16).astype(F32)
    rest = x - top
    middle = rest.astype(BF16).astype(F32)
    return top, middle, rest - middle


def pack_kernel(first_ref, counts_ref, lodf_ref, base_ref, second_ref, out_ref):
    width = lodf_ref.shape[0]
    firsts, cands = second_ref.shape
    peers = out_ref.shape[0]
    anchor = lax.axis_index("line") * width
    square = lodf_ref[:, pl.ds(pl.multiple_of(anchor, width), width)]
    row = iota((firsts, width), 0)
    lane = iota((firsts, width), 1)
    head = jnp.zeros((firsts, width), jnp.int32)
    lives = jnp.zeros((firsts, cands), jnp.int32)
    heads_row = jnp.zeros((1, width), F32)
    for j in range(firsts):
        local = first_ref[j] - anchor
        head = jnp.where(row == j, local, head)
        lives = jnp.where(row == j, counts_ref[j], lives)
        heads_row = jnp.where(iota((1, width), 1) == j, local.astype(F32), heads_row)
    hot = (lane == head).astype(BF16)
    first_row = jnp.dot(hot, square, preferred_element_type=F32)
    first_column = lax.dot_general(
        hot, square, (((1,), (1,)), ((), ())), preferred_element_type=F32
    )
    second = second_ref[...] - anchor
    p = jnp.take_along_axis(first_row, second, axis=1)
    q = jnp.take_along_axis(first_column, second, axis=1)
    live = iota((firsts, cands), 1) < lives
    ids = jnp.where(live, second.astype(F32), -1.0)
    top, middle, low = split3(base_ref[...])
    fill = jnp.zeros((firsts - 4, width), F32)
    block = jnp.concatenate([p, q, ids, top, middle, low, heads_row, fill], axis=0)
    block = block.astype(BF16)
    for peer in range(peers):
        out_ref[peer] = block


def screen_kernel(
    got_ref,
    lodf_ref,
    base_ref,
    limits_ref,
    squares_ref,
    pressure_ref,
    grad_ref,
    low_ref,
    high_ref,
    sum_ref,
    one_ref,
    two_ref,
    ids_ref,
    heads_ref,
):
    width = lodf_ref.shape[0]
    tiles = got_ref.shape[0]
    firsts = squares_ref.shape[1]
    cands = squares_ref.shape[2]
    me = lax.axis_index("line")

    limit = 0.01 * limits_ref[...].astype(F32)
    base = base_ref[...]
    low_ref[...] = jnp.transpose(jnp.broadcast_to(-limit - base, (width, width)))
    high_ref[...] = jnp.transpose(jnp.broadcast_to(limit - base, (width, width)))
    sum_ref[...] = jnp.zeros_like(sum_ref)

    got = got_ref[...].astype(F32)
    shape = (tiles, firsts, cands)
    flat = (tiles * firsts, cands)
    p = got[:, :firsts].reshape(flat)
    q = got[:, firsts : 2 * firsts].reshape(flat)
    ids = got[:, 2 * firsts : 3 * firsts].reshape(flat)
    tail = got[:, 3 * firsts :]
    flows = jnp.broadcast_to(
        tail[:, 0:1] + tail[:, 1:2] + tail[:, 2:3], shape
    ).reshape(flat)
    own = iota(shape, 2) == iota(shape, 1)
    heads = jnp.sum(
        jnp.where(own, jnp.broadcast_to(tail[:, 3:4], shape), 0.0).reshape(flat),
        axis=1,
        keepdims=True,
    )
    lane = iota(flat, 1, F32)
    first_flow = jnp.sum(jnp.where(lane == heads, flows, 0.0), axis=1, keepdims=True)
    live = ids >= 0.0
    second_flow = jnp.take_along_axis(
        flows, jnp.maximum(ids, 0.0).astype(jnp.int32), axis=1
    )
    det = 1.0 - p * q
    one_ref[...] = jnp.where(live, (first_flow + p * second_flow) / det, 0.0)
    two_ref[...] = jnp.where(live, (second_flow + q * first_flow) / det, 0.0)
    ids_ref[...] = ids
    heads_ref[...] = jnp.broadcast_to(heads, flat)

    line = iota((width, cands), 0, F32)
    column = iota((width, cands), 0, F32).astype(BF16)
    lane_row = iota((1, width), 1, F32)

    def wide(row):
        return jnp.broadcast_to(row, (width, cands)).astype(BF16)

    def one_tile(tile, masked):
        rows = pl.ds(pl.multiple_of(tile * firsts, firsts), firsts)
        span = pl.ds(pl.multiple_of(tile * width, width), width)
        factors = lodf_ref[:, span]
        twice = jnp.concatenate([factors, factors], axis=1)
        scale_one = one_ref[rows, :]
        scale_two = two_ref[rows, :]
        second = ids_ref[rows, :]
        first = heads_ref[rows, :]
        alive = (second >= 0.0).astype(F32)
        grad = jnp.zeros((width, width), F32)
        total = sum_ref[...]
        squares = []
        group = 2
        for start in range(0, firsts, group):
            hots, tops, lows = [], [], []
            for j in range(start, start + group):
                pick = slice(j, j + 1)
                one_top = scale_one[pick].astype(BF16).astype(F32)
                two_top = scale_two[pick].astype(BF16).astype(F32)
                is_two = column == wide(second[pick])
                is_one = column == wide(first[pick])
                zero = jnp.zeros((), BF16)
                hots.append(jnp.where(is_two, jnp.ones((), BF16), zero))
                tops.append(
                    jnp.where(
                        is_one, wide(one_top), jnp.where(is_two, wide(two_top), zero)
                    )
                )
                lows.append(
                    jnp.where(
                        is_one,
                        wide(scale_one[pick] - one_top),
                        jnp.where(is_two, wide(scale_two[pick] - two_top), zero),
                    )
                )
            hot = jnp.concatenate(hots, axis=1)
            mix = jnp.concatenate(
                [jnp.concatenate(tops, axis=1), jnp.concatenate(lows, axis=1)], axis=0
            )
            change = jnp.dot(twice, mix, preferred_element_type=F32)
            weights = []
            for j in range(start, start + group):
                pick = slice(j, j + 1)
                part = change[:, (j - start) * cands : (j - start + 1) * cands]
                excess = part - jnp.minimum(
                    jnp.maximum(part, low_ref[...]), high_ref[...]
                )
                keep = alive[pick]
                if masked:
                    out = (line == second[pick]) | (line == first[pick])
                    excess = jnp.where(out, 0.0, excess)
                excess = excess * keep
                squares.append(jnp.sum(excess * excess, axis=0, keepdims=True))
                total = total + excess
                weights.append((excess * (2.0 * scale_two[pick])).astype(BF16))
                lead = jnp.sum(
                    excess * (2.0 * scale_one[pick]), axis=1, keepdims=True
                )
                grad = grad + jnp.where(lane_row == first[pick], lead, 0.0)
            grad = grad + lax.dot_general(
                jnp.concatenate(weights, axis=1),
                hot,
                (((1,), (1,)), ((), ())),
                preferred_element_type=F32,
            )
        sum_ref[...] = total
        squares_ref[tile] = jnp.concatenate(squares, axis=0)
        grad_ref[:, span] = (grad * (1.0 / cands)).astype(BF16)

    one_tile(me, True)

    @pl.loop(1, tiles)
    def _(step):
        tile = me + step
        one_tile(jnp.where(tile >= tiles, tile - tiles, tile), False)

    pressure_ref[...] = jnp.sum(jnp.transpose(sum_ref[...]), axis=0, keepdims=True) * (
        2.0 / (tiles * firsts * cands)
    )


def per_device(lodf, limits, base_flow, first_ids, second_ids, counts):
    width, lines = lodf.shape
    firsts, cands = second_ids.shape
    tiles = lax.axis_size("line")
    vmem = pl.BlockSpec(memory_space=pltpu.VMEM)
    smem = pl.BlockSpec(memory_space=pltpu.SMEM)
    base = base_flow.reshape(1, width)
    packed = pl.pallas_call(
        pack_kernel,
        out_shape=jax.ShapeDtypeStruct((tiles, 4 * firsts, cands), BF16),
        in_specs=[smem, smem, vmem, vmem, vmem],
        out_specs=vmem,
        name="pack_pairs",
    )(first_ids, counts, lodf, base, second_ids)
    got = lax.all_to_all(packed, "line", split_axis=0, concat_axis=0, tiled=True)
    pairs = tiles * firsts
    squares, pressure, grad = pl.pallas_call(
        screen_kernel,
        out_shape=(
            jax.ShapeDtypeStruct((tiles, firsts, cands), F32),
            jax.ShapeDtypeStruct((1, width), F32),
            jax.ShapeDtypeStruct((width, lines), BF16),
        ),
        in_specs=[vmem] * 4,
        out_specs=(vmem,) * 3,
        scratch_shapes=[
            pltpu.VMEM((width, width), F32),
            pltpu.VMEM((width, width), F32),
            pltpu.VMEM((width, cands), F32),
            pltpu.VMEM((pairs, cands), F32),
            pltpu.VMEM((pairs, cands), F32),
            pltpu.VMEM((pairs, cands), F32),
            pltpu.VMEM((pairs, cands), F32),
        ],
        compiler_params=pltpu.CompilerParams(vmem_limit_bytes=32 * 1024 * 1024),
        name="screen_lines",
    )(got, lodf, base, limits.reshape(1, width))
    sums = lax.all_to_all(squares, "line", split_axis=0, concat_axis=0, tiled=True)
    pair_penalty = jnp.sum(sums, axis=0) * (1.0 / lines)
    return (pair_penalty, pressure.reshape(width), grad)


def solution(mesh):
    return jax.shard_map(
        per_device,
        mesh=mesh,
        in_specs=(
            P("line", None),
            P("line"),
            P(("groups", "line")),
            P(("groups", "line")),
            P(("groups", "line"), None),
            P(("groups", "line")),
        ),
        out_specs=(P(("groups", "line"), None), P(("groups", "line")), P(("groups", "line"), None)),
        check_vma=False,
    )
```

```python
import functools

import jax
import jax.numpy as jnp
from jax import lax
from jax.experimental import pallas as pl
from jax.experimental.pallas import tpu as pltpu
from jax.sharding import PartitionSpec as P

F32 = jnp.float32
BF16 = jnp.bfloat16


def iota(shape, dim, dtype=jnp.int32):
    return lax.broadcasted_iota(jnp.int32, shape, dim).astype(dtype)


def split3(x):
    top = x.astype(BF16).astype(F32)
    rest = x - top
    middle = rest.astype(BF16).astype(F32)
    return top, middle, rest - middle


def pack_kernel(first_ref, counts_ref, lodf_ref, base_ref, second_ref, out_ref):
    width = lodf_ref.shape[0]
    firsts, cands = second_ref.shape
    anchor = lax.axis_index("line") * width
    square = lodf_ref[:, pl.ds(pl.multiple_of(anchor, width), width)]
    row = iota((firsts, width), 0)
    lane = iota((firsts, width), 1)
    head = jnp.zeros((firsts, width), jnp.int32)
    lives = jnp.zeros((firsts, cands), jnp.int32)
    heads_row = jnp.zeros((1, width), F32)
    for j in range(firsts):
        local = first_ref[j] - anchor
        head = jnp.where(row == j, local, head)
        lives = jnp.where(row == j, counts_ref[j], lives)
        heads_row = jnp.where(iota((1, width), 1) == j, local.astype(F32), heads_row)
    hot = (lane == head).astype(BF16)
    first_row = jnp.dot(hot, square, preferred_element_type=F32)
    first_column = lax.dot_general(
        hot, square, (((1,), (1,)), ((), ())), preferred_element_type=F32
    )
    second = second_ref[...] - anchor
    p = jnp.take_along_axis(first_row, second, axis=1)
    q = jnp.take_along_axis(first_column, second, axis=1)
    live = iota((firsts, cands), 1) < lives
    ids = jnp.where(live, second.astype(F32), -1.0)
    top, middle, low = split3(base_ref[...])
    fill = jnp.zeros((firsts - 4, width), F32)
    block = jnp.concatenate([p, q, ids, top, middle, low, heads_row, fill], axis=0)
    out_ref[...] = block.astype(BF16)


def screen_kernel(tiles, *refs):
    got_refs = refs[:tiles]
    lodf_ref, base_ref, limits_ref = refs[tiles : tiles + 3]
    squares_refs = refs[tiles + 3 : 2 * tiles + 3]
    pressure_ref, grad_ref = refs[2 * tiles + 3 : 2 * tiles + 5]
    (low_ref, high_ref, sum_ref, one_ref, two_ref, ids_ref, heads_ref, square_ref) = refs[
        2 * tiles + 5 :
    ]
    width = lodf_ref.shape[0]
    firsts, cands = squares_refs[0].shape
    me = lax.axis_index("line")

    limit = 0.01 * limits_ref[...].astype(F32)
    base = base_ref[...]
    low_ref[...] = jnp.transpose(jnp.broadcast_to(-limit - base, (width, width)))
    high_ref[...] = jnp.transpose(jnp.broadcast_to(limit - base, (width, width)))
    sum_ref[...] = jnp.zeros_like(sum_ref)

    got = jnp.stack([ref[...] for ref in got_refs]).astype(F32)
    shape = (tiles, firsts, cands)
    flat = (tiles * firsts, cands)
    p = got[:, :firsts].reshape(flat)
    q = got[:, firsts : 2 * firsts].reshape(flat)
    ids = got[:, 2 * firsts : 3 * firsts].reshape(flat)
    tail = got[:, 3 * firsts :]
    flows = jnp.broadcast_to(
        tail[:, 0:1] + tail[:, 1:2] + tail[:, 2:3], shape
    ).reshape(flat)
    own = iota(shape, 2) == iota(shape, 1)
    heads = jnp.sum(
        jnp.where(own, jnp.broadcast_to(tail[:, 3:4], shape), 0.0).reshape(flat),
        axis=1,
        keepdims=True,
    )
    lane = iota(flat, 1, F32)
    first_flow = jnp.sum(jnp.where(lane == heads, flows, 0.0), axis=1, keepdims=True)
    live = ids >= 0.0
    second_flow = jnp.take_along_axis(
        flows, jnp.maximum(ids, 0.0).astype(jnp.int32), axis=1
    )
    det = 1.0 - p * q
    one_ref[...] = jnp.where(live, (first_flow + p * second_flow) / det, 0.0)
    two_ref[...] = jnp.where(live, (second_flow + q * first_flow) / det, 0.0)
    ids_ref[...] = ids
    heads_ref[...] = jnp.broadcast_to(heads, flat)

    line = iota((width, cands), 0, F32)
    column = iota((width, cands), 0, F32).astype(BF16)
    lane_row = iota((1, width), 1, F32)

    def wide(row):
        return jnp.broadcast_to(row, (width, cands)).astype(BF16)

    def one_tile(step, masked):
        tile = jnp.where(step > me, me - step + tiles, me - step)
        rows = pl.ds(pl.multiple_of(step * firsts, firsts), firsts)
        span = pl.ds(pl.multiple_of(tile * width, width), width)
        factors = lodf_ref[:, span]
        twice = jnp.concatenate([factors, factors], axis=1)
        scale_one = one_ref[rows, :]
        scale_two = two_ref[rows, :]
        second = ids_ref[rows, :]
        first = heads_ref[rows, :]
        alive = (second >= 0.0).astype(F32)
        grad = jnp.zeros((width, width), F32)
        total = sum_ref[...]
        squares = []
        group = 2
        for start in range(0, firsts, group):
            hots, tops, lows = [], [], []
            for j in range(start, start + group):
                pick = slice(j, j + 1)
                one_top = scale_one[pick].astype(BF16).astype(F32)
                two_top = scale_two[pick].astype(BF16).astype(F32)
                is_two = column == wide(second[pick])
                is_one = column == wide(first[pick])
                zero = jnp.zeros((), BF16)
                hots.append(jnp.where(is_two, jnp.ones((), BF16), zero))
                tops.append(
                    jnp.where(
                        is_one, wide(one_top), jnp.where(is_two, wide(two_top), zero)
                    )
                )
                lows.append(
                    jnp.where(
                        is_one,
                        wide(scale_one[pick] - one_top),
                        jnp.where(is_two, wide(scale_two[pick] - two_top), zero),
                    )
                )
            hot = jnp.concatenate(hots, axis=1)
            mix = jnp.concatenate(
                [jnp.concatenate(tops, axis=1), jnp.concatenate(lows, axis=1)], axis=0
            )
            change = jnp.dot(twice, mix, preferred_element_type=F32)
            weights = []
            for j in range(start, start + group):
                pick = slice(j, j + 1)
                part = change[:, (j - start) * cands : (j - start + 1) * cands]
                excess = part - jnp.minimum(
                    jnp.maximum(part, low_ref[...]), high_ref[...]
                )
                keep = alive[pick]
                if masked:
                    out = (line == second[pick]) | (line == first[pick])
                    excess = jnp.where(out, 0.0, excess)
                excess = excess * keep
                squares.append(jnp.sum(excess * excess, axis=0, keepdims=True))
                total = total + excess
                weights.append((excess * (2.0 * scale_two[pick])).astype(BF16))
                lead = jnp.sum(
                    excess * (2.0 * scale_one[pick]), axis=1, keepdims=True
                )
                grad = grad + jnp.where(lane_row == first[pick], lead, 0.0)
            grad = grad + lax.dot_general(
                jnp.concatenate(weights, axis=1),
                hot,
                (((1,), (1,)), ((), ())),
                preferred_element_type=F32,
            )
        sum_ref[...] = total
        square_ref[rows, :] = jnp.concatenate(squares, axis=0)
        grad_ref[:, span] = (grad * (1.0 / cands)).astype(BF16)

    one_tile(0, True)

    @pl.loop(1, tiles)
    def _(step):
        one_tile(step, False)

    for step in range(tiles):
        squares_refs[step][...] = square_ref[step * firsts : (step + 1) * firsts, :]
    pressure_ref[...] = jnp.sum(jnp.transpose(sum_ref[...]), axis=0, keepdims=True) * (
        2.0 / (tiles * firsts * cands)
    )


def total_kernel(scale, *refs):
    total = refs[0][...]
    for ref in refs[1:-1]:
        total = total + ref[...]
    refs[-1][...] = total * scale


def per_device(lodf, limits, base_flow, first_ids, second_ids, counts):
    width, lines = lodf.shape
    firsts, cands = second_ids.shape
    tiles = lax.axis_size("line")
    vmem = pl.BlockSpec(memory_space=pltpu.VMEM)
    smem = pl.BlockSpec(memory_space=pltpu.SMEM)
    base = base_flow.reshape(1, width)
    packed = pl.pallas_call(
        pack_kernel,
        out_shape=jax.ShapeDtypeStruct((4 * firsts, cands), BF16),
        in_specs=[smem, smem, vmem, vmem, vmem],
        out_specs=vmem,
        name="pack_pairs",
    )(first_ids, counts, lodf, base, second_ids)

    def shifted(x, shift):
        return lax.ppermute(x, "line", [(i, (i + shift) % tiles) for i in range(tiles)])

    got = [packed] + [shifted(packed, step) for step in range(1, tiles)]
    pairs = tiles * firsts
    *squares, pressure, grad = pl.pallas_call(
        functools.partial(screen_kernel, tiles),
        out_shape=[jax.ShapeDtypeStruct((firsts, cands), F32)] * tiles
        + [
            jax.ShapeDtypeStruct((1, width), F32),
            jax.ShapeDtypeStruct((width, lines), BF16),
        ],
        in_specs=[vmem] * (tiles + 3),
        out_specs=[vmem] * (tiles + 2),
        scratch_shapes=[
            pltpu.VMEM((width, width), F32),
            pltpu.VMEM((width, width), F32),
            pltpu.VMEM((width, cands), F32),
            pltpu.VMEM((pairs, cands), F32),
            pltpu.VMEM((pairs, cands), F32),
            pltpu.VMEM((pairs, cands), F32),
            pltpu.VMEM((pairs, cands), F32),
            pltpu.VMEM((pairs, cands), F32),
        ],
        compiler_params=pltpu.CompilerParams(vmem_limit_bytes=32 * 1024 * 1024),
        name="screen_lines",
    )(*got, lodf, base, limits.reshape(1, width))
    sums = [squares[0]] + [
        shifted(squares[step], tiles - step) for step in range(1, tiles)
    ]
    pair_penalty = pl.pallas_call(
        functools.partial(total_kernel, 1.0 / lines),
        out_shape=jax.ShapeDtypeStruct((firsts, cands), F32),
        in_specs=[vmem] * tiles,
        out_specs=vmem,
        name="total_pairs",
    )(*sums)
    return (pair_penalty, pressure.reshape(width), grad)


def solution(mesh):
    return jax.shard_map(
        per_device,
        mesh=mesh,
        in_specs=(
            P("line", None),
            P("line"),
            P(("groups", "line")),
            P(("groups", "line")),
            P(("groups", "line"), None),
            P(("groups", "line")),
        ),
        out_specs=(P(("groups", "line"), None), P(("groups", "line")), P(("groups", "line"), None)),
        check_vma=False,
    )
```

```python
import jax
import jax.numpy as jnp
from jax import lax
from jax.experimental import pallas as pl
from jax.experimental.pallas import tpu as pltpu
from jax.sharding import PartitionSpec as P

F32 = jnp.float32
BF16 = jnp.bfloat16
MIB = 1024 * 1024


def iota(shape, dim, dtype=jnp.int32):
    return lax.broadcasted_iota(jnp.int32, shape, dim).astype(dtype)


def split3(x):
    top = x.astype(BF16).astype(F32)
    rest = x - top
    middle = rest.astype(BF16).astype(F32)
    return top, middle, rest - middle


def pack_kernel(first_ref, counts_ref, lodf_ref, base_ref, second_ref, out_ref):
    width = lodf_ref.shape[0]
    firsts, cands = second_ref.shape
    peers = out_ref.shape[0]
    anchor = lax.axis_index("line") * width
    square = lodf_ref[:, pl.ds(pl.multiple_of(anchor, width), width)]
    row = iota((firsts, width), 0)
    lane = iota((firsts, width), 1)
    head = jnp.zeros((firsts, width), jnp.int32)
    lives = jnp.zeros((firsts, cands), jnp.int32)
    heads_row = jnp.zeros((1, width), F32)
    for j in range(firsts):
        local = first_ref[j] - anchor
        head = jnp.where(row == j, local, head)
        lives = jnp.where(row == j, counts_ref[j], lives)
        heads_row = jnp.where(iota((1, width), 1) == j, local.astype(F32), heads_row)
    hot = (lane == head).astype(BF16)
    first_row = jnp.dot(hot, square, preferred_element_type=F32)
    first_column = lax.dot_general(
        hot, square, (((1,), (1,)), ((), ())), preferred_element_type=F32
    )
    second = second_ref[...] - anchor
    p = jnp.take_along_axis(first_row, second, axis=1)
    q = jnp.take_along_axis(first_column, second, axis=1)
    live = iota((firsts, cands), 1) < lives
    ids = jnp.where(live, second.astype(F32), -1.0)
    top, middle, low = split3(base_ref[...])
    fill = jnp.zeros((firsts - 4, width), F32)
    block = jnp.concatenate([p, q, ids, top, middle, low, heads_row, fill], axis=0)
    block = block.astype(BF16)
    for peer in range(peers):
        out_ref[peer] = block


def coefficients(got, firsts, cands):
    tiles = got.shape[0]
    got = got.astype(F32)
    shape = (tiles, firsts, cands)
    flat = (tiles * firsts, cands)
    p = got[:, :firsts].reshape(flat)
    q = got[:, firsts : 2 * firsts].reshape(flat)
    ids = got[:, 2 * firsts : 3 * firsts].reshape(flat)
    tail = got[:, 3 * firsts :]
    flows = jnp.broadcast_to(
        tail[:, 0:1] + tail[:, 1:2] + tail[:, 2:3], shape
    ).reshape(flat)
    own = iota(shape, 2) == iota(shape, 1)
    heads = jnp.sum(
        jnp.where(own, jnp.broadcast_to(tail[:, 3:4], shape), 0.0).reshape(flat),
        axis=1,
        keepdims=True,
    )
    lane = iota(flat, 1, F32)
    first_flow = jnp.sum(jnp.where(lane == heads, flows, 0.0), axis=1, keepdims=True)
    live = ids >= 0.0
    second_flow = jnp.take_along_axis(
        flows, jnp.maximum(ids, 0.0).astype(jnp.int32), axis=1
    )
    det = 1.0 - p * q
    one = jnp.where(live, (first_flow + p * second_flow) / det, 0.0)
    two = jnp.where(live, (second_flow + q * first_flow) / det, 0.0)
    return one, two, ids, jnp.broadcast_to(heads, flat)


def wide(row, width):
    return jnp.broadcast_to(row, (width, row.shape[1])).astype(BF16)


def flow_excess(factors, one, two, second, first, low, high):
    width = factors.shape[0]
    firsts, cands = one.shape
    column = iota((width, cands), 0, F32).astype(BF16)
    zero = jnp.zeros((), BF16)
    twice = jnp.concatenate([factors, factors], axis=1)
    parts = []
    group = 2
    for start in range(0, firsts, group):
        tops, lows = [], []
        for j in range(start, start + group):
            pick = slice(j, j + 1)
            one_top = one[pick].astype(BF16).astype(F32)
            two_top = two[pick].astype(BF16).astype(F32)
            is_two = column == wide(second[pick], width)
            is_one = column == wide(first[pick], width)
            tops.append(
                jnp.where(
                    is_one,
                    wide(one_top, width),
                    jnp.where(is_two, wide(two_top, width), zero),
                )
            )
            lows.append(
                jnp.where(
                    is_one,
                    wide(one[pick] - one_top, width),
                    jnp.where(is_two, wide(two[pick] - two_top, width), zero),
                )
            )
        mix = jnp.concatenate(
            [jnp.concatenate(tops, axis=1), jnp.concatenate(lows, axis=1)], axis=0
        )
        change = jnp.dot(twice, mix, preferred_element_type=F32)
        for j in range(group):
            part = change[:, j * cands : (j + 1) * cands]
            parts.append(part - jnp.minimum(jnp.maximum(part, low), high))
    return parts


def own_kernel(
    packed_ref,
    lodf_ref,
    base_ref,
    limits_ref,
    low_ref,
    high_ref,
    excess_ref,
    squares_ref,
):
    width = lodf_ref.shape[0]
    firsts, cands = squares_ref.shape
    me = lax.axis_index("line")

    limit = 0.01 * limits_ref[...].astype(F32)
    base = base_ref[...]
    low = jnp.transpose(jnp.broadcast_to(-limit - base, (width, width)))
    high = jnp.transpose(jnp.broadcast_to(limit - base, (width, width)))
    low_ref[...] = low
    high_ref[...] = high
    one, two, second, first = coefficients(packed_ref[0:1], firsts, cands)
    factors = lodf_ref[:, pl.ds(pl.multiple_of(me * width, width), width)]
    line = iota((width, cands), 0, F32)
    parts = flow_excess(factors, one, two, second, first, low, high)
    squares = []
    for j in range(firsts):
        pick = slice(j, j + 1)
        out = (line == second[pick]) | (line == first[pick])
        part = jnp.where(out, 0.0, parts[j])
        excess_ref[:, j * cands : (j + 1) * cands] = part
        squares.append(jnp.sum(part * part, axis=0, keepdims=True))
    squares_ref[...] = jnp.where(second >= 0.0, jnp.concatenate(squares, axis=0), 0.0)


def excess_kernel(
    got_ref,
    lodf_ref,
    low_ref,
    high_ref,
    own_ref,
    squares_ref,
    excess_ref,
    one_ref,
    two_ref,
    ids_ref,
    heads_ref,
):
    width = lodf_ref.shape[0]
    tiles, firsts, cands = squares_ref.shape
    me = lax.axis_index("line")
    one_ref[...], two_ref[...], ids_ref[...], heads_ref[...] = coefficients(
        got_ref[...], firsts, cands
    )
    squares_ref[me] = own_ref[...]

    @pl.loop(1, tiles)
    def _(step):
        tile = me + step
        tile = jnp.where(tile >= tiles, tile - tiles, tile)
        rows = pl.ds(pl.multiple_of(tile * firsts, firsts), firsts)
        span = pl.ds(pl.multiple_of(tile * width, width), width)
        second = ids_ref[rows, :]
        parts = flow_excess(
            lodf_ref[:, span],
            one_ref[rows, :],
            two_ref[rows, :],
            second,
            heads_ref[rows, :],
            low_ref[...],
            high_ref[...],
        )
        squares = []
        for j in range(firsts):
            excess_ref[step - 1, :, j * cands : (j + 1) * cands] = parts[j]
            squares.append(jnp.sum(parts[j] * parts[j], axis=0, keepdims=True))
        squares_ref[tile] = jnp.where(
            second >= 0.0, jnp.concatenate(squares, axis=0), 0.0
        )


def grad_kernel(
    own_ref,
    excess_ref,
    one_ref,
    two_ref,
    ids_ref,
    heads_ref,
    pressure_ref,
    grad_ref,
    sum_ref,
):
    width = own_ref.shape[0]
    tiles = excess_ref.shape[0] + 1
    cands = ids_ref.shape[1]
    firsts = ids_ref.shape[0] // tiles
    me = lax.axis_index("line")
    column = iota((width, cands), 0, F32).astype(BF16)
    lane_row = iota((1, width), 1, F32)

    def one_tile(tile, read, total):
        rows = pl.ds(pl.multiple_of(tile * firsts, firsts), firsts)
        span = pl.ds(pl.multiple_of(tile * width, width), width)
        one = 2.0 * one_ref[rows, :]
        two = 2.0 * two_ref[rows, :]
        second = ids_ref[rows, :]
        first = heads_ref[rows, :]
        alive = (second >= 0.0).astype(F32)
        grad = jnp.zeros((width, width), F32)
        group = 2
        for start in range(0, firsts, group):
            hots, weights = [], []
            for j in range(start, start + group):
                pick = slice(j, j + 1)
                excess = read(j)
                total = total + excess * alive[pick]
                hots.append(
                    jnp.where(
                        column == wide(second[pick], width),
                        jnp.ones((), BF16),
                        jnp.zeros((), BF16),
                    )
                )
                weights.append((excess * two[pick]).astype(BF16))
                lead = jnp.sum(excess * one[pick], axis=1, keepdims=True)
                grad = grad + jnp.where(lane_row == first[pick], lead, 0.0)
            grad = grad + lax.dot_general(
                jnp.concatenate(weights, axis=1),
                jnp.concatenate(hots, axis=1),
                (((1,), (1,)), ((), ())),
                preferred_element_type=F32,
            )
        grad_ref[:, span] = (grad * (1.0 / cands)).astype(BF16)
        return total

    def own(j):
        return own_ref[:, j * cands : (j + 1) * cands]

    sum_ref[...] = one_tile(me, own, jnp.zeros((width, cands), F32))

    @pl.loop(1, tiles)
    def _(step):
        tile = me + step

        def other(j):
            return excess_ref[step - 1, :, j * cands : (j + 1) * cands]

        sum_ref[...] = one_tile(
            jnp.where(tile >= tiles, tile - tiles, tile), other, sum_ref[...]
        )

    pressure_ref[...] = jnp.sum(jnp.transpose(sum_ref[...]), axis=0, keepdims=True) * (
        2.0 / (tiles * firsts * cands)
    )


def per_device(lodf, limits, base_flow, first_ids, second_ids, counts):
    width, lines = lodf.shape
    firsts, cands = second_ids.shape
    tiles = lax.axis_size("line")
    pairs = tiles * firsts
    vmem = pl.BlockSpec(memory_space=pltpu.VMEM)
    smem = pl.BlockSpec(memory_space=pltpu.SMEM)
    base = base_flow.reshape(1, width)
    size = pairs * cands * width * 4
    params = pltpu.CompilerParams(vmem_limit_bytes=size + 16 * MIB)
    packed = pl.pallas_call(
        pack_kernel,
        out_shape=jax.ShapeDtypeStruct((tiles, 4 * firsts, cands), BF16),
        in_specs=[smem, smem, vmem, vmem, vmem],
        out_specs=vmem,
        name="pack_pairs",
    )(first_ids, counts, lodf, base, second_ids)
    got = lax.all_to_all(packed, "line", split_axis=0, concat_axis=0, tiled=True)
    low, high, own_excess, own_squares = pl.pallas_call(
        own_kernel,
        out_shape=(
            jax.ShapeDtypeStruct((width, cands), F32),
            jax.ShapeDtypeStruct((width, cands), F32),
            jax.ShapeDtypeStruct((width, firsts * cands), F32),
            jax.ShapeDtypeStruct((firsts, cands), F32),
        ),
        in_specs=[vmem] * 4,
        out_specs=(vmem,) * 4,
        compiler_params=pltpu.CompilerParams(vmem_limit_bytes=16 * MIB),
        cost_estimate=pl.CostEstimate(
            flops=4 * width * width * firsts * cands,
            bytes_accessed=4 * width * firsts * cands,
            transcendentals=0,
        ),
        name="screen_own",
    )(packed, lodf, base, limits.reshape(1, width))
    pair_rows = jax.ShapeDtypeStruct((pairs, cands), F32)
    squares, excess, one, two, ids, heads = pl.pallas_call(
        excess_kernel,
        out_shape=(
            jax.ShapeDtypeStruct((tiles, firsts, cands), F32),
            jax.ShapeDtypeStruct((tiles - 1, width, firsts * cands), F32),
            pair_rows,
            pair_rows,
            pair_rows,
            pair_rows,
        ),
        in_specs=[vmem] * 5,
        out_specs=(vmem,) * 6,
        compiler_params=params,
        cost_estimate=pl.CostEstimate(
            flops=4 * width * width * pairs * cands,
            bytes_accessed=size,
            transcendentals=0,
        ),
        name="screen_others",
    )(got, lodf, low, high, own_squares)
    sums = lax.all_to_all(squares, "line", split_axis=0, concat_axis=0, tiled=True)
    pressure, grad = pl.pallas_call(
        grad_kernel,
        out_shape=(
            jax.ShapeDtypeStruct((1, width), F32),
            jax.ShapeDtypeStruct((width, lines), BF16),
        ),
        in_specs=[vmem] * 6,
        out_specs=(vmem,) * 2,
        scratch_shapes=[pltpu.VMEM((width, cands), F32)],
        compiler_params=params,
        cost_estimate=pl.CostEstimate(
            flops=4 * width * width * pairs * cands,
            bytes_accessed=size,
            transcendentals=0,
        ),
        name="column_sensitivities",
    )(own_excess, excess, one, two, ids, heads)
    pair_penalty = jnp.sum(sums, axis=0) * (1.0 / lines)
    return (pair_penalty, pressure.reshape(width), grad)


def solution(mesh):
    return jax.shard_map(
        per_device,
        mesh=mesh,
        in_specs=(
            P("line", None),
            P("line"),
            P(("groups", "line")),
            P(("groups", "line")),
            P(("groups", "line"), None),
            P(("groups", "line")),
        ),
        out_specs=(P(("groups", "line"), None), P(("groups", "line")), P(("groups", "line"), None)),
        check_vma=False,
    )
```

```python
import functools

import jax
import jax.numpy as jnp
from jax import lax
from jax.experimental import pallas as pl
from jax.experimental.pallas import tpu as pltpu
from jax.sharding import PartitionSpec as P

F32 = jnp.float32
BF16 = jnp.bfloat16


def iota(shape, dim, dtype=jnp.int32):
    return lax.broadcasted_iota(jnp.int32, shape, dim).astype(dtype)


def split3(x):
    top = x.astype(BF16).astype(F32)
    rest = x - top
    middle = rest.astype(BF16).astype(F32)
    return top, middle, rest - middle


def pack_kernel(first_ref, counts_ref, lodf_ref, base_ref, second_ref, out_ref):
    width = lodf_ref.shape[0]
    firsts, cands = second_ref.shape
    peers = out_ref.shape[0]
    anchor = lax.axis_index("line") * width
    square = lodf_ref[:, pl.ds(pl.multiple_of(anchor, width), width)]
    row = iota((firsts, width), 0)
    lane = iota((firsts, width), 1)
    head = jnp.zeros((firsts, width), jnp.int32)
    lives = jnp.zeros((firsts, cands), jnp.int32)
    heads_row = jnp.zeros((1, width), F32)
    for j in range(firsts):
        local = first_ref[j] - anchor
        head = jnp.where(row == j, local, head)
        lives = jnp.where(row == j, counts_ref[j], lives)
        heads_row = jnp.where(iota((1, width), 1) == j, local.astype(F32), heads_row)
    hot = (lane == head).astype(BF16)
    first_row = jnp.dot(hot, square, preferred_element_type=F32)
    first_column = lax.dot_general(
        hot, square, (((1,), (1,)), ((), ())), preferred_element_type=F32
    )
    second = second_ref[...] - anchor
    p = jnp.take_along_axis(first_row, second, axis=1)
    q = jnp.take_along_axis(first_column, second, axis=1)
    live = iota((firsts, cands), 1) < lives
    ids = jnp.where(live, second.astype(F32), -1.0)
    top, middle, low = split3(base_ref[...])
    fill = jnp.zeros((firsts - 4, width), F32)
    block = jnp.concatenate([p, q, ids, top, middle, low, heads_row, fill], axis=0)
    block = block.astype(BF16)
    for peer in range(peers):
        out_ref[peer] = block


def screen_kernel(
    near_ref,
    far_ref,
    lodf_ref,
    base_ref,
    limits_ref,
    near_squares_ref,
    far_squares_ref,
    pressure_ref,
    grad_ref,
    low_ref,
    high_ref,
    sum_ref,
    one_ref,
    two_ref,
    ids_ref,
    heads_ref,
    square_ref,
):
    width = lodf_ref.shape[0]
    chips, firsts, cands = near_squares_ref.shape
    tiles = 2 * chips
    me = lax.axis_index("line")
    core = lax.rem(me, 2)

    limit = 0.01 * limits_ref[...].astype(F32)
    base = base_ref[...]
    low_ref[...] = jnp.transpose(jnp.broadcast_to(-limit - base, (width, width)))
    high_ref[...] = jnp.transpose(jnp.broadcast_to(limit - base, (width, width)))
    sum_ref[...] = jnp.zeros_like(sum_ref)

    got = jnp.concatenate([near_ref[...], far_ref[...]], axis=0).astype(F32)
    shape = (tiles, firsts, cands)
    flat = (tiles * firsts, cands)
    p = got[:, :firsts].reshape(flat)
    q = got[:, firsts : 2 * firsts].reshape(flat)
    ids = got[:, 2 * firsts : 3 * firsts].reshape(flat)
    tail = got[:, 3 * firsts :]
    flows = jnp.broadcast_to(
        tail[:, 0:1] + tail[:, 1:2] + tail[:, 2:3], shape
    ).reshape(flat)
    own = iota(shape, 2) == iota(shape, 1)
    heads = jnp.sum(
        jnp.where(own, jnp.broadcast_to(tail[:, 3:4], shape), 0.0).reshape(flat),
        axis=1,
        keepdims=True,
    )
    lane = iota(flat, 1, F32)
    first_flow = jnp.sum(jnp.where(lane == heads, flows, 0.0), axis=1, keepdims=True)
    live = ids >= 0.0
    second_flow = jnp.take_along_axis(
        flows, jnp.maximum(ids, 0.0).astype(jnp.int32), axis=1
    )
    det = 1.0 - p * q
    one_ref[...] = jnp.where(live, (first_flow + p * second_flow) / det, 0.0)
    two_ref[...] = jnp.where(live, (second_flow + q * first_flow) / det, 0.0)
    ids_ref[...] = ids
    heads_ref[...] = jnp.broadcast_to(heads, flat)

    line = iota((width, cands), 0, F32)
    column = iota((width, cands), 0, F32).astype(BF16)
    lane_row = iota((1, width), 1, F32)

    def wide(row):
        return jnp.broadcast_to(row, (width, cands)).astype(BF16)

    def one_tile(place, masked):
        tile = jnp.where(place >= chips, 2 * (place - chips) + 1 - core, 2 * place + core)
        rows = pl.ds(pl.multiple_of(place * firsts, firsts), firsts)
        span = pl.ds(pl.multiple_of(tile * width, width), width)
        factors = lodf_ref[:, span]
        twice = jnp.concatenate([factors, factors], axis=1)
        scale_one = one_ref[rows, :]
        scale_two = two_ref[rows, :]
        second = ids_ref[rows, :]
        first = heads_ref[rows, :]
        alive = (second >= 0.0).astype(F32)
        grad = jnp.zeros((width, width), F32)
        total = sum_ref[...]
        squares = []
        group = 2
        for start in range(0, firsts, group):
            hots, tops, lows = [], [], []
            for j in range(start, start + group):
                pick = slice(j, j + 1)
                one_top = scale_one[pick].astype(BF16).astype(F32)
                two_top = scale_two[pick].astype(BF16).astype(F32)
                is_two = column == wide(second[pick])
                is_one = column == wide(first[pick])
                zero = jnp.zeros((), BF16)
                hots.append(jnp.where(is_two, jnp.ones((), BF16), zero))
                tops.append(
                    jnp.where(
                        is_one, wide(one_top), jnp.where(is_two, wide(two_top), zero)
                    )
                )
                lows.append(
                    jnp.where(
                        is_one,
                        wide(scale_one[pick] - one_top),
                        jnp.where(is_two, wide(scale_two[pick] - two_top), zero),
                    )
                )
            hot = jnp.concatenate(hots, axis=1)
            mix = jnp.concatenate(
                [jnp.concatenate(tops, axis=1), jnp.concatenate(lows, axis=1)], axis=0
            )
            change = jnp.dot(twice, mix, preferred_element_type=F32)
            weights = []
            for j in range(start, start + group):
                pick = slice(j, j + 1)
                part = change[:, (j - start) * cands : (j - start + 1) * cands]
                excess = part - jnp.minimum(
                    jnp.maximum(part, low_ref[...]), high_ref[...]
                )
                keep = alive[pick]
                if masked:
                    out = (line == second[pick]) | (line == first[pick])
                    excess = jnp.where(out, 0.0, excess)
                excess = excess * keep
                squares.append(jnp.sum(excess * excess, axis=0, keepdims=True))
                total = total + excess
                weights.append((excess * (2.0 * scale_two[pick])).astype(BF16))
                lead = jnp.sum(
                    excess * (2.0 * scale_one[pick]), axis=1, keepdims=True
                )
                grad = grad + jnp.where(lane_row == first[pick], lead, 0.0)
            grad = grad + lax.dot_general(
                jnp.concatenate(weights, axis=1),
                hot,
                (((1,), (1,)), ((), ())),
                preferred_element_type=F32,
            )
        sum_ref[...] = total
        square_ref[place] = jnp.concatenate(squares, axis=0)
        grad_ref[:, span] = (grad * (1.0 / cands)).astype(BF16)

    start = lax.div(me, 2)
    one_tile(start, True)

    @pl.loop(1, tiles)
    def _(step):
        place = start + step
        one_tile(jnp.where(place >= tiles, place - tiles, place), False)

    near_squares_ref[...] = square_ref[:chips]
    far_squares_ref[...] = square_ref[chips:]

    pressure_ref[...] = jnp.sum(jnp.transpose(sum_ref[...]), axis=0, keepdims=True) * (
        2.0 / (tiles * firsts * cands)
    )


def per_device(lodf, limits, base_flow, first_ids, second_ids, counts):
    width, lines = lodf.shape
    firsts, cands = second_ids.shape
    tiles = lax.axis_size("line")
    chips = tiles // 2
    groups = [list(range(core, tiles, 2)) for core in range(2)]

    def across_chips(x):
        return lax.all_to_all(
            x, "line", split_axis=0, concat_axis=0, axis_index_groups=groups, tiled=True
        )

    def other_core(x):
        return lax.ppermute(x, "line", [(i, i + 1 - 2 * (i % 2)) for i in range(tiles)])

    vmem = pl.BlockSpec(memory_space=pltpu.VMEM)
    smem = pl.BlockSpec(memory_space=pltpu.SMEM)
    base = base_flow.reshape(1, width)
    packed = pl.pallas_call(
        pack_kernel,
        out_shape=jax.ShapeDtypeStruct((chips, 4 * firsts, cands), BF16),
        in_specs=[smem, smem, vmem, vmem, vmem],
        out_specs=vmem,
        name="pack_pairs",
    )(first_ids, counts, lodf, base, second_ids)
    near = across_chips(packed)
    far = other_core(near)
    pairs = tiles * firsts
    near_squares, far_squares, pressure, grad = pl.pallas_call(
        screen_kernel,
        out_shape=(
            jax.ShapeDtypeStruct((chips, firsts, cands), F32),
            jax.ShapeDtypeStruct((chips, firsts, cands), F32),
            jax.ShapeDtypeStruct((1, width), F32),
            jax.ShapeDtypeStruct((width, lines), BF16),
        ),
        in_specs=[vmem] * 5,
        out_specs=(vmem,) * 4,
        scratch_shapes=[
            pltpu.VMEM((width, width), F32),
            pltpu.VMEM((width, width), F32),
            pltpu.VMEM((width, cands), F32),
            pltpu.VMEM((pairs, cands), F32),
            pltpu.VMEM((pairs, cands), F32),
            pltpu.VMEM((pairs, cands), F32),
            pltpu.VMEM((pairs, cands), F32),
            pltpu.VMEM((tiles, firsts, cands), F32),
        ],
        compiler_params=pltpu.CompilerParams(vmem_limit_bytes=32 * 1024 * 1024),
        name="screen_lines",
    )(near, far, lodf, base, limits.reshape(1, width))
    sums = across_chips(near_squares + other_core(far_squares))
    pair_penalty = jnp.sum(sums, axis=0) * (1.0 / lines)
    return (pair_penalty, pressure.reshape(width), grad)


def solution(mesh):
    return jax.shard_map(
        per_device,
        mesh=mesh,
        in_specs=(
            P("line", None),
            P("line"),
            P(("groups", "line")),
            P(("groups", "line")),
            P(("groups", "line"), None),
            P(("groups", "line")),
        ),
        out_specs=(P(("groups", "line"), None), P(("groups", "line")), P(("groups", "line"), None)),
        check_vma=False,
    )
```

```python
import functools

import jax
import jax.numpy as jnp
from jax import lax
from jax.experimental import pallas as pl
from jax.experimental.pallas import tpu as pltpu
from jax.sharding import PartitionSpec as P

F32 = jnp.float32
BF16 = jnp.bfloat16


def iota(shape, dim, dtype=jnp.int32):
    return lax.broadcasted_iota(jnp.int32, shape, dim).astype(dtype)


def split3(x):
    top = x.astype(BF16).astype(F32)
    rest = x - top
    middle = rest.astype(BF16).astype(F32)
    return top, middle, rest - middle


def pack_kernel(first_ref, counts_ref, lodf_ref, base_ref, second_ref, out_ref):
    width = lodf_ref.shape[0]
    firsts, cands = second_ref.shape
    anchor = lax.axis_index("line") * width
    square = lodf_ref[:, pl.ds(pl.multiple_of(anchor, width), width)]
    row = iota((firsts, width), 0)
    lane = iota((firsts, width), 1)
    head = jnp.zeros((firsts, width), jnp.int32)
    lives = jnp.zeros((firsts, cands), jnp.int32)
    heads_row = jnp.zeros((1, width), F32)
    for j in range(firsts):
        local = first_ref[j] - anchor
        head = jnp.where(row == j, local, head)
        lives = jnp.where(row == j, counts_ref[j], lives)
        heads_row = jnp.where(iota((1, width), 1) == j, local.astype(F32), heads_row)
    hot = (lane == head).astype(BF16)
    first_row = jnp.dot(hot, square, preferred_element_type=F32)
    first_column = lax.dot_general(
        hot, square, (((1,), (1,)), ((), ())), preferred_element_type=F32
    )
    second = second_ref[...] - anchor
    p = jnp.take_along_axis(first_row, second, axis=1)
    q = jnp.take_along_axis(first_column, second, axis=1)
    live = iota((firsts, cands), 1) < lives
    ids = jnp.where(live, second.astype(F32), -1.0)
    top, middle, low = split3(base_ref[...])
    fill = jnp.zeros((firsts - 4, width), F32)
    block = jnp.concatenate([p, q, ids, top, middle, low, heads_row, fill], axis=0)
    out_ref[0] = block.astype(BF16)


def tile_at(place, me, rounds):
    for r in range(rounds):
        bit = lax.bitwise_and(lax.shift_right_logical(place, r), 1)
        me = lax.bitwise_xor(me, lax.shift_left(bit, rounds - 1 - r))
    return me


def screen_kernel(
    rounds,
    near_ref,
    far_ref,
    lodf_ref,
    base_ref,
    limits_ref,
    near_squares_ref,
    far_squares_ref,
    pressure_ref,
    grad_ref,
    low_ref,
    high_ref,
    sum_ref,
    one_ref,
    two_ref,
    ids_ref,
    heads_ref,
    square_ref,
):
    width = lodf_ref.shape[0]
    half, firsts, cands = near_squares_ref.shape
    tiles = 2 * half
    me = lax.axis_index("line")

    limit = 0.01 * limits_ref[...].astype(F32)
    base = base_ref[...]
    low_ref[...] = jnp.transpose(jnp.broadcast_to(-limit - base, (width, width)))
    high_ref[...] = jnp.transpose(jnp.broadcast_to(limit - base, (width, width)))
    sum_ref[...] = jnp.zeros_like(sum_ref)

    got = jnp.concatenate([near_ref[...], far_ref[...]], axis=0).astype(F32)
    shape = (tiles, firsts, cands)
    flat = (tiles * firsts, cands)
    p = got[:, :firsts].reshape(flat)
    q = got[:, firsts : 2 * firsts].reshape(flat)
    ids = got[:, 2 * firsts : 3 * firsts].reshape(flat)
    tail = got[:, 3 * firsts :]
    flows = jnp.broadcast_to(
        tail[:, 0:1] + tail[:, 1:2] + tail[:, 2:3], shape
    ).reshape(flat)
    own = iota(shape, 2) == iota(shape, 1)
    heads = jnp.sum(
        jnp.where(own, jnp.broadcast_to(tail[:, 3:4], shape), 0.0).reshape(flat),
        axis=1,
        keepdims=True,
    )
    lane = iota(flat, 1, F32)
    first_flow = jnp.sum(jnp.where(lane == heads, flows, 0.0), axis=1, keepdims=True)
    live = ids >= 0.0
    second_flow = jnp.take_along_axis(
        flows, jnp.maximum(ids, 0.0).astype(jnp.int32), axis=1
    )
    det = 1.0 - p * q
    one_ref[...] = jnp.where(live, (first_flow + p * second_flow) / det, 0.0)
    two_ref[...] = jnp.where(live, (second_flow + q * first_flow) / det, 0.0)
    ids_ref[...] = ids
    heads_ref[...] = jnp.broadcast_to(heads, flat)

    line = iota((width, cands), 0, F32)
    column = iota((width, cands), 0, F32).astype(BF16)
    lane_row = iota((1, width), 1, F32)

    def wide(row):
        return jnp.broadcast_to(row, (width, cands)).astype(BF16)

    def one_tile(place, masked):
        tile = tile_at(jnp.int32(place), me, rounds)
        rows = pl.ds(pl.multiple_of(place * firsts, firsts), firsts)
        span = pl.ds(pl.multiple_of(tile * width, width), width)
        factors = lodf_ref[:, span]
        twice = jnp.concatenate([factors, factors], axis=1)
        scale_one = one_ref[rows, :]
        scale_two = two_ref[rows, :]
        second = ids_ref[rows, :]
        first = heads_ref[rows, :]
        alive = (second >= 0.0).astype(F32)
        grad = jnp.zeros((width, width), F32)
        total = sum_ref[...]
        squares = []
        group = 2
        for start in range(0, firsts, group):
            hots, tops, lows = [], [], []
            for j in range(start, start + group):
                pick = slice(j, j + 1)
                one_top = scale_one[pick].astype(BF16).astype(F32)
                two_top = scale_two[pick].astype(BF16).astype(F32)
                is_two = column == wide(second[pick])
                is_one = column == wide(first[pick])
                zero = jnp.zeros((), BF16)
                hots.append(jnp.where(is_two, jnp.ones((), BF16), zero))
                tops.append(
                    jnp.where(
                        is_one, wide(one_top), jnp.where(is_two, wide(two_top), zero)
                    )
                )
                lows.append(
                    jnp.where(
                        is_one,
                        wide(scale_one[pick] - one_top),
                        jnp.where(is_two, wide(scale_two[pick] - two_top), zero),
                    )
                )
            hot = jnp.concatenate(hots, axis=1)
            mix = jnp.concatenate(
                [jnp.concatenate(tops, axis=1), jnp.concatenate(lows, axis=1)], axis=0
            )
            change = jnp.dot(twice, mix, preferred_element_type=F32)
            weights = []
            for j in range(start, start + group):
                pick = slice(j, j + 1)
                part = change[:, (j - start) * cands : (j - start + 1) * cands]
                excess = part - jnp.minimum(
                    jnp.maximum(part, low_ref[...]), high_ref[...]
                )
                keep = alive[pick]
                if masked:
                    out = (line == second[pick]) | (line == first[pick])
                    excess = jnp.where(out, 0.0, excess)
                excess = excess * keep
                squares.append(jnp.sum(excess * excess, axis=0, keepdims=True))
                total = total + excess
                weights.append((excess * (2.0 * scale_two[pick])).astype(BF16))
                lead = jnp.sum(
                    excess * (2.0 * scale_one[pick]), axis=1, keepdims=True
                )
                grad = grad + jnp.where(lane_row == first[pick], lead, 0.0)
            grad = grad + lax.dot_general(
                jnp.concatenate(weights, axis=1),
                hot,
                (((1,), (1,)), ((), ())),
                preferred_element_type=F32,
            )
        sum_ref[...] = total
        square_ref[place] = jnp.concatenate(squares, axis=0)
        grad_ref[:, span] = (grad * (1.0 / cands)).astype(BF16)

    one_tile(0, True)

    @pl.loop(1, tiles)
    def _(place):
        one_tile(place, False)

    near_squares_ref[...] = square_ref[:half]
    far_squares_ref[...] = square_ref[half:]

    pressure_ref[...] = jnp.sum(jnp.transpose(sum_ref[...]), axis=0, keepdims=True) * (
        2.0 / (tiles * firsts * cands)
    )


def per_device(lodf, limits, base_flow, first_ids, second_ids, counts):
    width, lines = lodf.shape
    firsts, cands = second_ids.shape
    tiles = lax.axis_size("line")
    rounds = tiles.bit_length() - 1

    def exchange(x, bit):
        return lax.ppermute(x, "line", [(i, i ^ bit) for i in range(tiles)])

    vmem = pl.BlockSpec(memory_space=pltpu.VMEM)
    smem = pl.BlockSpec(memory_space=pltpu.SMEM)
    base = base_flow.reshape(1, width)
    packed = pl.pallas_call(
        pack_kernel,
        out_shape=jax.ShapeDtypeStruct((1, 4 * firsts, cands), BF16),
        in_specs=[smem, smem, vmem, vmem, vmem],
        out_specs=vmem,
        name="pack_pairs",
    )(first_ids, counts, lodf, base, second_ids)
    near, far = packed, exchange(packed, tiles // 2)
    for r in range(1, rounds):
        near = jnp.concatenate([near, far], axis=0)
        far = exchange(near, tiles >> (r + 1))
    pairs = tiles * firsts
    near_squares, far_squares, pressure, grad = pl.pallas_call(
        functools.partial(screen_kernel, rounds),
        out_shape=(
            jax.ShapeDtypeStruct((tiles // 2, firsts, cands), F32),
            jax.ShapeDtypeStruct((tiles // 2, firsts, cands), F32),
            jax.ShapeDtypeStruct((1, width), F32),
            jax.ShapeDtypeStruct((width, lines), BF16),
        ),
        in_specs=[vmem] * 5,
        out_specs=(vmem,) * 4,
        scratch_shapes=[
            pltpu.VMEM((width, width), F32),
            pltpu.VMEM((width, width), F32),
            pltpu.VMEM((width, cands), F32),
            pltpu.VMEM((pairs, cands), F32),
            pltpu.VMEM((pairs, cands), F32),
            pltpu.VMEM((pairs, cands), F32),
            pltpu.VMEM((pairs, cands), F32),
            pltpu.VMEM((tiles, firsts, cands), F32),
        ],
        compiler_params=pltpu.CompilerParams(vmem_limit_bytes=32 * 1024 * 1024),
        name="screen_lines",
    )(near, far, lodf, base, limits.reshape(1, width))
    sums = near_squares + exchange(far_squares, 1)
    for r in range(1, rounds):
        half = sums.shape[0] // 2
        sums = sums[:half] + exchange(sums[half:], 1 << r)
    pair_penalty = sums[0] * (1.0 / lines)
    return (pair_penalty, pressure.reshape(width), grad)


def solution(mesh):
    return jax.shard_map(
        per_device,
        mesh=mesh,
        in_specs=(
            P("line", None),
            P("line"),
            P(("groups", "line")),
            P(("groups", "line")),
            P(("groups", "line"), None),
            P(("groups", "line")),
        ),
        out_specs=(P(("groups", "line"), None), P(("groups", "line")), P(("groups", "line"), None)),
        check_vma=False,
    )
```

```python
import jax
import jax.numpy as jnp
from jax import lax
from jax.experimental import pallas as pl
from jax.experimental.pallas import tpu as pltpu
from jax.sharding import PartitionSpec as P

F32 = jnp.float32
BF16 = jnp.bfloat16


def iota(shape, dim, dtype=jnp.int32):
    return lax.broadcasted_iota(jnp.int32, shape, dim).astype(dtype)


def split3(x):
    top = x.astype(BF16).astype(F32)
    rest = x - top
    middle = rest.astype(BF16).astype(F32)
    return top, middle, rest - middle


def pack_kernel(
    first_ref, counts_ref, lodf_ref, base_ref, limits_ref, second_ref, out_ref
):
    width = lodf_ref.shape[0]
    firsts, cands = second_ref.shape
    peers = out_ref.shape[0]
    anchor = lax.axis_index("line") * width
    square = lodf_ref[:, pl.ds(pl.multiple_of(anchor, width), width)]
    row = iota((firsts, width), 0)
    lane = iota((firsts, width), 1)
    head = jnp.zeros((firsts, width), jnp.int32)
    lives = jnp.zeros((firsts, cands), jnp.int32)
    heads_row = jnp.zeros((1, width), F32)
    for j in range(firsts):
        local = first_ref[j] - anchor
        head = jnp.where(row == j, local, head)
        lives = jnp.where(row == j, counts_ref[j], lives)
        heads_row = jnp.where(iota((1, width), 1) == j, local.astype(F32), heads_row)
    hot = (lane == head).astype(BF16)
    first_row = jnp.dot(hot, square, preferred_element_type=F32)
    first_column = lax.dot_general(
        hot, square, (((1,), (1,)), ((), ())), preferred_element_type=F32
    )
    second = second_ref[...] - anchor
    p = jnp.take_along_axis(first_row, second, axis=1)
    q = jnp.take_along_axis(first_column, second, axis=1)
    live = iota((firsts, cands), 1) < lives
    ids = jnp.where(live, second.astype(F32), -1.0)
    top, middle, low = split3(base_ref[...])
    limits = limits_ref[...].astype(F32)
    fill = jnp.zeros((firsts - 5, width), F32)
    block = jnp.concatenate(
        [p, q, ids, top, middle, low, heads_row, limits, fill], axis=0
    )
    block = block.astype(BF16)
    for peer in range(peers):
        out_ref[peer] = block


def screen_kernel(
    got_ref,
    lodf_ref,
    squares_ref,
    pressure_ref,
    grad_ref,
    low_ref,
    high_ref,
    sum_ref,
    one_ref,
    two_ref,
    ids_ref,
    heads_ref,
):
    width = lodf_ref.shape[0]
    tiles = got_ref.shape[0]
    firsts = squares_ref.shape[1]
    cands = squares_ref.shape[2]
    me = lax.axis_index("line")

    mine = got_ref[me].astype(F32)[3 * firsts :]
    base = mine[0:1] + mine[1:2] + mine[2:3]
    limit = 0.01 * mine[4:5]
    low_ref[...] = jnp.transpose(jnp.broadcast_to(-limit - base, (width, width)))
    high_ref[...] = jnp.transpose(jnp.broadcast_to(limit - base, (width, width)))
    sum_ref[...] = jnp.zeros_like(sum_ref)

    got = got_ref[...].astype(F32)
    shape = (tiles, firsts, cands)
    flat = (tiles * firsts, cands)
    p = got[:, :firsts].reshape(flat)
    q = got[:, firsts : 2 * firsts].reshape(flat)
    ids = got[:, 2 * firsts : 3 * firsts].reshape(flat)
    tail = got[:, 3 * firsts :]
    flows = jnp.broadcast_to(
        tail[:, 0:1] + tail[:, 1:2] + tail[:, 2:3], shape
    ).reshape(flat)
    own = iota(shape, 2) == iota(shape, 1)
    heads = jnp.sum(
        jnp.where(own, jnp.broadcast_to(tail[:, 3:4], shape), 0.0).reshape(flat),
        axis=1,
        keepdims=True,
    )
    lane = iota(flat, 1, F32)
    first_flow = jnp.sum(jnp.where(lane == heads, flows, 0.0), axis=1, keepdims=True)
    live = ids >= 0.0
    second_flow = jnp.take_along_axis(
        flows, jnp.maximum(ids, 0.0).astype(jnp.int32), axis=1
    )
    det = 1.0 - p * q
    one_ref[...] = jnp.where(live, (first_flow + p * second_flow) / det, 0.0)
    two_ref[...] = jnp.where(live, (second_flow + q * first_flow) / det, 0.0)
    ids_ref[...] = ids
    heads_ref[...] = jnp.broadcast_to(heads, flat)

    line = iota((width, cands), 0, F32)
    column = iota((width, cands), 0, F32).astype(BF16)

    def wide(row):
        return jnp.broadcast_to(row, (width, cands)).astype(BF16)

    def one_tile(tile, masked):
        rows = pl.ds(pl.multiple_of(tile * firsts, firsts), firsts)
        span = pl.ds(pl.multiple_of(tile * width, width), width)
        factors = lodf_ref[:, span]
        twice = jnp.concatenate([factors, factors], axis=1)
        scale_one = one_ref[rows, :]
        scale_two = two_ref[rows, :]
        second = ids_ref[rows, :]
        first = heads_ref[rows, :]
        alive = (second >= 0.0).astype(F32)
        grad = jnp.zeros((width, width), F32)
        total = sum_ref[...]
        squares = []
        group = 2
        for start in range(0, firsts, group):
            hots, heads, tops, lows = [], [], [], []
            for j in range(start, start + group):
                pick = slice(j, j + 1)
                one_top = scale_one[pick].astype(BF16).astype(F32)
                two_top = scale_two[pick].astype(BF16).astype(F32)
                is_two = column == wide(second[pick])
                is_one = column == wide(first[pick])
                zero = jnp.zeros((), BF16)
                hots.append(jnp.where(is_two, jnp.ones((), BF16), zero))
                heads.append(jnp.where(is_one, jnp.ones((), BF16), zero))
                tops.append(
                    jnp.where(
                        is_one, wide(one_top), jnp.where(is_two, wide(two_top), zero)
                    )
                )
                lows.append(
                    jnp.where(
                        is_one,
                        wide(scale_one[pick] - one_top),
                        jnp.where(is_two, wide(scale_two[pick] - two_top), zero),
                    )
                )
            mix = jnp.concatenate(
                [jnp.concatenate(tops, axis=1), jnp.concatenate(lows, axis=1)], axis=0
            )
            change = jnp.dot(twice, mix, preferred_element_type=F32)
            weights, leads, rests = [], [], []
            for j in range(start, start + group):
                pick = slice(j, j + 1)
                part = change[:, (j - start) * cands : (j - start + 1) * cands]
                excess = part - jnp.minimum(
                    jnp.maximum(part, low_ref[...]), high_ref[...]
                )
                keep = alive[pick]
                if masked:
                    out = (line == second[pick]) | (line == first[pick])
                    excess = jnp.where(out, 0.0, excess)
                excess = excess * keep
                squares.append(jnp.sum(excess * excess, axis=0, keepdims=True))
                total = total + excess
                weights.append((excess * (2.0 * scale_two[pick])).astype(BF16))
                lead = excess * (2.0 * scale_one[pick])
                leads.append(lead.astype(BF16))
                rests.append((lead - leads[-1].astype(F32)).astype(BF16))
            grad = grad + lax.dot_general(
                jnp.concatenate(weights + leads + rests, axis=1),
                jnp.concatenate(hots + heads + heads, axis=1),
                (((1,), (1,)), ((), ())),
                preferred_element_type=F32,
            )
        sum_ref[...] = total
        squares_ref[tile] = (
            jnp.concatenate(squares, axis=0) * (1.0 / (tiles * width))
        ).astype(BF16)
        grad_ref[:, span] = (grad * (1.0 / cands)).astype(BF16)

    one_tile(me, True)

    @pl.loop(1, tiles)
    def _(step):
        tile = me + step
        one_tile(jnp.where(tile >= tiles, tile - tiles, tile), False)

    pressure_ref[...] = jnp.sum(jnp.transpose(sum_ref[...]), axis=0, keepdims=True) * (
        2.0 / (tiles * firsts * cands)
    )


def per_device(lodf, limits, base_flow, first_ids, second_ids, counts):
    width, lines = lodf.shape
    firsts, cands = second_ids.shape
    tiles = lax.axis_size("line")
    vmem = pl.BlockSpec(memory_space=pltpu.VMEM)
    smem = pl.BlockSpec(memory_space=pltpu.SMEM)
    base = base_flow.reshape(1, width)
    packed = pl.pallas_call(
        pack_kernel,
        out_shape=jax.ShapeDtypeStruct((tiles, 4 * firsts, cands), BF16),
        in_specs=[smem, smem, vmem, vmem, vmem, vmem],
        out_specs=vmem,
        compiler_params=pltpu.CompilerParams(vmem_limit_bytes=8 * 1024 * 1024),
        name="pack_pairs",
    )(first_ids, counts, lodf, base, limits.reshape(1, width), second_ids)
    got = lax.all_to_all(packed, "line", split_axis=0, concat_axis=0, tiled=True)
    pairs = tiles * firsts
    squares, pressure, grad = pl.pallas_call(
        screen_kernel,
        out_shape=(
            jax.ShapeDtypeStruct((tiles, firsts, cands), BF16),
            jax.ShapeDtypeStruct((1, width), F32),
            jax.ShapeDtypeStruct((width, lines), BF16),
        ),
        in_specs=[vmem] * 2,
        out_specs=(vmem,) * 3,
        scratch_shapes=[
            pltpu.VMEM((width, width), F32),
            pltpu.VMEM((width, width), F32),
            pltpu.VMEM((width, cands), F32),
            pltpu.VMEM((pairs, cands), F32),
            pltpu.VMEM((pairs, cands), F32),
            pltpu.VMEM((pairs, cands), F32),
            pltpu.VMEM((pairs, cands), F32),
        ],
        compiler_params=pltpu.CompilerParams(vmem_limit_bytes=32 * 1024 * 1024),
        name="screen_lines",
    )(got, lodf)
    sums = lax.all_to_all(squares, "line", split_axis=0, concat_axis=0, tiled=True)
    pair_penalty = jnp.sum(sums.astype(F32), axis=0)
    return (pair_penalty, pressure.reshape(width), grad)


def solution(mesh):
    return jax.shard_map(
        per_device,
        mesh=mesh,
        in_specs=(
            P("line", None),
            P("line"),
            P(("groups", "line")),
            P(("groups", "line")),
            P(("groups", "line"), None),
            P(("groups", "line")),
        ),
        out_specs=(P(("groups", "line"), None), P(("groups", "line")), P(("groups", "line"), None)),
        check_vma=False,
    )
```

```python
import math

import jax
import jax.numpy as jnp
from jax import lax
from jax.experimental import pallas as pl
from jax.experimental.pallas import tpu as pltpu
from jax.sharding import PartitionSpec as P

F32 = jnp.float32
BF16 = jnp.bfloat16


def iota(shape, dim, dtype=jnp.int32):
    return lax.broadcasted_iota(jnp.int32, shape, dim).astype(dtype)


def split3(x):
    top = x.astype(BF16).astype(F32)
    rest = x - top
    middle = rest.astype(BF16).astype(F32)
    return top, middle, rest - middle


def pack_kernel(
    first_ref, counts_ref, lodf_ref, base_ref, limits_ref, second_ref, out_ref
):
    width = lodf_ref.shape[0]
    firsts, cands = second_ref.shape
    peers = out_ref.shape[0]
    anchor = lax.axis_index("line") * width
    square = lodf_ref[:, pl.ds(pl.multiple_of(anchor, width), width)]
    row = iota((firsts, width), 0)
    lane = iota((firsts, width), 1)
    head = jnp.zeros((firsts, width), jnp.int32)
    lives = jnp.zeros((firsts, cands), jnp.int32)
    heads_row = jnp.zeros((1, width), F32)
    for j in range(firsts):
        local = first_ref[j] - anchor
        head = jnp.where(row == j, local, head)
        lives = jnp.where(row == j, counts_ref[j], lives)
        heads_row = jnp.where(iota((1, width), 1) == j, local.astype(F32), heads_row)
    hot = (lane == head).astype(BF16)
    first_row = jnp.dot(hot, square, preferred_element_type=F32)
    first_column = lax.dot_general(
        hot, square, (((1,), (1,)), ((), ())), preferred_element_type=F32
    )
    second = second_ref[...] - anchor
    p = jnp.take_along_axis(first_row, second, axis=1)
    q = jnp.take_along_axis(first_column, second, axis=1)
    live = iota((firsts, cands), 1) < lives
    ids = jnp.where(live, second.astype(F32), -1.0)
    top, middle, low = split3(base_ref[...])
    limits = limits_ref[...].astype(F32)
    fill = jnp.zeros((firsts - 5, width), F32)
    block = jnp.concatenate(
        [p, q, ids, top, middle, low, heads_row, limits, fill], axis=0
    )
    block = block.astype(BF16)
    for peer in range(peers):
        out_ref[peer] = block


def screen_kernel(
    got_ref,
    lodf_ref,
    squares_ref,
    pressure_ref,
    grad_ref,
    low_ref,
    high_ref,
    sum_ref,
    one_ref,
    two_ref,
    ids_ref,
    heads_ref,
):
    width = lodf_ref.shape[0]
    tiles = got_ref.shape[0]
    firsts = squares_ref.shape[1]
    cands = squares_ref.shape[2]
    me = lax.axis_index("line")

    mine = got_ref[me].astype(F32)[3 * firsts :]
    base = mine[0:1] + mine[1:2] + mine[2:3]
    limit = 0.01 * mine[4:5]
    low_ref[...] = jnp.transpose(jnp.broadcast_to(-limit - base, (width, width)))
    high_ref[...] = jnp.transpose(jnp.broadcast_to(limit - base, (width, width)))
    sum_ref[...] = jnp.zeros_like(sum_ref)

    got = got_ref[...].astype(F32)
    shape = (tiles, firsts, cands)
    flat = (tiles * firsts, cands)
    p = got[:, :firsts].reshape(flat)
    q = got[:, firsts : 2 * firsts].reshape(flat)
    ids = got[:, 2 * firsts : 3 * firsts].reshape(flat)
    tail = got[:, 3 * firsts :]
    flows = jnp.broadcast_to(
        tail[:, 0:1] + tail[:, 1:2] + tail[:, 2:3], shape
    ).reshape(flat)
    own = iota(shape, 2) == iota(shape, 1)
    heads = jnp.sum(
        jnp.where(own, jnp.broadcast_to(tail[:, 3:4], shape), 0.0).reshape(flat),
        axis=1,
        keepdims=True,
    )
    lane = iota(flat, 1, F32)
    first_flow = jnp.sum(jnp.where(lane == heads, flows, 0.0), axis=1, keepdims=True)
    live = ids >= 0.0
    second_flow = jnp.take_along_axis(
        flows, jnp.maximum(ids, 0.0).astype(jnp.int32), axis=1
    )
    det = 1.0 - p * q
    one_ref[...] = jnp.where(live, (first_flow + p * second_flow) / det, 0.0)
    two_ref[...] = jnp.where(live, (second_flow + q * first_flow) / det, 0.0)
    ids_ref[...] = ids
    heads_ref[...] = jnp.broadcast_to(heads, flat)

    line = iota((width, cands), 0, F32)
    column = iota((width, cands), 0, F32).astype(BF16)
    lane_row = iota((1, width), 1, F32)

    def wide(row):
        return jnp.broadcast_to(row, (width, cands)).astype(BF16)

    def one_tile(tile, masked):
        rows = pl.ds(pl.multiple_of(tile * firsts, firsts), firsts)
        span = pl.ds(pl.multiple_of(tile * width, width), width)
        factors = lodf_ref[:, span]
        twice = jnp.concatenate([factors, factors], axis=1)
        scale_one = one_ref[rows, :]
        scale_two = two_ref[rows, :]
        second = ids_ref[rows, :]
        first = heads_ref[rows, :]
        alive = (second >= 0.0).astype(F32)
        grad = jnp.zeros((width, width), F32)
        total = sum_ref[...]
        squares = []
        group = math.gcd(firsts, 4)
        for start in range(0, firsts, group):
            hots, tops, lows = [], [], []
            for j in range(start, start + group):
                pick = slice(j, j + 1)
                one_top = scale_one[pick].astype(BF16).astype(F32)
                two_top = scale_two[pick].astype(BF16).astype(F32)
                is_two = column == wide(second[pick])
                is_one = column == wide(first[pick])
                zero = jnp.zeros((), BF16)
                hots.append(jnp.where(is_two, jnp.ones((), BF16), zero))
                tops.append(
                    jnp.where(
                        is_one, wide(one_top), jnp.where(is_two, wide(two_top), zero)
                    )
                )
                lows.append(
                    jnp.where(
                        is_one,
                        wide(scale_one[pick] - one_top),
                        jnp.where(is_two, wide(scale_two[pick] - two_top), zero),
                    )
                )
            mix = jnp.concatenate(
                [jnp.concatenate(tops, axis=1), jnp.concatenate(lows, axis=1)], axis=0
            )
            change = jnp.dot(twice, mix, preferred_element_type=F32)
            weights = []
            for j in range(start, start + group):
                pick = slice(j, j + 1)
                part = change[:, (j - start) * cands : (j - start + 1) * cands]
                excess = part - jnp.minimum(
                    jnp.maximum(part, low_ref[...]), high_ref[...]
                )
                keep = alive[pick]
                if masked:
                    out = (line == second[pick]) | (line == first[pick])
                    excess = jnp.where(out, 0.0, excess)
                excess = excess * keep
                squares.append(jnp.sum(excess * excess, axis=0, keepdims=True))
                total = total + excess
                weights.append((excess * (2.0 * scale_two[pick])).astype(BF16))
                lead = jnp.sum(
                    excess * (2.0 * scale_one[pick]), axis=1, keepdims=True
                )
                grad = grad + jnp.where(lane_row == first[pick], lead, 0.0)
            grad = grad + lax.dot_general(
                jnp.concatenate(weights, axis=1),
                jnp.concatenate(hots, axis=1),
                (((1,), (1,)), ((), ())),
                preferred_element_type=F32,
            )
        sum_ref[...] = total
        squares_ref[tile] = (
            jnp.concatenate(squares, axis=0) * (1.0 / (tiles * width))
        ).astype(BF16)
        grad_ref[:, span] = (grad * (1.0 / cands)).astype(BF16)

    one_tile(me, True)

    @pl.loop(1, tiles)
    def _(step):
        tile = me + step
        one_tile(jnp.where(tile >= tiles, tile - tiles, tile), False)

    pressure_ref[...] = jnp.sum(jnp.transpose(sum_ref[...]), axis=0, keepdims=True) * (
        2.0 / (tiles * firsts * cands)
    )


def per_device(lodf, limits, base_flow, first_ids, second_ids, counts):
    width, lines = lodf.shape
    firsts, cands = second_ids.shape
    tiles = lax.axis_size("line")
    vmem = pl.BlockSpec(memory_space=pltpu.VMEM)
    smem = pl.BlockSpec(memory_space=pltpu.SMEM)
    base = base_flow.reshape(1, width)
    packed = pl.pallas_call(
        pack_kernel,
        out_shape=jax.ShapeDtypeStruct((tiles, 4 * firsts, cands), BF16),
        in_specs=[smem, smem, vmem, vmem, vmem, vmem],
        out_specs=vmem,
        name="pack_pairs",
    )(first_ids, counts, lodf, base, limits.reshape(1, width), second_ids)
    got = lax.all_to_all(packed, "line", split_axis=0, concat_axis=0, tiled=True)
    pairs = tiles * firsts
    squares, pressure, grad = pl.pallas_call(
        screen_kernel,
        out_shape=(
            jax.ShapeDtypeStruct((tiles, firsts, cands), BF16),
            jax.ShapeDtypeStruct((1, width), F32),
            jax.ShapeDtypeStruct((width, lines), BF16),
        ),
        in_specs=[vmem] * 2,
        out_specs=(vmem,) * 3,
        scratch_shapes=[
            pltpu.VMEM((width, width), F32),
            pltpu.VMEM((width, width), F32),
            pltpu.VMEM((width, cands), F32),
            pltpu.VMEM((pairs, cands), F32),
            pltpu.VMEM((pairs, cands), F32),
            pltpu.VMEM((pairs, cands), F32),
            pltpu.VMEM((pairs, cands), F32),
        ],
        compiler_params=pltpu.CompilerParams(vmem_limit_bytes=32 * 1024 * 1024),
        name="screen_lines",
    )(got, lodf)
    sums = lax.all_to_all(squares, "line", split_axis=0, concat_axis=0, tiled=True)
    pair_penalty = jnp.sum(sums.astype(F32), axis=0)
    return (pair_penalty, pressure.reshape(width), grad)


def solution(mesh):
    return jax.shard_map(
        per_device,
        mesh=mesh,
        in_specs=(
            P("line", None),
            P("line"),
            P(("groups", "line")),
            P(("groups", "line")),
            P(("groups", "line"), None),
            P(("groups", "line")),
        ),
        out_specs=(P(("groups", "line"), None), P(("groups", "line")), P(("groups", "line"), None)),
        check_vma=False,
    )
```

```python
import math

import jax
import jax.numpy as jnp
from jax import lax
from jax.experimental import pallas as pl
from jax.experimental.pallas import tpu as pltpu
from jax.sharding import PartitionSpec as P

F32 = jnp.float32
BF16 = jnp.bfloat16


def iota(shape, dim, dtype=jnp.int32):
    return lax.broadcasted_iota(jnp.int32, shape, dim).astype(dtype)


def split3(x):
    top = x.astype(BF16).astype(F32)
    rest = x - top
    middle = rest.astype(BF16).astype(F32)
    return top, middle, rest - middle


def pack_kernel(
    first_ref, counts_ref, lodf_ref, base_ref, limits_ref, second_ref, out_ref
):
    width = lodf_ref.shape[0]
    firsts, cands = second_ref.shape
    peers = out_ref.shape[0]
    anchor = lax.axis_index("line") * width
    square = lodf_ref[:, pl.ds(pl.multiple_of(anchor, width), width)]
    row = iota((firsts, width), 0)
    lane = iota((firsts, width), 1)
    head = jnp.zeros((firsts, width), jnp.int32)
    lives = jnp.zeros((firsts, cands), jnp.int32)
    heads_row = jnp.zeros((1, width), F32)
    for j in range(firsts):
        local = first_ref[j] - anchor
        head = jnp.where(row == j, local, head)
        lives = jnp.where(row == j, counts_ref[j], lives)
        heads_row = jnp.where(iota((1, width), 1) == j, local.astype(F32), heads_row)
    hot = (lane == head).astype(BF16)
    first_row = jnp.dot(hot, square, preferred_element_type=F32)
    first_column = lax.dot_general(
        hot, square, (((1,), (1,)), ((), ())), preferred_element_type=F32
    )
    second = second_ref[...] - anchor
    p = jnp.take_along_axis(first_row, second, axis=1)
    q = jnp.take_along_axis(first_column, second, axis=1)
    live = iota((firsts, cands), 1) < lives
    ids = jnp.where(live, second.astype(F32), -1.0)
    top, middle, low = split3(base_ref[...])
    limits = limits_ref[...].astype(F32)
    fill = jnp.zeros((firsts - 5, width), F32)
    block = jnp.concatenate(
        [p, q, ids, top, middle, low, heads_row, limits, fill], axis=0
    )
    block = block.astype(BF16)
    for peer in range(peers):
        out_ref[peer] = block


def coefficients(got, firsts, cands):
    tiles = got.shape[0]
    shape = (tiles, firsts, cands)
    flat = (tiles * firsts, cands)
    p = got[:, :firsts].reshape(flat)
    q = got[:, firsts : 2 * firsts].reshape(flat)
    ids = got[:, 2 * firsts : 3 * firsts].reshape(flat)
    tail = got[:, 3 * firsts :]
    flows = jnp.broadcast_to(
        tail[:, 0:1] + tail[:, 1:2] + tail[:, 2:3], shape
    ).reshape(flat)
    own = iota(shape, 2) == iota(shape, 1)
    heads = jnp.sum(
        jnp.where(own, jnp.broadcast_to(tail[:, 3:4], shape), 0.0).reshape(flat),
        axis=1,
        keepdims=True,
    )
    lane = iota(flat, 1, F32)
    first_flow = jnp.sum(jnp.where(lane == heads, flows, 0.0), axis=1, keepdims=True)
    live = ids >= 0.0
    second_flow = jnp.take_along_axis(
        flows, jnp.maximum(ids, 0.0).astype(jnp.int32), axis=1
    )
    det = 1.0 - p * q
    one = jnp.where(live, (first_flow + p * second_flow) / det, 0.0)
    two = jnp.where(live, (second_flow + q * first_flow) / det, 0.0)
    return one, two, ids, jnp.broadcast_to(heads, flat)


def excess_kernel(
    got_ref,
    lodf_ref,
    squares_ref,
    excess_ref,
    one_ref,
    two_ref,
    ids_ref,
    heads_ref,
    low_ref,
    high_ref,
    slots_ref,
    sems,
):
    width = lodf_ref.shape[0]
    tiles, firsts, cands = squares_ref.shape
    me = lax.axis_index("line")

    mine = got_ref[me].astype(F32)[3 * firsts :]
    base = mine[0:1] + mine[1:2] + mine[2:3]
    limit = 0.01 * mine[4:5]
    low_ref[...] = jnp.transpose(jnp.broadcast_to(-limit - base, (width, width)))
    high_ref[...] = jnp.transpose(jnp.broadcast_to(limit - base, (width, width)))

    one_ref[...], two_ref[...], ids_ref[...], heads_ref[...] = coefficients(
        got_ref[...].astype(F32), firsts, cands
    )
    line = iota((width, cands), 0, F32)
    column = iota((width, cands), 0, F32).astype(BF16)
    zero = jnp.zeros((), BF16)

    def wide(row):
        return jnp.broadcast_to(row, (width, cands)).astype(BF16)

    def tile_of(step):
        tile = me + step
        return jnp.where(tile >= tiles, tile - tiles, tile)

    def sending(step, slot):
        return pltpu.make_async_copy(
            slots_ref.at[slot], excess_ref.at[tile_of(step)], sems.at[slot]
        )

    def one_tile(step, slot, masked):
        tile = tile_of(step)
        rows = pl.ds(pl.multiple_of(tile * firsts, firsts), firsts)
        span = pl.ds(pl.multiple_of(tile * width, width), width)
        factors = lodf_ref[:, span]
        twice = jnp.concatenate([factors, factors], axis=1)
        scale_one = one_ref[rows, :]
        scale_two = two_ref[rows, :]
        second = ids_ref[rows, :]
        first = heads_ref[rows, :]
        squares = []
        group = math.gcd(firsts, 4)
        for start in range(0, firsts, group):
            tops, lows = [], []
            for j in range(start, start + group):
                pick = slice(j, j + 1)
                one_top = scale_one[pick].astype(BF16).astype(F32)
                two_top = scale_two[pick].astype(BF16).astype(F32)
                is_two = column == wide(second[pick])
                is_one = column == wide(first[pick])
                tops.append(
                    jnp.where(
                        is_one, wide(one_top), jnp.where(is_two, wide(two_top), zero)
                    )
                )
                lows.append(
                    jnp.where(
                        is_one,
                        wide(scale_one[pick] - one_top),
                        jnp.where(is_two, wide(scale_two[pick] - two_top), zero),
                    )
                )
            mix = jnp.concatenate(
                [jnp.concatenate(tops, axis=1), jnp.concatenate(lows, axis=1)], axis=0
            )
            change = jnp.dot(twice, mix, preferred_element_type=F32)
            for j in range(start, start + group):
                pick = slice(j, j + 1)
                part = change[:, (j - start) * cands : (j - start + 1) * cands]
                excess = part - jnp.minimum(
                    jnp.maximum(part, low_ref[...]), high_ref[...]
                )
                if masked:
                    out = (line == second[pick]) | (line == first[pick])
                    excess = jnp.where(out, 0.0, excess)
                slots_ref[slot, :, j * cands : (j + 1) * cands] = excess
                squares.append(jnp.sum(excess * excess, axis=0, keepdims=True))
        squares = jnp.where(second >= 0.0, jnp.concatenate(squares, axis=0), 0.0)
        squares_ref[tile] = (squares * (1.0 / (tiles * width))).astype(BF16)

    one_tile(0, 0, True)
    sending(0, 0).start()

    @pl.loop(1, tiles)
    def _(step):
        slot = lax.rem(step, 2)

        @pl.when(step >= 2)
        def _():
            sending(step - 2, slot).wait()

        one_tile(step, slot, False)
        sending(step, slot).start()

    sending(tiles - 2, (tiles - 2) % 2).wait()
    sending(tiles - 1, (tiles - 1) % 2).wait()


def grad_kernel(
    excess_ref,
    one_ref,
    two_ref,
    ids_ref,
    heads_ref,
    pressure_ref,
    grad_ref,
    sum_ref,
    slots_ref,
    sems,
):
    tiles, width, _ = excess_ref.shape
    pairs, cands = ids_ref.shape
    firsts = pairs // tiles
    column = iota((width, cands), 0, F32).astype(BF16)
    lane_row = iota((1, width), 1, F32)

    def fetching(tile, slot):
        return pltpu.make_async_copy(
            excess_ref.at[tile], slots_ref.at[slot], sems.at[slot]
        )

    fetching(0, 0).start()
    sum_ref[...] = jnp.zeros_like(sum_ref)

    @pl.loop(0, tiles)
    def _(tile):
        slot = lax.rem(tile, 2)

        @pl.when(tile + 1 < tiles)
        def _():
            fetching(tile + 1, 1 - slot).start()

        fetching(tile, slot).wait()
        rows = pl.ds(pl.multiple_of(tile * firsts, firsts), firsts)
        span = pl.ds(pl.multiple_of(tile * width, width), width)
        one = 2.0 * one_ref[rows, :]
        two = 2.0 * two_ref[rows, :]
        second = ids_ref[rows, :]
        first = heads_ref[rows, :]
        alive = (second >= 0.0).astype(F32)
        grad = jnp.zeros((width, width), F32)
        total = sum_ref[...]
        group = math.gcd(firsts, 4)
        for start in range(0, firsts, group):
            hots, weights = [], []
            for j in range(start, start + group):
                pick = slice(j, j + 1)
                excess = slots_ref[slot, :, j * cands : (j + 1) * cands]
                total = total + excess * alive[pick]
                hots.append(
                    jnp.where(
                        column
                        == jnp.broadcast_to(second[pick], (width, cands)).astype(BF16),
                        jnp.ones((), BF16),
                        jnp.zeros((), BF16),
                    )
                )
                weights.append((excess * two[pick]).astype(BF16))
                lead = jnp.sum(excess * one[pick], axis=1, keepdims=True)
                grad = grad + jnp.where(lane_row == first[pick], lead, 0.0)
            grad = grad + lax.dot_general(
                jnp.concatenate(weights, axis=1),
                jnp.concatenate(hots, axis=1),
                (((1,), (1,)), ((), ())),
                preferred_element_type=F32,
            )
        sum_ref[...] = total
        grad_ref[:, span] = (grad * (1.0 / cands)).astype(BF16)

    pressure_ref[...] = jnp.sum(jnp.transpose(sum_ref[...]), axis=0, keepdims=True) * (
        2.0 / (tiles * firsts * cands)
    )


def per_device(lodf, limits, base_flow, first_ids, second_ids, counts):
    width, lines = lodf.shape
    firsts, cands = second_ids.shape
    tiles = lax.axis_size("line")
    vmem = pl.BlockSpec(memory_space=pltpu.VMEM)
    smem = pl.BlockSpec(memory_space=pltpu.SMEM)
    base = base_flow.reshape(1, width)
    packed = pl.pallas_call(
        pack_kernel,
        out_shape=jax.ShapeDtypeStruct((tiles, 4 * firsts, cands), BF16),
        in_specs=[smem, smem, vmem, vmem, vmem, vmem],
        out_specs=vmem,
        name="pack_pairs",
    )(first_ids, counts, lodf, base, limits.reshape(1, width), second_ids)
    got = lax.all_to_all(packed, "line", split_axis=0, concat_axis=0, tiled=True)
    pairs = tiles * firsts
    hbm = pl.BlockSpec(memory_space=pl.ANY)
    pair_rows = jax.ShapeDtypeStruct((pairs, cands), F32)
    slots = [
        pltpu.VMEM((2, width, firsts * cands), F32),
        pltpu.SemaphoreType.DMA((2,)),
    ]
    cost = pl.CostEstimate(
        flops=4 * width * width * pairs * cands,
        bytes_accessed=4 * width * pairs * cands,
        transcendentals=0,
    )
    squares, excess, *rest = pl.pallas_call(
        excess_kernel,
        out_shape=(
            jax.ShapeDtypeStruct((tiles, firsts, cands), BF16),
            jax.ShapeDtypeStruct((tiles, width, firsts * cands), F32),
            pair_rows,
            pair_rows,
            pair_rows,
            pair_rows,
        ),
        in_specs=[vmem] * 2,
        out_specs=(vmem, hbm, vmem, vmem, vmem, vmem),
        scratch_shapes=[
            pltpu.VMEM((width, cands), F32),
            pltpu.VMEM((width, cands), F32),
        ]
        + slots,
        compiler_params=pltpu.CompilerParams(vmem_limit_bytes=56 * 1024 * 1024),
        cost_estimate=cost,
        name="screen_lines",
    )(got, lodf)
    sums = lax.all_to_all(squares, "line", split_axis=0, concat_axis=0, tiled=True)
    pressure, grad = pl.pallas_call(
        grad_kernel,
        out_shape=(
            jax.ShapeDtypeStruct((1, width), F32),
            jax.ShapeDtypeStruct((width, lines), BF16),
        ),
        in_specs=[hbm] + [vmem] * 4,
        out_specs=(vmem,) * 2,
        scratch_shapes=[pltpu.VMEM((width, cands), F32)] + slots,
        compiler_params=pltpu.CompilerParams(vmem_limit_bytes=56 * 1024 * 1024),
        cost_estimate=cost,
        name="column_sensitivities",
    )(excess, *rest)
    pair_penalty = jnp.sum(sums.astype(F32), axis=0)
    return (pair_penalty, pressure.reshape(width), grad)


def solution(mesh):
    return jax.shard_map(
        per_device,
        mesh=mesh,
        in_specs=(
            P("line", None),
            P("line"),
            P(("groups", "line")),
            P(("groups", "line")),
            P(("groups", "line"), None),
            P(("groups", "line")),
        ),
        out_specs=(P(("groups", "line"), None), P(("groups", "line")), P(("groups", "line"), None)),
        check_vma=False,
    )
```

```python
import math

import jax
import jax.numpy as jnp
from jax import lax
from jax.experimental import pallas as pl
from jax.experimental.pallas import tpu as pltpu
from jax.sharding import PartitionSpec as P

F32 = jnp.float32
BF16 = jnp.bfloat16
RING = 4


def iota(shape, dim, dtype=jnp.int32):
    return lax.broadcasted_iota(jnp.int32, shape, dim).astype(dtype)


def split3(x):
    top = x.astype(BF16).astype(F32)
    rest = x - top
    middle = rest.astype(BF16).astype(F32)
    return top, middle, rest - middle


def pack_kernel(
    first_ref, counts_ref, lodf_ref, base_ref, limits_ref, second_ref, out_ref
):
    width = lodf_ref.shape[0]
    firsts, cands = second_ref.shape
    peers = out_ref.shape[0]
    anchor = lax.axis_index("line") * width
    square = lodf_ref[:, pl.ds(pl.multiple_of(anchor, width), width)]
    row = iota((firsts, width), 0)
    lane = iota((firsts, width), 1)
    head = jnp.zeros((firsts, width), jnp.int32)
    lives = jnp.zeros((firsts, cands), jnp.int32)
    heads_row = jnp.zeros((1, width), F32)
    for j in range(firsts):
        local = first_ref[j] - anchor
        head = jnp.where(row == j, local, head)
        lives = jnp.where(row == j, counts_ref[j], lives)
        heads_row = jnp.where(iota((1, width), 1) == j, local.astype(F32), heads_row)
    hot = (lane == head).astype(BF16)
    first_row = jnp.dot(hot, square, preferred_element_type=F32)
    first_column = lax.dot_general(
        hot, square, (((1,), (1,)), ((), ())), preferred_element_type=F32
    )
    second = second_ref[...] - anchor
    p = jnp.take_along_axis(first_row, second, axis=1)
    q = jnp.take_along_axis(first_column, second, axis=1)
    live = iota((firsts, cands), 1) < lives
    ids = jnp.where(live, second.astype(F32), -1.0)
    top, middle, low = split3(base_ref[...])
    limits = limits_ref[...].astype(F32)
    fill = jnp.zeros((firsts - 5, width), F32)
    block = jnp.concatenate(
        [p, q, ids, top, middle, low, heads_row, limits, fill], axis=0
    )
    block = block.astype(BF16)
    for peer in range(peers):
        out_ref[peer] = block


def coefficients(got, firsts, cands):
    tiles = got.shape[0]
    shape = (tiles, firsts, cands)
    flat = (tiles * firsts, cands)
    p = got[:, :firsts].reshape(flat)
    q = got[:, firsts : 2 * firsts].reshape(flat)
    ids = got[:, 2 * firsts : 3 * firsts].reshape(flat)
    tail = got[:, 3 * firsts :]
    flows = jnp.broadcast_to(
        tail[:, 0:1] + tail[:, 1:2] + tail[:, 2:3], shape
    ).reshape(flat)
    own = iota(shape, 2) == iota(shape, 1)
    heads = jnp.sum(
        jnp.where(own, jnp.broadcast_to(tail[:, 3:4], shape), 0.0).reshape(flat),
        axis=1,
        keepdims=True,
    )
    lane = iota(flat, 1, F32)
    first_flow = jnp.sum(jnp.where(lane == heads, flows, 0.0), axis=1, keepdims=True)
    live = ids >= 0.0
    second_flow = jnp.take_along_axis(
        flows, jnp.maximum(ids, 0.0).astype(jnp.int32), axis=1
    )
    det = 1.0 - p * q
    one = jnp.where(live, (first_flow + p * second_flow) / det, 0.0)
    two = jnp.where(live, (second_flow + q * first_flow) / det, 0.0)
    return one, two, ids, jnp.broadcast_to(heads, flat)


def excess_kernel(
    got_ref,
    lodf_ref,
    squares_ref,
    excess_ref,
    one_ref,
    two_ref,
    ids_ref,
    heads_ref,
    low_ref,
    high_ref,
    slots_ref,
    sems,
):
    width = lodf_ref.shape[0]
    tiles, firsts, cands = squares_ref.shape
    me = lax.axis_index("line")

    mine = got_ref[me].astype(F32)[3 * firsts :]
    base = mine[0:1] + mine[1:2] + mine[2:3]
    limit = 0.01 * mine[4:5]
    low_ref[...] = jnp.transpose(jnp.broadcast_to(-limit - base, (width, width)))
    high_ref[...] = jnp.transpose(jnp.broadcast_to(limit - base, (width, width)))

    one_ref[...], two_ref[...], ids_ref[...], heads_ref[...] = coefficients(
        got_ref[...].astype(F32), firsts, cands
    )
    line = iota((width, cands), 0, F32)
    column = iota((width, cands), 0, F32).astype(BF16)
    zero = jnp.zeros((), BF16)

    def wide(row):
        return jnp.broadcast_to(row, (width, cands)).astype(BF16)

    def tile_of(step):
        tile = me + step
        return jnp.where(tile >= tiles, tile - tiles, tile)

    def sending(step, slot):
        return pltpu.make_async_copy(
            slots_ref.at[slot], excess_ref.at[tile_of(step)], sems.at[slot]
        )

    def one_tile(step, slot, masked):
        tile = tile_of(step)
        rows = pl.ds(pl.multiple_of(tile * firsts, firsts), firsts)
        span = pl.ds(pl.multiple_of(tile * width, width), width)
        factors = lodf_ref[:, span]
        twice = jnp.concatenate([factors, factors], axis=1)
        scale_one = one_ref[rows, :]
        scale_two = two_ref[rows, :]
        second = ids_ref[rows, :]
        first = heads_ref[rows, :]
        squares = []
        group = math.gcd(firsts, 4)
        for start in range(0, firsts, group):
            tops, lows = [], []
            for j in range(start, start + group):
                pick = slice(j, j + 1)
                one_top = scale_one[pick].astype(BF16).astype(F32)
                two_top = scale_two[pick].astype(BF16).astype(F32)
                is_two = column == wide(second[pick])
                is_one = column == wide(first[pick])
                tops.append(
                    jnp.where(
                        is_one, wide(one_top), jnp.where(is_two, wide(two_top), zero)
                    )
                )
                lows.append(
                    jnp.where(
                        is_one,
                        wide(scale_one[pick] - one_top),
                        jnp.where(is_two, wide(scale_two[pick] - two_top), zero),
                    )
                )
            mix = jnp.concatenate(
                [jnp.concatenate(tops, axis=1), jnp.concatenate(lows, axis=1)], axis=0
            )
            change = jnp.dot(twice, mix, preferred_element_type=F32)
            for j in range(start, start + group):
                pick = slice(j, j + 1)
                part = change[:, (j - start) * cands : (j - start + 1) * cands]
                excess = part - jnp.minimum(
                    jnp.maximum(part, low_ref[...]), high_ref[...]
                )
                if masked:
                    out = (line == second[pick]) | (line == first[pick])
                    excess = jnp.where(out, 0.0, excess)
                slots_ref[slot, :, j * cands : (j + 1) * cands] = excess
                squares.append(jnp.sum(excess * excess, axis=0, keepdims=True))
        squares = jnp.where(second >= 0.0, jnp.concatenate(squares, axis=0), 0.0)
        squares_ref[tile] = (squares * (1.0 / (tiles * width))).astype(BF16)

    one_tile(0, 0, True)
    sending(0, 0).start()

    @pl.loop(1, tiles)
    def _(step):
        slot = lax.rem(step, RING)

        @pl.when(step >= RING)
        def _():
            sending(step - RING, slot).wait()

        one_tile(step, slot, False)
        sending(step, slot).start()

    for step in range(max(tiles - RING, 0), tiles):
        sending(step, step % RING).wait()


def grad_kernel(
    excess_ref,
    one_ref,
    two_ref,
    ids_ref,
    heads_ref,
    pressure_ref,
    grad_ref,
    sum_ref,
    slots_ref,
    sems,
):
    tiles, width, _ = excess_ref.shape
    pairs, cands = ids_ref.shape
    firsts = pairs // tiles
    column = iota((width, cands), 0, F32).astype(BF16)
    lane_row = iota((1, width), 1, F32)

    def fetching(tile, slot):
        return pltpu.make_async_copy(
            excess_ref.at[tile], slots_ref.at[slot], sems.at[slot]
        )

    for tile in range(min(RING - 1, tiles)):
        fetching(tile, tile).start()
    sum_ref[...] = jnp.zeros_like(sum_ref)

    @pl.loop(0, tiles)
    def _(tile):
        slot = lax.rem(tile, RING)

        @pl.when(tile + RING - 1 < tiles)
        def _():
            fetching(tile + RING - 1, lax.rem(tile + RING - 1, RING)).start()

        fetching(tile, slot).wait()
        rows = pl.ds(pl.multiple_of(tile * firsts, firsts), firsts)
        span = pl.ds(pl.multiple_of(tile * width, width), width)
        one = 2.0 * one_ref[rows, :]
        two = 2.0 * two_ref[rows, :]
        second = ids_ref[rows, :]
        first = heads_ref[rows, :]
        alive = (second >= 0.0).astype(F32)
        grad = jnp.zeros((width, width), F32)
        total = sum_ref[...]
        group = math.gcd(firsts, 4)
        for start in range(0, firsts, group):
            hots, weights = [], []
            for j in range(start, start + group):
                pick = slice(j, j + 1)
                excess = slots_ref[slot, :, j * cands : (j + 1) * cands]
                total = total + excess * alive[pick]
                hots.append(
                    jnp.where(
                        column
                        == jnp.broadcast_to(second[pick], (width, cands)).astype(BF16),
                        jnp.ones((), BF16),
                        jnp.zeros((), BF16),
                    )
                )
                weights.append((excess * two[pick]).astype(BF16))
                lead = jnp.sum(excess * one[pick], axis=1, keepdims=True)
                grad = grad + jnp.where(lane_row == first[pick], lead, 0.0)
            grad = grad + lax.dot_general(
                jnp.concatenate(weights, axis=1),
                jnp.concatenate(hots, axis=1),
                (((1,), (1,)), ((), ())),
                preferred_element_type=F32,
            )
        sum_ref[...] = total
        grad_ref[:, span] = (grad * (1.0 / cands)).astype(BF16)

    pressure_ref[...] = jnp.sum(jnp.transpose(sum_ref[...]), axis=0, keepdims=True) * (
        2.0 / (tiles * firsts * cands)
    )


def per_device(lodf, limits, base_flow, first_ids, second_ids, counts):
    width, lines = lodf.shape
    firsts, cands = second_ids.shape
    tiles = lax.axis_size("line")
    vmem = pl.BlockSpec(memory_space=pltpu.VMEM)
    smem = pl.BlockSpec(memory_space=pltpu.SMEM)
    base = base_flow.reshape(1, width)
    packed = pl.pallas_call(
        pack_kernel,
        out_shape=jax.ShapeDtypeStruct((tiles, 4 * firsts, cands), BF16),
        in_specs=[smem, smem, vmem, vmem, vmem, vmem],
        out_specs=vmem,
        name="pack_pairs",
    )(first_ids, counts, lodf, base, limits.reshape(1, width), second_ids)
    got = lax.all_to_all(packed, "line", split_axis=0, concat_axis=0, tiled=True)
    pairs = tiles * firsts
    hbm = pl.BlockSpec(memory_space=pl.ANY)
    pair_rows = jax.ShapeDtypeStruct((pairs, cands), F32)
    slots = [
        pltpu.VMEM((RING, width, firsts * cands), F32),
        pltpu.SemaphoreType.DMA((RING,)),
    ]
    cost = pl.CostEstimate(
        flops=4 * width * width * pairs * cands,
        bytes_accessed=4 * width * pairs * cands,
        transcendentals=0,
    )
    squares, excess, *rest = pl.pallas_call(
        excess_kernel,
        out_shape=(
            jax.ShapeDtypeStruct((tiles, firsts, cands), BF16),
            jax.ShapeDtypeStruct((tiles, width, firsts * cands), F32),
            pair_rows,
            pair_rows,
            pair_rows,
            pair_rows,
        ),
        in_specs=[vmem] * 2,
        out_specs=(vmem, hbm, vmem, vmem, vmem, vmem),
        scratch_shapes=[
            pltpu.VMEM((width, cands), F32),
            pltpu.VMEM((width, cands), F32),
        ]
        + slots,
        compiler_params=pltpu.CompilerParams(vmem_limit_bytes=56 * 1024 * 1024),
        cost_estimate=cost,
        name="screen_lines",
    )(got, lodf)
    sums = lax.all_to_all(squares, "line", split_axis=0, concat_axis=0, tiled=True)
    pressure, grad = pl.pallas_call(
        grad_kernel,
        out_shape=(
            jax.ShapeDtypeStruct((1, width), F32),
            jax.ShapeDtypeStruct((width, lines), BF16),
        ),
        in_specs=[hbm] + [vmem] * 4,
        out_specs=(vmem,) * 2,
        scratch_shapes=[pltpu.VMEM((width, cands), F32)] + slots,
        compiler_params=pltpu.CompilerParams(vmem_limit_bytes=56 * 1024 * 1024),
        cost_estimate=cost,
        name="column_sensitivities",
    )(excess, *rest)
    pair_penalty = jnp.sum(sums.astype(F32), axis=0)
    return (pair_penalty, pressure.reshape(width), grad)


def solution(mesh):
    return jax.shard_map(
        per_device,
        mesh=mesh,
        in_specs=(
            P("line", None),
            P("line"),
            P(("groups", "line")),
            P(("groups", "line")),
            P(("groups", "line"), None),
            P(("groups", "line")),
        ),
        out_specs=(P(("groups", "line"), None), P(("groups", "line")), P(("groups", "line"), None)),
        check_vma=False,
    )
```

```python
import math

import jax
import jax.numpy as jnp
from jax import lax
from jax.experimental import pallas as pl
from jax.experimental.pallas import tpu as pltpu
from jax.sharding import PartitionSpec as P

F32 = jnp.float32
BF16 = jnp.bfloat16
RING = 4


def iota(shape, dim, dtype=jnp.int32):
    return lax.broadcasted_iota(jnp.int32, shape, dim).astype(dtype)


def split3(x):
    top = x.astype(BF16).astype(F32)
    rest = x - top
    middle = rest.astype(BF16).astype(F32)
    return top, middle, rest - middle


def pack_kernel(
    first_ref, counts_ref, lodf_ref, base_ref, limits_ref, second_ref, out_ref
):
    width = lodf_ref.shape[0]
    firsts, cands = second_ref.shape
    peers = out_ref.shape[0]
    anchor = lax.axis_index("line") * width
    square = lodf_ref[:, pl.ds(pl.multiple_of(anchor, width), width)]
    row = iota((firsts, width), 0)
    lane = iota((firsts, width), 1)
    head = jnp.zeros((firsts, width), jnp.int32)
    lives = jnp.zeros((firsts, cands), jnp.int32)
    heads_row = jnp.zeros((1, width), F32)
    for j in range(firsts):
        local = first_ref[j] - anchor
        head = jnp.where(row == j, local, head)
        lives = jnp.where(row == j, counts_ref[j], lives)
        heads_row = jnp.where(iota((1, width), 1) == j, local.astype(F32), heads_row)
    hot = (lane == head).astype(BF16)
    first_row = jnp.dot(hot, square, preferred_element_type=F32)
    first_column = lax.dot_general(
        hot, square, (((1,), (1,)), ((), ())), preferred_element_type=F32
    )
    second = second_ref[...] - anchor
    p = jnp.take_along_axis(first_row, second, axis=1)
    q = jnp.take_along_axis(first_column, second, axis=1)
    live = iota((firsts, cands), 1) < lives
    ids = jnp.where(live, second.astype(F32), -1.0)
    top, middle, low = split3(base_ref[...])
    limits = limits_ref[...].astype(F32)
    fill = jnp.zeros((firsts - 5, width), F32)
    block = jnp.concatenate(
        [p, q, ids, top, middle, low, heads_row, limits, fill], axis=0
    )
    block = block.astype(BF16)
    for peer in range(peers):
        out_ref[peer] = block


def parts(source, target, sem, rows):
    step = rows // 4
    return [
        pltpu.make_async_copy(
            source.at[pl.ds(start, step)], target.at[pl.ds(start, step)], sem
        )
        for start in range(0, rows, step)
    ]


def coefficients(got, firsts, cands):
    tiles = got.shape[0]
    shape = (tiles, firsts, cands)
    flat = (tiles * firsts, cands)
    p = got[:, :firsts].reshape(flat)
    q = got[:, firsts : 2 * firsts].reshape(flat)
    ids = got[:, 2 * firsts : 3 * firsts].reshape(flat)
    tail = got[:, 3 * firsts :]
    flows = jnp.broadcast_to(
        tail[:, 0:1] + tail[:, 1:2] + tail[:, 2:3], shape
    ).reshape(flat)
    own = iota(shape, 2) == iota(shape, 1)
    heads = jnp.sum(
        jnp.where(own, jnp.broadcast_to(tail[:, 3:4], shape), 0.0).reshape(flat),
        axis=1,
        keepdims=True,
    )
    lane = iota(flat, 1, F32)
    first_flow = jnp.sum(jnp.where(lane == heads, flows, 0.0), axis=1, keepdims=True)
    live = ids >= 0.0
    second_flow = jnp.take_along_axis(
        flows, jnp.maximum(ids, 0.0).astype(jnp.int32), axis=1
    )
    det = 1.0 - p * q
    one = jnp.where(live, (first_flow + p * second_flow) / det, 0.0)
    two = jnp.where(live, (second_flow + q * first_flow) / det, 0.0)
    return one, two, ids, jnp.broadcast_to(heads, flat)


def screen_kernel(
    got_ref,
    lodf_ref,
    squares_ref,
    pressure_ref,
    ids_ref,
    weighted_ref,
    lead_ref,
    one_ref,
    two_ref,
    heads_ref,
    low_ref,
    high_ref,
    sum_ref,
    slots_ref,
    leads_ref,
    sems,
):
    width = lodf_ref.shape[0]
    tiles, firsts, cands = squares_ref.shape
    me = lax.axis_index("line")

    mine = got_ref[me].astype(F32)[3 * firsts :]
    base = mine[0:1] + mine[1:2] + mine[2:3]
    limit = 0.01 * mine[4:5]
    low_ref[...] = jnp.transpose(jnp.broadcast_to(-limit - base, (width, width)))
    high_ref[...] = jnp.transpose(jnp.broadcast_to(limit - base, (width, width)))

    one_ref[...], two_ref[...], ids_ref[...], heads_ref[...] = coefficients(
        got_ref[...].astype(F32), firsts, cands
    )
    sum_ref[...] = jnp.zeros_like(sum_ref)
    line = iota((width, cands), 0, F32)
    lane_row = iota((1, width), 1, F32)
    column = iota((width, cands), 0, F32).astype(BF16)
    zero = jnp.zeros((), BF16)

    def wide(row):
        return jnp.broadcast_to(row, (width, cands)).astype(BF16)

    def tile_of(step):
        tile = me + step
        return jnp.where(tile >= tiles, tile - tiles, tile)

    def sends(step, slot):
        tile = tile_of(step)
        return parts(
            slots_ref.at[slot], weighted_ref.at[tile], sems.at[0, slot], width
        ) + [
            pltpu.make_async_copy(
                leads_ref.at[slot], lead_ref.at[tile], sems.at[1, slot]
            )
        ]

    def send(step, slot):
        for copy in sends(step, slot):
            copy.start()

    def sent(step, slot):
        tile = tile_of(step)
        pltpu.make_async_copy(
            slots_ref.at[slot], weighted_ref.at[tile], sems.at[0, slot]
        ).wait()
        pltpu.make_async_copy(
            leads_ref.at[slot], lead_ref.at[tile], sems.at[1, slot]
        ).wait()

    def one_tile(step, slot, masked):
        tile = tile_of(step)
        rows = pl.ds(pl.multiple_of(tile * firsts, firsts), firsts)
        span = pl.ds(pl.multiple_of(tile * width, width), width)
        factors = lodf_ref[:, span]
        twice = jnp.concatenate([factors, factors], axis=1)
        scale_one = one_ref[rows, :]
        scale_two = two_ref[rows, :]
        second = ids_ref[rows, :]
        first = heads_ref[rows, :]
        alive = (second >= 0.0).astype(F32)
        total = sum_ref[...]
        grad = jnp.zeros((width, width), F32)
        squares = []
        group = math.gcd(firsts, 4)
        for start in range(0, firsts, group):
            tops, lows = [], []
            for j in range(start, start + group):
                pick = slice(j, j + 1)
                one_top = scale_one[pick].astype(BF16).astype(F32)
                two_top = scale_two[pick].astype(BF16).astype(F32)
                is_two = column == wide(second[pick])
                is_one = column == wide(first[pick])
                tops.append(
                    jnp.where(
                        is_one, wide(one_top), jnp.where(is_two, wide(two_top), zero)
                    )
                )
                lows.append(
                    jnp.where(
                        is_one,
                        wide(scale_one[pick] - one_top),
                        jnp.where(is_two, wide(scale_two[pick] - two_top), zero),
                    )
                )
            mix = jnp.concatenate(
                [jnp.concatenate(tops, axis=1), jnp.concatenate(lows, axis=1)], axis=0
            )
            change = jnp.dot(twice, mix, preferred_element_type=F32)
            for j in range(start, start + group):
                pick = slice(j, j + 1)
                part = change[:, (j - start) * cands : (j - start + 1) * cands]
                excess = part - jnp.minimum(
                    jnp.maximum(part, low_ref[...]), high_ref[...]
                )
                if masked:
                    out = (line == second[pick]) | (line == first[pick])
                    excess = jnp.where(out, 0.0, excess)
                total = total + excess * alive[pick]
                slots_ref[slot, :, j * cands : (j + 1) * cands] = (
                    excess * (2.0 * scale_two[pick])
                ).astype(BF16)
                lead = jnp.sum(
                    excess * (2.0 * scale_one[pick]), axis=1, keepdims=True
                )
                grad = grad + jnp.where(lane_row == first[pick], lead, 0.0)
                squares.append(jnp.sum(excess * excess, axis=0, keepdims=True))
        sum_ref[...] = total
        leads_ref[slot] = grad
        squares = jnp.where(second >= 0.0, jnp.concatenate(squares, axis=0), 0.0)
        squares_ref[tile] = (squares * (1.0 / (tiles * width))).astype(BF16)

    one_tile(0, 0, True)
    send(0, 0)

    @pl.loop(1, tiles)
    def _(step):
        slot = lax.rem(step, RING)

        @pl.when(step >= RING)
        def _():
            sent(step - RING, slot)

        one_tile(step, slot, False)
        send(step, slot)

    pressure_ref[...] = jnp.sum(jnp.transpose(sum_ref[...]), axis=0, keepdims=True) * (
        2.0 / (tiles * firsts * cands)
    )
    for step in range(max(tiles - RING, 0), tiles):
        sent(step, step % RING)


def spread_kernel(
    weighted_ref, lead_ref, ids_ref, grad_ref, slots_ref, leads_ref, sems
):
    tiles, width, _ = weighted_ref.shape
    pairs, cands = ids_ref.shape
    firsts = pairs // tiles
    column = iota((width, cands), 0, F32).astype(BF16)

    def fetch(tile, slot):
        for copy in parts(
            weighted_ref.at[tile], slots_ref.at[slot], sems.at[0, slot], width
        ):
            copy.start()
        pltpu.make_async_copy(
            lead_ref.at[tile], leads_ref.at[slot], sems.at[1, slot]
        ).start()

    for tile in range(min(RING - 1, tiles)):
        fetch(tile, tile)

    @pl.loop(0, tiles)
    def _(tile):
        slot = lax.rem(tile, RING)

        @pl.when(tile + RING - 1 < tiles)
        def _():
            fetch(tile + RING - 1, lax.rem(tile + RING - 1, RING))

        rows = pl.ds(pl.multiple_of(tile * firsts, firsts), firsts)
        span = pl.ds(pl.multiple_of(tile * width, width), width)
        second = ids_ref[rows, :]
        hots = []
        for j in range(firsts):
            wide = jnp.broadcast_to(second[j : j + 1], (width, cands)).astype(BF16)
            hots.append(
                jnp.where(column == wide, jnp.ones((), BF16), jnp.zeros((), BF16))
            )
        pltpu.make_async_copy(
            weighted_ref.at[tile], slots_ref.at[slot], sems.at[0, slot]
        ).wait()
        pltpu.make_async_copy(
            lead_ref.at[tile], leads_ref.at[slot], sems.at[1, slot]
        ).wait()
        grad = leads_ref[slot] + lax.dot_general(
            slots_ref[slot],
            jnp.concatenate(hots, axis=1),
            (((1,), (1,)), ((), ())),
            preferred_element_type=F32,
        )
        grad_ref[:, span] = (grad * (1.0 / cands)).astype(BF16)


def per_device(lodf, limits, base_flow, first_ids, second_ids, counts):
    width, lines = lodf.shape
    firsts, cands = second_ids.shape
    tiles = lax.axis_size("line")
    vmem = pl.BlockSpec(memory_space=pltpu.VMEM)
    smem = pl.BlockSpec(memory_space=pltpu.SMEM)
    base = base_flow.reshape(1, width)
    packed = pl.pallas_call(
        pack_kernel,
        out_shape=jax.ShapeDtypeStruct((tiles, 4 * firsts, cands), BF16),
        in_specs=[smem, smem, vmem, vmem, vmem, vmem],
        out_specs=vmem,
        name="pack_pairs",
    )(first_ids, counts, lodf, base, limits.reshape(1, width), second_ids)
    got = lax.all_to_all(packed, "line", split_axis=0, concat_axis=0, tiled=True)
    pairs = tiles * firsts
    hbm = pl.BlockSpec(memory_space=pl.ANY)
    pair_rows = jax.ShapeDtypeStruct((pairs, cands), F32)
    slots = [
        pltpu.VMEM((RING, width, firsts * cands), BF16),
        pltpu.VMEM((RING, width, width), F32),
        pltpu.SemaphoreType.DMA((2, RING)),
    ]
    cost = pl.CostEstimate(
        flops=4 * width * width * pairs * cands,
        bytes_accessed=2 * width * pairs * cands,
        transcendentals=0,
    )
    squares, pressure, ids, weighted, lead = pl.pallas_call(
        screen_kernel,
        out_shape=(
            jax.ShapeDtypeStruct((tiles, firsts, cands), BF16),
            jax.ShapeDtypeStruct((1, width), F32),
            pair_rows,
            jax.ShapeDtypeStruct((tiles, width, firsts * cands), BF16),
            jax.ShapeDtypeStruct((tiles, width, width), F32),
        ),
        in_specs=[vmem] * 2,
        out_specs=(vmem, vmem, vmem, hbm, hbm),
        scratch_shapes=[
            pltpu.VMEM((pairs, cands), F32),
            pltpu.VMEM((pairs, cands), F32),
            pltpu.VMEM((pairs, cands), F32),
            pltpu.VMEM((width, cands), F32),
            pltpu.VMEM((width, cands), F32),
            pltpu.VMEM((width, cands), F32),
        ]
        + slots,
        compiler_params=pltpu.CompilerParams(vmem_limit_bytes=56 * 1024 * 1024),
        cost_estimate=cost,
        name="screen_lines",
    )(got, lodf)
    sums = lax.all_to_all(squares, "line", split_axis=0, concat_axis=0, tiled=True)
    grad = pl.pallas_call(
        spread_kernel,
        out_shape=jax.ShapeDtypeStruct((width, lines), BF16),
        in_specs=[hbm, hbm, vmem],
        out_specs=vmem,
        scratch_shapes=slots,
        compiler_params=pltpu.CompilerParams(vmem_limit_bytes=56 * 1024 * 1024),
        cost_estimate=cost,
        name="spread_slopes",
    )(weighted, lead, ids)
    pair_penalty = jnp.sum(sums.astype(F32), axis=0)
    return (pair_penalty, pressure.reshape(width), grad)


def solution(mesh):
    return jax.shard_map(
        per_device,
        mesh=mesh,
        in_specs=(
            P("line", None),
            P("line"),
            P(("groups", "line")),
            P(("groups", "line")),
            P(("groups", "line"), None),
            P(("groups", "line")),
        ),
        out_specs=(P(("groups", "line"), None), P(("groups", "line")), P(("groups", "line"), None)),
        check_vma=False,
    )
```

```python
import functools
import math

import jax
import jax.numpy as jnp
from jax import lax
from jax.experimental import pallas as pl
from jax.experimental.pallas import tpu as pltpu
from jax.sharding import PartitionSpec as P

F32 = jnp.float32
BF16 = jnp.bfloat16
CHUNK = 32


def iota(shape, dim, dtype=jnp.int32):
    return lax.broadcasted_iota(jnp.int32, shape, dim).astype(dtype)


def split3(x):
    top = x.astype(BF16).astype(F32)
    rest = x - top
    middle = rest.astype(BF16).astype(F32)
    return top, middle, rest - middle


def pack_kernel(
    first_ref, counts_ref, lodf_ref, base_ref, limits_ref, second_ref, out_ref, ids_ref
):
    width = lodf_ref.shape[0]
    firsts, cands = second_ref.shape
    peers = out_ref.shape[0]
    anchor = lax.axis_index("line") * width
    square = lodf_ref[:, pl.ds(pl.multiple_of(anchor, width), width)]
    row = iota((firsts, width), 0)
    lane = iota((firsts, width), 1)
    head = jnp.zeros((firsts, width), jnp.int32)
    lives = jnp.zeros((firsts, cands), jnp.int32)
    heads_row = jnp.zeros((1, width), F32)
    for j in range(firsts):
        local = first_ref[j] - anchor
        head = jnp.where(row == j, local, head)
        lives = jnp.where(iota((firsts, cands), 0) == j, counts_ref[j], lives)
        heads_row = jnp.where(iota((1, width), 1) == j, local.astype(F32), heads_row)
    hot = (lane == head).astype(BF16)
    first_row = jnp.dot(hot, square, preferred_element_type=F32)
    first_column = lax.dot_general(
        hot, square, (((1,), (1,)), ((), ())), preferred_element_type=F32
    )
    ids = jnp.where(iota((firsts, cands), 1) < lives, second_ref[...] - anchor, -1)
    ids_ref[...] = ids
    ones = jnp.ones((firsts, cands), BF16)
    line = iota((width, cands), 0)
    mult = jnp.zeros((firsts, width), F32)
    for j in range(firsts):
        named = (line == ids[j : j + 1]).astype(F32).astype(BF16)
        times = lax.dot_general(
            ones, named, (((1,), (1,)), ((), ())), preferred_element_type=F32
        )
        mult = jnp.where(row == j, times, mult)
    top, middle, low = split3(base_ref[...])
    limits = limits_ref[...].astype(F32)
    fill = jnp.zeros((firsts - 5, width), F32)
    block = jnp.concatenate(
        [first_row, first_column, mult, top, middle, low, heads_row, limits, fill],
        axis=0,
    )
    block = block.astype(BF16)
    for peer in range(peers):
        out_ref[peer] = block


def screen_kernel(
    cands,
    got_ref,
    lodf_ref,
    squares_ref,
    pressure_ref,
    grad_ref,
    low_ref,
    high_ref,
    sum_ref,
    one_ref,
    two_ref,
    mult_ref,
    lead_ref,
    heads_ref,
):
    width = lodf_ref.shape[0]
    tiles, firsts, _ = squares_ref.shape
    me = lax.axis_index("line")

    mine = got_ref[me].astype(F32)[3 * firsts :]
    base = mine[0:1] + mine[1:2] + mine[2:3]
    limit = 0.01 * mine[4:5]
    low_ref[...] = jnp.transpose(jnp.broadcast_to(-limit - base, (width, width)))
    high_ref[...] = jnp.transpose(jnp.broadcast_to(limit - base, (width, width)))
    sum_ref[...] = jnp.zeros_like(sum_ref)

    got = got_ref[...].astype(F32)
    shape = (tiles, firsts, width)
    flat = (tiles * firsts, width)
    p = got[:, :firsts].reshape(flat)
    q = got[:, firsts : 2 * firsts].reshape(flat)
    mult = got[:, 2 * firsts : 3 * firsts].reshape(flat)
    tail = got[:, 3 * firsts :]
    flows = jnp.broadcast_to(
        tail[:, 0:1] + tail[:, 1:2] + tail[:, 2:3], shape
    ).reshape(flat)
    own = iota(shape, 2) == iota(shape, 1)
    heads = jnp.sum(
        jnp.where(own, jnp.broadcast_to(tail[:, 3:4], shape), 0.0).reshape(flat),
        axis=1,
        keepdims=True,
    )
    lane = iota(flat, 1, F32)
    first_flow = jnp.sum(jnp.where(lane == heads, flows, 0.0), axis=1, keepdims=True)
    det = 1.0 - p * q
    one = (first_flow + p * flows) / det
    one_ref[...] = one
    two_ref[...] = (flows + q * first_flow) / det
    mult_ref[...] = mult
    lead_ref[...] = 2.0 * mult * one
    heads_ref[...] = jnp.broadcast_to(heads, flat).astype(jnp.int32)

    chunk = math.gcd(width, CHUNK)

    def one_tile(tile, masked):
        rows = pl.ds(pl.multiple_of(tile * firsts, firsts), firsts)
        span = pl.ds(pl.multiple_of(tile * width, width), width)
        one = one_ref[rows, :]
        two = two_ref[rows, :]
        twice = 2.0 * two
        mult = mult_ref[rows, :]
        lead = lead_ref[rows, :]
        first = heads_ref[rows, :]
        squares = [jnp.zeros((8, width), F32)] * firsts
        lane = iota((chunk, width), 1)
        for start in range(0, width, chunk):
            lines = slice(start, start + chunk)
            factors = lodf_ref[lines, span].astype(F32)
            low = low_ref[lines]
            high = high_ref[lines]
            total = sum_ref[lines]
            grad = jnp.zeros((chunk, width), F32)
            for j in range(firsts):
                pick = slice(j, j + 1)
                head = jnp.broadcast_to(first[pick], (chunk, width))
                at_head = jnp.take_along_axis(factors, head, axis=1)
                change = at_head * one[pick] + factors * two[pick]
                excess = change - jnp.minimum(jnp.maximum(change, low), high)
                if masked:
                    line = iota((chunk, width), 0) + start
                    excess = jnp.where((line == lane) | (line == head), 0.0, excess)
                squares[j] = squares[j] + jnp.sum(
                    (excess * excess).reshape(chunk // 8, 8, width), axis=0
                )
                total = total + excess * mult[pick]
                weighted = (excess * twice[pick]).astype(BF16).astype(F32)
                grad = grad + weighted * mult[pick]
                first_part = jnp.sum(excess * lead[pick], axis=1, keepdims=True)
                grad = grad + jnp.where(lane == head, first_part, 0.0)
            sum_ref[lines] = total
            grad_ref[lines, span] = (grad * (1.0 / cands)).astype(BF16)
        squares_ref[tile] = (
            jnp.concatenate(
                [jnp.sum(part, axis=0, keepdims=True) for part in squares], axis=0
            )
            * (1.0 / (tiles * width))
        ).astype(BF16)

    one_tile(me, True)

    @pl.loop(1, tiles)
    def _(step):
        tile = me + step
        one_tile(jnp.where(tile >= tiles, tile - tiles, tile), False)

    pressure_ref[...] = jnp.sum(jnp.transpose(sum_ref[...]), axis=0, keepdims=True) * (
        2.0 / (tiles * firsts * cands)
    )


def penalty_kernel(sums_ref, ids_ref, out_ref):
    sums = jnp.sum(sums_ref[...].astype(F32), axis=0)
    ids = ids_ref[...]
    found = jnp.take_along_axis(sums, jnp.maximum(ids, 0), axis=1)
    out_ref[...] = jnp.where(ids >= 0, found, 0.0)


def per_device(lodf, limits, base_flow, first_ids, second_ids, counts):
    width, lines = lodf.shape
    firsts, cands = second_ids.shape
    tiles = lax.axis_size("line")
    vmem = pl.BlockSpec(memory_space=pltpu.VMEM)
    smem = pl.BlockSpec(memory_space=pltpu.SMEM)
    base = base_flow.reshape(1, width)
    packed, ids = pl.pallas_call(
        pack_kernel,
        out_shape=(
            jax.ShapeDtypeStruct((tiles, 4 * firsts, width), BF16),
            jax.ShapeDtypeStruct((firsts, cands), jnp.int32),
        ),
        in_specs=[smem, smem, vmem, vmem, vmem, vmem],
        out_specs=(vmem, vmem),
        name="pack_pairs",
    )(first_ids, counts, lodf, base, limits.reshape(1, width), second_ids)
    got = lax.all_to_all(packed, "line", split_axis=0, concat_axis=0, tiled=True)
    pairs = tiles * firsts
    squares, pressure, grad = pl.pallas_call(
        functools.partial(screen_kernel, cands),
        out_shape=(
            jax.ShapeDtypeStruct((tiles, firsts, width), BF16),
            jax.ShapeDtypeStruct((1, width), F32),
            jax.ShapeDtypeStruct((width, lines), BF16),
        ),
        in_specs=[vmem] * 2,
        out_specs=(vmem,) * 3,
        scratch_shapes=[pltpu.VMEM((width, width), F32)] * 3
        + [pltpu.VMEM((pairs, width), F32)] * 4
        + [pltpu.VMEM((pairs, width), jnp.int32)],
        compiler_params=pltpu.CompilerParams(vmem_limit_bytes=32 * 1024 * 1024),
        name="screen_lines",
    )(got, lodf)
    sums = lax.all_to_all(squares, "line", split_axis=0, concat_axis=0, tiled=True)
    pair_penalty = pl.pallas_call(
        penalty_kernel,
        out_shape=jax.ShapeDtypeStruct((firsts, cands), F32),
        in_specs=[vmem, vmem],
        out_specs=vmem,
        compiler_params=pltpu.CompilerParams(vmem_limit_bytes=16 * 1024 * 1024),
        name="look_up",
    )(sums, ids)
    return (pair_penalty, pressure.reshape(width), grad)


def solution(mesh):
    return jax.shard_map(
        per_device,
        mesh=mesh,
        in_specs=(
            P("line", None),
            P("line"),
            P(("groups", "line")),
            P(("groups", "line")),
            P(("groups", "line"), None),
            P(("groups", "line")),
        ),
        out_specs=(P(("groups", "line"), None), P(("groups", "line")), P(("groups", "line"), None)),
        check_vma=False,
    )
```

```python
import functools
import math

import jax
import jax.numpy as jnp
from jax import lax
from jax.experimental import pallas as pl
from jax.experimental.pallas import tpu as pltpu
from jax.sharding import PartitionSpec as P

F32 = jnp.float32
BF16 = jnp.bfloat16
CHUNK = 32


def iota(shape, dim, dtype=jnp.int32):
    return lax.broadcasted_iota(jnp.int32, shape, dim).astype(dtype)


def split3(x):
    top = x.astype(BF16).astype(F32)
    rest = x - top
    middle = rest.astype(BF16).astype(F32)
    return top, middle, rest - middle


def pack_kernel(
    first_ref, counts_ref, lodf_ref, base_ref, limits_ref, second_ref, out_ref, ids_ref
):
    width = lodf_ref.shape[0]
    firsts, cands = second_ref.shape
    peers = out_ref.shape[0]
    anchor = lax.axis_index("line") * width
    square = lodf_ref[:, pl.ds(pl.multiple_of(anchor, width), width)]
    row = iota((firsts, width), 0)
    lane = iota((firsts, width), 1)
    head = jnp.zeros((firsts, width), jnp.int32)
    lives = jnp.zeros((firsts, cands), jnp.int32)
    heads_row = jnp.zeros((1, width), F32)
    for j in range(firsts):
        local = first_ref[j] - anchor
        head = jnp.where(row == j, local, head)
        lives = jnp.where(iota((firsts, cands), 0) == j, counts_ref[j], lives)
        heads_row = jnp.where(iota((1, width), 1) == j, local.astype(F32), heads_row)
    hot = (lane == head).astype(BF16)
    first_row = jnp.dot(hot, square, preferred_element_type=F32)
    first_column = lax.dot_general(
        hot, square, (((1,), (1,)), ((), ())), preferred_element_type=F32
    )
    ids = jnp.where(iota((firsts, cands), 1) < lives, second_ref[...] - anchor, -1)
    ids_ref[...] = ids
    ones = jnp.ones((firsts, cands), BF16)
    line = iota((width, cands), 0)
    mult = jnp.zeros((firsts, width), F32)
    for j in range(firsts):
        named = (line == ids[j : j + 1]).astype(F32).astype(BF16)
        times = lax.dot_general(
            ones, named, (((1,), (1,)), ((), ())), preferred_element_type=F32
        )
        mult = jnp.where(row == j, times, mult)
    top, middle, low = split3(base_ref[...])
    limits = limits_ref[...].astype(F32)
    fill = jnp.zeros((firsts - 5, width), F32)
    block = jnp.concatenate(
        [first_row, first_column, mult, top, middle, low, heads_row, limits, fill],
        axis=0,
    )
    block = block.astype(BF16)
    for peer in range(peers):
        out_ref[peer] = block


def screen_kernel(
    cands,
    got_ref,
    lodf_ref,
    squares_ref,
    pressure_ref,
    grad_ref,
    low_ref,
    high_ref,
    sum_ref,
    two_ref,
    mult_ref,
    lead_ref,
    heads_ref,
    at_head_ref,
    mix_ref,
    even_ref,
    odd_ref,
):
    width = lodf_ref.shape[0]
    tiles, firsts, _ = squares_ref.shape
    me = lax.axis_index("line")

    mine = got_ref[me].astype(F32)[3 * firsts :]
    base = mine[0:1] + mine[1:2] + mine[2:3]
    limit = 0.01 * mine[4:5]
    low_ref[...] = jnp.transpose(jnp.broadcast_to(-limit - base, (width, width)))
    high_ref[...] = jnp.transpose(jnp.broadcast_to(limit - base, (width, width)))
    sum_ref[...] = jnp.zeros_like(sum_ref)

    got = got_ref[...].astype(F32)
    shape = (tiles, firsts, width)
    flat = (tiles * firsts, width)
    p = got[:, :firsts].reshape(flat)
    q = got[:, firsts : 2 * firsts].reshape(flat)
    mult = got[:, 2 * firsts : 3 * firsts].reshape(flat)
    tail = got[:, 3 * firsts :]
    flows = jnp.broadcast_to(
        tail[:, 0:1] + tail[:, 1:2] + tail[:, 2:3], shape
    ).reshape(flat)
    own = iota(shape, 2) == iota(shape, 1)
    heads = jnp.sum(
        jnp.where(own, jnp.broadcast_to(tail[:, 3:4], shape), 0.0).reshape(flat),
        axis=1,
        keepdims=True,
    )
    lane = iota(flat, 1, F32)
    first_flow = jnp.sum(jnp.where(lane == heads, flows, 0.0), axis=1, keepdims=True)
    det = 1.0 - p * q
    one = (first_flow + p * flows) / det
    two_ref[...] = (flows + q * first_flow) / det
    mult_ref[...] = mult
    lead_ref[...] = 2.0 * mult * one
    heads_ref[...] = jnp.broadcast_to(heads, flat)

    pairs = tiles * firsts
    top = one.astype(BF16).astype(F32)
    slot = lax.rem(iota(flat, 0), firsts)
    for j in range(firsts):
        span = slice(j * width, (j + 1) * width)
        mix_ref[:pairs, span] = jnp.where(slot == j, top, 0.0).astype(BF16)
        mix_ref[pairs:, span] = jnp.where(slot == j, one - top, 0.0).astype(BF16)

    line_of = jnp.broadcast_to(heads, flat) + width * lax.div(
        iota(flat, 0), firsts
    ).astype(F32)
    line_row = jnp.transpose(line_of)[0:1]
    block = 4 * width
    at_head_ref[...] = jnp.zeros_like(at_head_ref)

    @pl.loop(0, tiles // 4)
    def _(step):
        start = pl.multiple_of(step * block, block)
        line = (iota((block, pairs), 0) + start).astype(F32)
        hot = (line == line_row).astype(F32).astype(BF16)
        at_head_ref[...] += jnp.dot(
            lodf_ref[:, pl.ds(start, block)], hot, preferred_element_type=F32
        )

    chunk = math.gcd(width, CHUNK)

    def tile_of(step):
        tile = me + step
        return jnp.where(tile >= tiles, tile - tiles, tile)

    def first_terms(step, out_ref):
        place = iota((width, pairs), 1) - tile_of(step) * firsts
        part = jnp.where((place >= 0) & (place < firsts), at_head_ref[...], 0.0)
        part = part.astype(BF16)
        out_ref[...] = jnp.dot(
            jnp.concatenate([part, part], axis=1),
            mix_ref[...],
            preferred_element_type=F32,
        )

    def one_tile(step, terms_ref, masked):
        tile = tile_of(step)
        rows = pl.ds(pl.multiple_of(tile * firsts, firsts), firsts)
        span = pl.ds(pl.multiple_of(tile * width, width), width)
        two = two_ref[rows, :]
        twice = 2.0 * two
        mult = mult_ref[rows, :]
        lead = lead_ref[rows, :]
        first = heads_ref[rows, :]
        squares = [jnp.zeros((8, width), F32)] * firsts
        lane = iota((chunk, width), 1, F32)
        for start in range(0, width, chunk):
            lines = slice(start, start + chunk)
            factors = lodf_ref[lines, span].astype(F32)
            low = low_ref[lines]
            high = high_ref[lines]
            total = sum_ref[lines]
            grad = jnp.zeros((chunk, width), F32)
            for j in range(firsts):
                pick = slice(j, j + 1)
                head = jnp.broadcast_to(first[pick], (chunk, width))
                change = (
                    terms_ref[lines, j * width : (j + 1) * width]
                    + factors * two[pick]
                )
                excess = change - jnp.minimum(jnp.maximum(change, low), high)
                if masked:
                    line = (iota((chunk, width), 0) + start).astype(F32)
                    excess = jnp.where((line == lane) | (line == head), 0.0, excess)
                squares[j] = squares[j] + jnp.sum(
                    (excess * excess).reshape(chunk // 8, 8, width), axis=0
                )
                total = total + excess * mult[pick]
                weighted = (excess * twice[pick]).astype(BF16).astype(F32)
                grad = grad + weighted * mult[pick]
                first_part = jnp.sum(excess * lead[pick], axis=1, keepdims=True)
                grad = grad + jnp.where(lane == head, first_part, 0.0)
            sum_ref[lines] = total
            grad_ref[lines, span] = (grad * (1.0 / cands)).astype(BF16)
        squares_ref[tile] = (
            jnp.concatenate(
                [jnp.sum(part, axis=0, keepdims=True) for part in squares], axis=0
            )
            * (1.0 / (tiles * width))
        ).astype(BF16)

    first_terms(0, even_ref)
    first_terms(1, odd_ref)
    one_tile(0, even_ref, True)

    @pl.loop(0, tiles // 2 - 1)
    def _(turn):
        step = 2 * turn + 1
        first_terms(step + 1, even_ref)
        one_tile(step, odd_ref, False)
        first_terms(step + 2, odd_ref)
        one_tile(step + 1, even_ref, False)

    one_tile(tiles - 1, odd_ref, False)

    pressure_ref[...] = jnp.sum(jnp.transpose(sum_ref[...]), axis=0, keepdims=True) * (
        2.0 / (tiles * firsts * cands)
    )


def penalty_kernel(sums_ref, ids_ref, out_ref):
    sums = jnp.sum(sums_ref[...].astype(F32), axis=0)
    ids = ids_ref[...]
    found = jnp.take_along_axis(sums, jnp.maximum(ids, 0), axis=1)
    out_ref[...] = jnp.where(ids >= 0, found, 0.0)


def per_device(lodf, limits, base_flow, first_ids, second_ids, counts):
    width, lines = lodf.shape
    firsts, cands = second_ids.shape
    tiles = lax.axis_size("line")
    vmem = pl.BlockSpec(memory_space=pltpu.VMEM)
    smem = pl.BlockSpec(memory_space=pltpu.SMEM)
    base = base_flow.reshape(1, width)
    packed, ids = pl.pallas_call(
        pack_kernel,
        out_shape=(
            jax.ShapeDtypeStruct((tiles, 4 * firsts, width), BF16),
            jax.ShapeDtypeStruct((firsts, cands), jnp.int32),
        ),
        in_specs=[smem, smem, vmem, vmem, vmem, vmem],
        out_specs=(vmem, vmem),
        name="pack_pairs",
    )(first_ids, counts, lodf, base, limits.reshape(1, width), second_ids)
    got = lax.all_to_all(packed, "line", split_axis=0, concat_axis=0, tiled=True)
    pairs = tiles * firsts
    squares, pressure, grad = pl.pallas_call(
        functools.partial(screen_kernel, cands),
        out_shape=(
            jax.ShapeDtypeStruct((tiles, firsts, width), BF16),
            jax.ShapeDtypeStruct((1, width), F32),
            jax.ShapeDtypeStruct((width, lines), BF16),
        ),
        in_specs=[vmem] * 2,
        out_specs=(vmem,) * 3,
        scratch_shapes=[pltpu.VMEM((width, width), F32)] * 3
        + [pltpu.VMEM((pairs, width), F32)] * 4
        + [
            pltpu.VMEM((width, pairs), F32),
            pltpu.VMEM((2 * pairs, firsts * width), BF16),
            pltpu.VMEM((width, firsts * width), F32),
            pltpu.VMEM((width, firsts * width), F32),
        ],
        compiler_params=pltpu.CompilerParams(vmem_limit_bytes=32 * 1024 * 1024),
        name="screen_lines",
    )(got, lodf)
    sums = lax.all_to_all(squares, "line", split_axis=0, concat_axis=0, tiled=True)
    pair_penalty = pl.pallas_call(
        penalty_kernel,
        out_shape=jax.ShapeDtypeStruct((firsts, cands), F32),
        in_specs=[vmem, vmem],
        out_specs=vmem,
        compiler_params=pltpu.CompilerParams(vmem_limit_bytes=16 * 1024 * 1024),
        name="look_up",
    )(sums, ids)
    return (pair_penalty, pressure.reshape(width), grad)


def solution(mesh):
    return jax.shard_map(
        per_device,
        mesh=mesh,
        in_specs=(
            P("line", None),
            P("line"),
            P(("groups", "line")),
            P(("groups", "line")),
            P(("groups", "line"), None),
            P(("groups", "line")),
        ),
        out_specs=(P(("groups", "line"), None), P(("groups", "line")), P(("groups", "line"), None)),
        check_vma=False,
    )
```

```python
import functools
import math

import jax
import jax.numpy as jnp
from jax import lax
from jax.experimental import pallas as pl
from jax.experimental.pallas import tpu as pltpu
from jax.sharding import PartitionSpec as P

F32 = jnp.float32
BF16 = jnp.bfloat16
CHUNK = 32


def iota(shape, dim, dtype=jnp.int32):
    return lax.broadcasted_iota(jnp.int32, shape, dim).astype(dtype)


def split3(x):
    top = x.astype(BF16).astype(F32)
    rest = x - top
    middle = rest.astype(BF16).astype(F32)
    return top, middle, rest - middle


def pack_kernel(
    first_ref,
    counts_ref,
    lodf_ref,
    base_ref,
    limits_ref,
    second_ref,
    out_ref,
    ids_ref,
    square_ref,
    sem,
):
    width = lodf_ref.shape[0]
    firsts, cands = second_ref.shape
    peers = out_ref.shape[0]
    anchor = lax.axis_index("line") * width
    fetch = pltpu.make_async_copy(
        lodf_ref.at[:, pl.ds(pl.multiple_of(anchor, width), width)], square_ref, sem
    )
    fetch.start()
    row = iota((firsts, width), 0)
    lane = iota((firsts, width), 1)
    head = jnp.zeros((firsts, width), jnp.int32)
    lives = jnp.zeros((firsts, cands), jnp.int32)
    heads_row = jnp.zeros((1, width), F32)
    for j in range(firsts):
        local = first_ref[j] - anchor
        head = jnp.where(row == j, local, head)
        lives = jnp.where(iota((firsts, cands), 0) == j, counts_ref[j], lives)
        heads_row = jnp.where(iota((1, width), 1) == j, local.astype(F32), heads_row)
    hot = (lane == head).astype(BF16)
    ids = jnp.where(iota((firsts, cands), 1) < lives, second_ref[...] - anchor, -1)
    ids_ref[...] = ids
    ones = jnp.ones((firsts, cands), BF16)
    line = iota((width, cands), 0)
    mult = jnp.zeros((firsts, width), F32)
    for j in range(firsts):
        named = (line == ids[j : j + 1]).astype(F32).astype(BF16)
        times = lax.dot_general(
            ones, named, (((1,), (1,)), ((), ())), preferred_element_type=F32
        )
        mult = jnp.where(row == j, times, mult)
    fetch.wait()
    square = square_ref[...]
    first_row = jnp.dot(hot, square, preferred_element_type=F32)
    first_column = lax.dot_general(
        hot, square, (((1,), (1,)), ((), ())), preferred_element_type=F32
    )
    top, middle, low = split3(base_ref[...])
    limits = limits_ref[...].astype(F32)
    fill = jnp.zeros((firsts - 5, width), F32)
    block = jnp.concatenate(
        [first_row, first_column, mult, top, middle, low, heads_row, limits, fill],
        axis=0,
    )
    block = block.astype(BF16)
    for peer in range(peers):
        out_ref[peer] = block


def screen_kernel(
    cands,
    got_ref,
    lodf_ref,
    squares_ref,
    pressure_ref,
    grad_ref,
    low_ref,
    high_ref,
    sum_ref,
    two_ref,
    mult_ref,
    lead_ref,
    heads_ref,
    at_head_ref,
    mix_ref,
    even_ref,
    odd_ref,
):
    width = lodf_ref.shape[0]
    tiles, firsts, _ = squares_ref.shape
    me = lax.axis_index("line")

    mine = got_ref[me].astype(F32)[3 * firsts :]
    base = mine[0:1] + mine[1:2] + mine[2:3]
    limit = 0.01 * mine[4:5]
    low_ref[...] = jnp.transpose(jnp.broadcast_to(-limit - base, (width, width)))
    high_ref[...] = jnp.transpose(jnp.broadcast_to(limit - base, (width, width)))
    sum_ref[...] = jnp.zeros_like(sum_ref)

    got = got_ref[...].astype(F32)
    shape = (tiles, firsts, width)
    flat = (tiles * firsts, width)
    p = got[:, :firsts].reshape(flat)
    q = got[:, firsts : 2 * firsts].reshape(flat)
    mult = got[:, 2 * firsts : 3 * firsts].reshape(flat)
    tail = got[:, 3 * firsts :]
    flows = jnp.broadcast_to(
        tail[:, 0:1] + tail[:, 1:2] + tail[:, 2:3], shape
    ).reshape(flat)
    own = iota(shape, 2) == iota(shape, 1)
    heads = jnp.sum(
        jnp.where(own, jnp.broadcast_to(tail[:, 3:4], shape), 0.0).reshape(flat),
        axis=1,
        keepdims=True,
    )
    lane = iota(flat, 1, F32)
    first_flow = jnp.sum(jnp.where(lane == heads, flows, 0.0), axis=1, keepdims=True)
    det = 1.0 - p * q
    one = (first_flow + p * flows) / det
    two = (flows + q * first_flow) / det
    deep = (tiles * firsts, 8, width)

    def replicate(rows):
        return jnp.broadcast_to(rows[:, None, :], deep)

    two_ref[...] = replicate(two)
    mult_ref[...] = replicate(mult)
    lead_ref[...] = replicate(2.0 * mult * one)
    heads_ref[...] = replicate(jnp.broadcast_to(heads, flat))

    pairs = tiles * firsts
    top = one.astype(BF16).astype(F32)
    slot = lax.rem(iota(flat, 0), firsts)
    for j in range(firsts):
        span = slice(j * width, (j + 1) * width)
        mix_ref[:pairs, span] = jnp.where(slot == j, top, 0.0).astype(BF16)
        mix_ref[pairs:, span] = jnp.where(slot == j, one - top, 0.0).astype(BF16)

    line_of = jnp.broadcast_to(heads, flat) + width * lax.div(
        iota(flat, 0), firsts
    ).astype(F32)
    line_row = jnp.transpose(line_of)[0:1]
    block = 4 * width
    at_head_ref[...] = jnp.zeros_like(at_head_ref)

    @pl.loop(0, tiles // 4)
    def _(step):
        start = pl.multiple_of(step * block, block)
        line = (iota((block, pairs), 0) + start).astype(F32)
        hot = (line == line_row).astype(F32).astype(BF16)
        at_head_ref[...] += jnp.dot(
            lodf_ref[:, pl.ds(start, block)], hot, preferred_element_type=F32
        )

    chunk = math.gcd(width, CHUNK)

    def tile_of(step):
        tile = me + step
        return jnp.where(tile >= tiles, tile - tiles, tile)

    def first_terms(step, out_ref):
        place = iota((width, pairs), 1) - tile_of(step) * firsts
        part = jnp.where((place >= 0) & (place < firsts), at_head_ref[...], 0.0)
        part = part.astype(BF16)
        out_ref[...] = jnp.dot(
            jnp.concatenate([part, part], axis=1),
            mix_ref[...],
            preferred_element_type=F32,
        )

    def one_tile(step, terms_ref, masked):
        tile = tile_of(step)
        span = pl.ds(pl.multiple_of(tile * width, width), width)
        squares = [jnp.zeros((8, width), F32)] * firsts
        lane = iota((8, width), 1, F32)
        shape = (chunk // 8, 8, width)
        for start in range(0, width, chunk):
            lines = slice(start, start + chunk)
            factors = lodf_ref[lines, span].astype(F32).reshape(shape)
            low = low_ref[lines].reshape(shape)
            high = high_ref[lines].reshape(shape)
            total = sum_ref[lines].reshape(shape)
            grad = jnp.zeros(shape, F32)
            for j in range(firsts):
                row = tile * firsts + j
                two = two_ref[row]
                mult = mult_ref[row]
                head = heads_ref[row]
                terms = terms_ref[lines, j * width : (j + 1) * width].reshape(shape)
                change = terms + factors * two
                excess = change - jnp.minimum(jnp.maximum(change, low), high)
                if masked:
                    line = (iota(shape, 0) * 8 + iota(shape, 1) + start).astype(F32)
                    excess = jnp.where((line == lane) | (line == head), 0.0, excess)
                squares[j] = squares[j] + jnp.sum(excess * excess, axis=0)
                total = total + excess * mult
                weighted = (excess * (2.0 * two)).astype(BF16).astype(F32)
                grad = grad + weighted * mult
                first_part = jnp.sum(excess * lead_ref[row], axis=2, keepdims=True)
                grad = grad + jnp.where(lane == head, first_part, 0.0)
            sum_ref[lines] = total.reshape(chunk, width)
            grad_ref[lines, span] = (
                (grad * (1.0 / cands)).reshape(chunk, width).astype(BF16)
            )
        squares_ref[tile] = (
            jnp.concatenate(
                [jnp.sum(part, axis=0, keepdims=True) for part in squares], axis=0
            )
            * (1.0 / (tiles * width))
        ).astype(BF16)

    first_terms(0, even_ref)
    first_terms(1, odd_ref)
    one_tile(0, even_ref, True)

    @pl.loop(0, tiles // 2 - 1)
    def _(turn):
        step = 2 * turn + 1
        first_terms(step + 1, even_ref)
        one_tile(step, odd_ref, False)
        first_terms(step + 2, odd_ref)
        one_tile(step + 1, even_ref, False)

    one_tile(tiles - 1, odd_ref, False)

    pressure_ref[...] = jnp.sum(jnp.transpose(sum_ref[...]), axis=0, keepdims=True) * (
        2.0 / (tiles * firsts * cands)
    )


def penalty_kernel(sums_ref, ids_ref, out_ref):
    sums = jnp.sum(sums_ref[...].astype(F32), axis=0)
    ids = ids_ref[...]
    found = jnp.take_along_axis(sums, jnp.maximum(ids, 0), axis=1)
    out_ref[...] = jnp.where(ids >= 0, found, 0.0)


def per_device(lodf, limits, base_flow, first_ids, second_ids, counts):
    width, lines = lodf.shape
    firsts, cands = second_ids.shape
    tiles = lax.axis_size("line")
    vmem = pl.BlockSpec(memory_space=pltpu.VMEM)
    smem = pl.BlockSpec(memory_space=pltpu.SMEM)
    base = base_flow.reshape(1, width)
    packed, ids = pl.pallas_call(
        pack_kernel,
        out_shape=(
            jax.ShapeDtypeStruct((tiles, 4 * firsts, width), BF16),
            jax.ShapeDtypeStruct((firsts, cands), jnp.int32),
        ),
        in_specs=[smem, smem, pl.BlockSpec(memory_space=pl.ANY), vmem, vmem, vmem],
        out_specs=(vmem, vmem),
        scratch_shapes=[pltpu.VMEM((width, width), BF16), pltpu.SemaphoreType.DMA],
        name="pack_pairs",
    )(first_ids, counts, lodf, base, limits.reshape(1, width), second_ids)
    got = lax.all_to_all(packed, "line", split_axis=0, concat_axis=0, tiled=True)
    pairs = tiles * firsts
    squares, pressure, grad = pl.pallas_call(
        functools.partial(screen_kernel, cands),
        out_shape=(
            jax.ShapeDtypeStruct((tiles, firsts, width), BF16),
            jax.ShapeDtypeStruct((1, width), F32),
            jax.ShapeDtypeStruct((width, lines), BF16),
        ),
        in_specs=[vmem] * 2,
        out_specs=(vmem,) * 3,
        scratch_shapes=[pltpu.VMEM((width, width), F32)] * 3
        + [pltpu.VMEM((pairs, 8, width), F32)] * 4
        + [
            pltpu.VMEM((width, pairs), F32),
            pltpu.VMEM((2 * pairs, firsts * width), BF16),
            pltpu.VMEM((width, firsts * width), F32),
            pltpu.VMEM((width, firsts * width), F32),
        ],
        compiler_params=pltpu.CompilerParams(vmem_limit_bytes=32 * 1024 * 1024),
        name="screen_lines",
    )(got, lodf)
    sums = lax.all_to_all(squares, "line", split_axis=0, concat_axis=0, tiled=True)
    pair_penalty = pl.pallas_call(
        penalty_kernel,
        out_shape=jax.ShapeDtypeStruct((firsts, cands), F32),
        in_specs=[vmem, vmem],
        out_specs=vmem,
        compiler_params=pltpu.CompilerParams(vmem_limit_bytes=16 * 1024 * 1024),
        name="look_up",
    )(sums, ids)
    return (pair_penalty, pressure.reshape(width), grad)


def solution(mesh):
    return jax.shard_map(
        per_device,
        mesh=mesh,
        in_specs=(
            P("line", None),
            P("line"),
            P(("groups", "line")),
            P(("groups", "line")),
            P(("groups", "line"), None),
            P(("groups", "line")),
        ),
        out_specs=(P(("groups", "line"), None), P(("groups", "line")), P(("groups", "line"), None)),
        check_vma=False,
    )
```

```python
import functools
import math

import jax
import jax.numpy as jnp
from jax import lax
from jax.experimental import pallas as pl
from jax.experimental.pallas import tpu as pltpu
from jax.sharding import PartitionSpec as P

F32 = jnp.float32
BF16 = jnp.bfloat16
CHUNK = 32


def iota(shape, dim, dtype=jnp.int32):
    return lax.broadcasted_iota(jnp.int32, shape, dim).astype(dtype)


def split3(x):
    top = x.astype(BF16).astype(F32)
    rest = x - top
    middle = rest.astype(BF16).astype(F32)
    return top, middle, rest - middle


def pack_kernel(
    first_ref, counts_ref, lodf_ref, base_ref, limits_ref, second_ref, out_ref, ids_ref
):
    width = lodf_ref.shape[0]
    firsts, cands = second_ref.shape
    peers = out_ref.shape[0]
    anchor = lax.axis_index("line") * width
    square = lodf_ref[:, pl.ds(pl.multiple_of(anchor, width), width)]
    row = iota((firsts, width), 0)
    lane = iota((firsts, width), 1)
    head = jnp.zeros((firsts, width), jnp.int32)
    lives = jnp.zeros((firsts, cands), jnp.int32)
    heads_row = jnp.zeros((1, width), F32)
    for j in range(firsts):
        local = first_ref[j] - anchor
        head = jnp.where(row == j, local, head)
        lives = jnp.where(iota((firsts, cands), 0) == j, counts_ref[j], lives)
        heads_row = jnp.where(iota((1, width), 1) == j, local.astype(F32), heads_row)
    hot = (lane == head).astype(BF16)
    first_row = jnp.dot(hot, square, preferred_element_type=F32)
    first_column = lax.dot_general(
        hot, square, (((1,), (1,)), ((), ())), preferred_element_type=F32
    )
    ids = jnp.where(iota((firsts, cands), 1) < lives, second_ref[...] - anchor, -1)
    ids_ref[...] = ids
    ones = jnp.ones((firsts, cands), BF16)
    line = iota((width, cands), 0)
    mult = jnp.zeros((firsts, width), F32)
    for j in range(firsts):
        named = (line == ids[j : j + 1]).astype(F32).astype(BF16)
        times = lax.dot_general(
            ones, named, (((1,), (1,)), ((), ())), preferred_element_type=F32
        )
        mult = jnp.where(row == j, times, mult)
    top, middle, low = split3(base_ref[...])
    limits = limits_ref[...].astype(F32)
    fill = jnp.zeros((firsts - 5, width), F32)
    block = jnp.concatenate(
        [first_row, first_column, mult, top, middle, low, heads_row, limits, fill],
        axis=0,
    )
    block = block.astype(BF16)
    for peer in range(peers):
        out_ref[peer] = block


def screen_kernel(
    cands,
    got_ref,
    lodf_ref,
    squares_ref,
    pressure_ref,
    grad_ref,
    low_ref,
    high_ref,
    sum_ref,
    two_ref,
    mult_ref,
    lead_ref,
    heads_ref,
    at_head_ref,
    mix_ref,
    even_ref,
    odd_ref,
):
    width = lodf_ref.shape[0]
    tiles, firsts, _ = squares_ref.shape
    me = lax.axis_index("line")

    mine = got_ref[me].astype(F32)[3 * firsts :]
    base = mine[0:1] + mine[1:2] + mine[2:3]
    limit = 0.01 * mine[4:5]
    low_ref[...] = jnp.transpose(jnp.broadcast_to(-limit - base, (width, width)))
    high_ref[...] = jnp.transpose(jnp.broadcast_to(limit - base, (width, width)))
    sum_ref[...] = jnp.zeros_like(sum_ref)

    got = got_ref[...].astype(F32)
    shape = (tiles, firsts, width)
    flat = (tiles * firsts, width)
    p = got[:, :firsts].reshape(flat)
    q = got[:, firsts : 2 * firsts].reshape(flat)
    mult = got[:, 2 * firsts : 3 * firsts].reshape(flat)
    tail = got[:, 3 * firsts :]
    flows = jnp.broadcast_to(
        tail[:, 0:1] + tail[:, 1:2] + tail[:, 2:3], shape
    ).reshape(flat)
    own = iota(shape, 2) == iota(shape, 1)
    heads = jnp.sum(
        jnp.where(own, jnp.broadcast_to(tail[:, 3:4], shape), 0.0).reshape(flat),
        axis=1,
        keepdims=True,
    )
    lane = iota(flat, 1, F32)
    first_flow = jnp.sum(jnp.where(lane == heads, flows, 0.0), axis=1, keepdims=True)
    det = 1.0 - p * q
    one = (first_flow + p * flows) / det
    two_ref[...] = (flows + q * first_flow) / det
    mult_ref[...] = mult
    lead_ref[...] = 2.0 * mult * one
    heads_ref[...] = jnp.broadcast_to(heads, flat)

    pairs = tiles * firsts
    top = one.astype(BF16).astype(F32)
    slot = lax.rem(iota(flat, 0), firsts)
    for j in range(firsts):
        span = slice(j * width, (j + 1) * width)
        mix_ref[:pairs, span] = jnp.where(slot == j, top, 0.0).astype(BF16)
        mix_ref[pairs:, span] = jnp.where(slot == j, one - top, 0.0).astype(BF16)

    line_of = jnp.broadcast_to(heads, flat) + width * lax.div(
        iota(flat, 0), firsts
    ).astype(F32)
    line_row = jnp.transpose(line_of)[0:1]
    block = 4 * width
    at_head_ref[...] = jnp.zeros_like(at_head_ref)

    @pl.loop(0, tiles // 4)
    def _(step):
        start = pl.multiple_of(step * block, block)
        line = (iota((block, pairs), 0) + start).astype(F32)
        hot = (line == line_row).astype(F32).astype(BF16)
        at_head_ref[...] += jnp.dot(
            lodf_ref[:, pl.ds(start, block)], hot, preferred_element_type=F32
        )

    chunk = math.gcd(width, CHUNK)

    def tile_of(step):
        tile = me + step
        return jnp.where(tile >= tiles, tile - tiles, tile)

    def first_terms(step, out_ref):
        place = iota((width, pairs), 1) - tile_of(step) * firsts
        part = jnp.where((place >= 0) & (place < firsts), at_head_ref[...], 0.0)
        part = part.astype(BF16)
        out_ref[...] = jnp.dot(
            jnp.concatenate([part, part], axis=1),
            mix_ref[...],
            preferred_element_type=F32,
        )

    def one_tile(step, terms_ref, masked):
        tile = tile_of(step)
        rows = pl.ds(pl.multiple_of(tile * firsts, firsts), firsts)
        span = pl.ds(pl.multiple_of(tile * width, width), width)
        two = two_ref[rows, :]
        mult = mult_ref[rows, :]
        spread = 2.0 * two * mult
        lead = lead_ref[rows, :]
        first = heads_ref[rows, :]
        squares = [jnp.zeros((8, width), F32)] * firsts
        lane = iota((chunk, width), 1, F32)
        for start in range(0, width, chunk):
            lines = slice(start, start + chunk)
            factors = lodf_ref[lines, span].astype(F32)
            low = low_ref[lines]
            high = high_ref[lines]
            total = sum_ref[lines]
            grad = jnp.zeros((chunk, width), F32)
            for j in range(firsts):
                pick = slice(j, j + 1)
                head = jnp.broadcast_to(first[pick], (chunk, width))
                change = (
                    terms_ref[lines, j * width : (j + 1) * width]
                    + factors * two[pick]
                )
                excess = change - jnp.minimum(jnp.maximum(change, low), high)
                if masked:
                    line = (iota((chunk, width), 0) + start).astype(F32)
                    excess = jnp.where((line == lane) | (line == head), 0.0, excess)
                squares[j] = squares[j] + jnp.sum(
                    (excess * excess).reshape(chunk // 8, 8, width), axis=0
                )
                total = total + excess * mult[pick]
                grad = grad + excess * spread[pick]
                first_part = jnp.sum(excess * lead[pick], axis=1, keepdims=True)
                grad = grad + jnp.where(lane == head, first_part, 0.0)
            sum_ref[lines] = total
            grad_ref[lines, span] = (grad * (1.0 / cands)).astype(BF16)
        squares_ref[tile] = (
            jnp.concatenate(
                [jnp.sum(part, axis=0, keepdims=True) for part in squares], axis=0
            )
            * (1.0 / (tiles * width))
        ).astype(BF16)

    first_terms(0, even_ref)
    first_terms(1, odd_ref)
    one_tile(0, even_ref, True)

    @pl.loop(0, tiles // 2 - 1)
    def _(turn):
        step = 2 * turn + 1
        first_terms(step + 1, even_ref)
        one_tile(step, odd_ref, False)
        first_terms(step + 2, odd_ref)
        one_tile(step + 1, even_ref, False)

    one_tile(tiles - 1, odd_ref, False)

    pressure_ref[...] = jnp.sum(jnp.transpose(sum_ref[...]), axis=0, keepdims=True) * (
        2.0 / (tiles * firsts * cands)
    )


def penalty_kernel(sums_ref, ids_ref, out_ref):
    sums = jnp.sum(sums_ref[...].astype(F32), axis=0)
    ids = ids_ref[...]
    found = jnp.take_along_axis(sums, jnp.maximum(ids, 0), axis=1)
    out_ref[...] = jnp.where(ids >= 0, found, 0.0)


def per_device(lodf, limits, base_flow, first_ids, second_ids, counts):
    width, lines = lodf.shape
    firsts, cands = second_ids.shape
    tiles = lax.axis_size("line")
    vmem = pl.BlockSpec(memory_space=pltpu.VMEM)
    smem = pl.BlockSpec(memory_space=pltpu.SMEM)
    base = base_flow.reshape(1, width)
    packed, ids = pl.pallas_call(
        pack_kernel,
        out_shape=(
            jax.ShapeDtypeStruct((tiles, 4 * firsts, width), BF16),
            jax.ShapeDtypeStruct((firsts, cands), jnp.int32),
        ),
        in_specs=[smem, smem, vmem, vmem, vmem, vmem],
        out_specs=(vmem, vmem),
        name="pack_pairs",
    )(first_ids, counts, lodf, base, limits.reshape(1, width), second_ids)
    got = lax.all_to_all(packed, "line", split_axis=0, concat_axis=0, tiled=True)
    pairs = tiles * firsts
    squares, pressure, grad = pl.pallas_call(
        functools.partial(screen_kernel, cands),
        out_shape=(
            jax.ShapeDtypeStruct((tiles, firsts, width), BF16),
            jax.ShapeDtypeStruct((1, width), F32),
            jax.ShapeDtypeStruct((width, lines), BF16),
        ),
        in_specs=[vmem] * 2,
        out_specs=(vmem,) * 3,
        scratch_shapes=[pltpu.VMEM((width, width), F32)] * 3
        + [pltpu.VMEM((pairs, width), F32)] * 4
        + [
            pltpu.VMEM((width, pairs), F32),
            pltpu.VMEM((2 * pairs, firsts * width), BF16),
            pltpu.VMEM((width, firsts * width), F32),
            pltpu.VMEM((width, firsts * width), F32),
        ],
        compiler_params=pltpu.CompilerParams(vmem_limit_bytes=32 * 1024 * 1024),
        name="screen_lines",
    )(got, lodf)
    sums = lax.all_to_all(squares, "line", split_axis=0, concat_axis=0, tiled=True)
    pair_penalty = pl.pallas_call(
        penalty_kernel,
        out_shape=jax.ShapeDtypeStruct((firsts, cands), F32),
        in_specs=[vmem, vmem],
        out_specs=vmem,
        compiler_params=pltpu.CompilerParams(vmem_limit_bytes=16 * 1024 * 1024),
        name="look_up",
    )(sums, ids)
    return (pair_penalty, pressure.reshape(width), grad)


def solution(mesh):
    return jax.shard_map(
        per_device,
        mesh=mesh,
        in_specs=(
            P("line", None),
            P("line"),
            P(("groups", "line")),
            P(("groups", "line")),
            P(("groups", "line"), None),
            P(("groups", "line")),
        ),
        out_specs=(P(("groups", "line"), None), P(("groups", "line")), P(("groups", "line"), None)),
        check_vma=False,
    )
```

```python
import functools
import math

import jax
import jax.numpy as jnp
from jax import lax
from jax.experimental import pallas as pl
from jax.experimental.pallas import tpu as pltpu
from jax.sharding import PartitionSpec as P

F32 = jnp.float32
BF16 = jnp.bfloat16
CHUNK = 32


def iota(shape, dim, dtype=jnp.int32):
    return lax.broadcasted_iota(jnp.int32, shape, dim).astype(dtype)


def split3(x):
    top = x.astype(BF16).astype(F32)
    rest = x - top
    middle = rest.astype(BF16).astype(F32)
    return top, middle, rest - middle


def pack_kernel(
    first_ref,
    counts_ref,
    lodf_ref,
    base_hbm,
    limits_hbm,
    second_hbm,
    out_ref,
    ids_ref,
    square_ref,
    base_ref,
    limits_ref,
    second_ref,
    block_ref,
    in_sems,
    out_sems,
):
    width = lodf_ref.shape[0]
    firsts, cands = second_ref.shape
    peers = out_ref.shape[0]
    anchor = lax.axis_index("line") * width
    span = pl.ds(pl.multiple_of(anchor, width), width)
    fetches = [
        pltpu.make_async_copy(source, target, in_sems.at[place])
        for place, (source, target) in enumerate(
            (
                (second_hbm, second_ref),
                (lodf_ref.at[:, span], square_ref),
                (base_hbm, base_ref),
                (limits_hbm, limits_ref),
            )
        )
    ]
    for fetch in fetches:
        fetch.start()
    row = iota((firsts, width), 0)
    lane = iota((firsts, width), 1)
    head = jnp.zeros((firsts, width), jnp.int32)
    lives = jnp.zeros((firsts, cands), jnp.int32)
    heads_row = jnp.zeros((1, width), F32)
    for j in range(firsts):
        local = first_ref[j] - anchor
        head = jnp.where(row == j, local, head)
        lives = jnp.where(iota((firsts, cands), 0) == j, counts_ref[j], lives)
        heads_row = jnp.where(iota((1, width), 1) == j, local.astype(F32), heads_row)
    hot = (lane == head).astype(BF16)
    for fetch in fetches:
        fetch.wait()
    square = square_ref[...]
    first_row = jnp.dot(hot, square, preferred_element_type=F32)
    first_column = lax.dot_general(
        hot, square, (((1,), (1,)), ((), ())), preferred_element_type=F32
    )
    ids = jnp.where(iota((firsts, cands), 1) < lives, second_ref[...] - anchor, -1)
    ids_ref[...] = ids
    ones = jnp.ones((firsts, cands), BF16)
    line = iota((width, cands), 0)
    mult = jnp.zeros((firsts, width), F32)
    for j in range(firsts):
        named = (line == ids[j : j + 1]).astype(F32).astype(BF16)
        times = lax.dot_general(
            ones, named, (((1,), (1,)), ((), ())), preferred_element_type=F32
        )
        mult = jnp.where(row == j, times, mult)
    top, middle, low = split3(base_ref[...])
    limits = limits_ref[...].astype(F32)
    fill = jnp.zeros((firsts - 5, width), F32)
    block = jnp.concatenate(
        [first_row, first_column, mult, top, middle, low, heads_row, limits, fill],
        axis=0,
    )
    block_ref[...] = block.astype(BF16)
    sends = [
        pltpu.make_async_copy(block_ref, out_ref.at[peer], out_sems.at[peer])
        for peer in range(peers)
    ]
    for send in sends:
        send.start()
    for send in sends:
        send.wait()


def screen_kernel(
    cands,
    got_ref,
    lodf_ref,
    squares_ref,
    pressure_ref,
    grad_hbm,
    low_ref,
    high_ref,
    sum_ref,
    two_ref,
    mult_ref,
    lead_ref,
    heads_ref,
    at_head_ref,
    mix_ref,
    even_ref,
    odd_ref,
    grad_ref,
    grad_sem,
):
    width = lodf_ref.shape[0]
    tiles, firsts, _ = squares_ref.shape
    me = lax.axis_index("line")

    mine = got_ref[me].astype(F32)[3 * firsts :]
    base = mine[0:1] + mine[1:2] + mine[2:3]
    limit = 0.01 * mine[4:5]
    low_ref[...] = jnp.transpose(jnp.broadcast_to(-limit - base, (width, width)))
    high_ref[...] = jnp.transpose(jnp.broadcast_to(limit - base, (width, width)))
    sum_ref[...] = jnp.zeros_like(sum_ref)

    got = got_ref[...].astype(F32)
    shape = (tiles, firsts, width)
    flat = (tiles * firsts, width)
    p = got[:, :firsts].reshape(flat)
    q = got[:, firsts : 2 * firsts].reshape(flat)
    mult = got[:, 2 * firsts : 3 * firsts].reshape(flat)
    tail = got[:, 3 * firsts :]
    flows = jnp.broadcast_to(
        tail[:, 0:1] + tail[:, 1:2] + tail[:, 2:3], shape
    ).reshape(flat)
    own = iota(shape, 2) == iota(shape, 1)
    heads = jnp.sum(
        jnp.where(own, jnp.broadcast_to(tail[:, 3:4], shape), 0.0).reshape(flat),
        axis=1,
        keepdims=True,
    )
    lane = iota(flat, 1, F32)
    first_flow = jnp.sum(jnp.where(lane == heads, flows, 0.0), axis=1, keepdims=True)
    det = 1.0 - p * q
    one = (first_flow + p * flows) / det
    two_ref[...] = (flows + q * first_flow) / det
    mult_ref[...] = mult
    lead_ref[...] = 2.0 * mult * one
    heads_ref[...] = jnp.broadcast_to(heads, flat)

    pairs = tiles * firsts
    top = one.astype(BF16).astype(F32)
    slot = lax.rem(iota(flat, 0), firsts)
    for j in range(firsts):
        span = slice(j * width, (j + 1) * width)
        mix_ref[:pairs, span] = jnp.where(slot == j, top, 0.0).astype(BF16)
        mix_ref[pairs:, span] = jnp.where(slot == j, one - top, 0.0).astype(BF16)

    line_of = jnp.broadcast_to(heads, flat) + width * lax.div(
        iota(flat, 0), firsts
    ).astype(F32)
    line_row = jnp.transpose(line_of)[0:1]
    block = 4 * width
    at_head_ref[...] = jnp.zeros_like(at_head_ref)

    @pl.loop(0, tiles // 4, unroll=4)
    def _(step):
        start = pl.multiple_of(step * block, block)
        line = (iota((block, pairs), 0) + start).astype(F32)
        hot = (line == line_row).astype(F32).astype(BF16)
        at_head_ref[...] += jnp.dot(
            lodf_ref[:, pl.ds(start, block)], hot, preferred_element_type=F32
        )

    chunk = math.gcd(width, CHUNK)

    def tile_of(step):
        tile = me + step
        return jnp.where(tile >= tiles, tile - tiles, tile)

    def first_terms(step, out_ref):
        place = iota((width, pairs), 1) - tile_of(step) * firsts
        part = jnp.where((place >= 0) & (place < firsts), at_head_ref[...], 0.0)
        part = part.astype(BF16)
        out_ref[...] = jnp.dot(
            jnp.concatenate([part, part], axis=1),
            mix_ref[...],
            preferred_element_type=F32,
        )

    def one_tile(step, terms_ref, masked):
        tile = tile_of(step)
        rows = pl.ds(pl.multiple_of(tile * firsts, firsts), firsts)
        span = pl.ds(pl.multiple_of(tile * width, width), width)
        two = two_ref[rows, :]
        twice = 2.0 * two
        mult = mult_ref[rows, :]
        lead = lead_ref[rows, :]
        first = heads_ref[rows, :]
        squares = [jnp.zeros((8, width), F32)] * firsts
        lane = iota((chunk, width), 1, F32)
        for start in range(0, width, chunk):
            lines = slice(start, start + chunk)
            factors = lodf_ref[lines, span].astype(F32)
            low = low_ref[lines]
            high = high_ref[lines]
            total = sum_ref[lines]
            grad = jnp.zeros((chunk, width), F32)
            for j in range(firsts):
                pick = slice(j, j + 1)
                head = jnp.broadcast_to(first[pick], (chunk, width))
                change = (
                    terms_ref[lines, j * width : (j + 1) * width]
                    + factors * two[pick]
                )
                excess = change - jnp.minimum(jnp.maximum(change, low), high)
                if masked:
                    line = (iota((chunk, width), 0) + start).astype(F32)
                    excess = jnp.where((line == lane) | (line == head), 0.0, excess)
                squares[j] = squares[j] + jnp.sum(
                    (excess * excess).reshape(chunk // 8, 8, width), axis=0
                )
                total = total + excess * mult[pick]
                weighted = (excess * twice[pick]).astype(BF16).astype(F32)
                grad = grad + weighted * mult[pick]
                first_part = jnp.sum(excess * lead[pick], axis=1, keepdims=True)
                grad = grad + jnp.where(lane == head, first_part, 0.0)
            sum_ref[lines] = total
            grad_ref[lines, span] = (grad * (1.0 / cands)).astype(BF16)
        pltpu.make_async_copy(
            grad_ref.at[:, span], grad_hbm.at[:, span], grad_sem
        ).start()
        squares_ref[tile] = (
            jnp.concatenate(
                [jnp.sum(part, axis=0, keepdims=True) for part in squares], axis=0
            )
            * (1.0 / (tiles * width))
        ).astype(BF16)

    first_terms(0, even_ref)
    first_terms(1, odd_ref)
    one_tile(0, even_ref, True)

    @pl.loop(0, tiles // 2 - 1)
    def _(turn):
        step = 2 * turn + 1
        first_terms(step + 1, even_ref)
        one_tile(step, odd_ref, False)
        first_terms(step + 2, odd_ref)
        one_tile(step + 1, even_ref, False)

    one_tile(tiles - 1, odd_ref, False)

    pltpu.make_async_copy(grad_ref, grad_hbm, grad_sem).wait()
    pressure_ref[...] = jnp.sum(jnp.transpose(sum_ref[...]), axis=0, keepdims=True) * (
        2.0 / (tiles * firsts * cands)
    )


def penalty_kernel(sums_ref, ids_ref, out_ref):
    sums = jnp.sum(sums_ref[...].astype(F32), axis=0)
    ids = ids_ref[...]
    found = jnp.take_along_axis(sums, jnp.maximum(ids, 0), axis=1)
    out_ref[...] = jnp.where(ids >= 0, found, 0.0)


def per_device(lodf, limits, base_flow, first_ids, second_ids, counts):
    width, lines = lodf.shape
    firsts, cands = second_ids.shape
    tiles = lax.axis_size("line")
    vmem = pl.BlockSpec(memory_space=pltpu.VMEM)
    smem = pl.BlockSpec(memory_space=pltpu.SMEM)
    hbm = pl.BlockSpec(memory_space=pl.ANY)
    base = base_flow.reshape(1, width)
    packed, ids = pl.pallas_call(
        pack_kernel,
        out_shape=(
            jax.ShapeDtypeStruct((tiles, 4 * firsts, width), BF16),
            jax.ShapeDtypeStruct((firsts, cands), jnp.int32),
        ),
        in_specs=[smem, smem] + [hbm] * 4,
        out_specs=(hbm, vmem),
        scratch_shapes=[
            pltpu.VMEM((width, width), BF16),
            pltpu.VMEM((1, width), F32),
            pltpu.VMEM((1, width), jnp.int32),
            pltpu.VMEM((firsts, cands), jnp.int32),
            pltpu.VMEM((4 * firsts, width), BF16),
            pltpu.SemaphoreType.DMA((4,)),
            pltpu.SemaphoreType.DMA((tiles,)),
        ],
        name="pack_pairs",
    )(first_ids, counts, lodf, base, limits.reshape(1, width), second_ids)
    got = lax.all_to_all(packed, "line", split_axis=0, concat_axis=0, tiled=True)
    pairs = tiles * firsts
    squares, pressure, grad = pl.pallas_call(
        functools.partial(screen_kernel, cands),
        out_shape=(
            jax.ShapeDtypeStruct((tiles, firsts, width), BF16),
            jax.ShapeDtypeStruct((1, width), F32),
            jax.ShapeDtypeStruct((width, lines), BF16),
        ),
        in_specs=[vmem] * 2,
        out_specs=(vmem, vmem, hbm),
        scratch_shapes=[pltpu.VMEM((width, width), F32)] * 3
        + [pltpu.VMEM((pairs, width), F32)] * 4
        + [
            pltpu.VMEM((width, pairs), F32),
            pltpu.VMEM((2 * pairs, firsts * width), BF16),
            pltpu.VMEM((width, firsts * width), F32),
            pltpu.VMEM((width, firsts * width), F32),
            pltpu.VMEM((width, lines), BF16),
            pltpu.SemaphoreType.DMA,
        ],
        compiler_params=pltpu.CompilerParams(vmem_limit_bytes=32 * 1024 * 1024),
        name="screen_lines",
    )(got, lodf)
    sums = lax.all_to_all(squares, "line", split_axis=0, concat_axis=0, tiled=True)
    pair_penalty = pl.pallas_call(
        penalty_kernel,
        out_shape=jax.ShapeDtypeStruct((firsts, cands), F32),
        in_specs=[vmem, vmem],
        out_specs=vmem,
        compiler_params=pltpu.CompilerParams(vmem_limit_bytes=16 * 1024 * 1024),
        name="look_up",
    )(sums, ids)
    return (pair_penalty, pressure.reshape(width), grad)


def solution(mesh):
    return jax.shard_map(
        per_device,
        mesh=mesh,
        in_specs=(
            P("line", None),
            P("line"),
            P(("groups", "line")),
            P(("groups", "line")),
            P(("groups", "line"), None),
            P(("groups", "line")),
        ),
        out_specs=(P(("groups", "line"), None), P(("groups", "line")), P(("groups", "line"), None)),
        check_vma=False,
    )
```

```python
import functools
import math

import jax
import jax.numpy as jnp
from jax import lax
from jax.experimental import pallas as pl
from jax.experimental.pallas import tpu as pltpu
from jax.sharding import PartitionSpec as P

F32 = jnp.float32
BF16 = jnp.bfloat16
CHUNK = 32


def iota(shape, dim, dtype=jnp.int32):
    return lax.broadcasted_iota(jnp.int32, shape, dim).astype(dtype)


def split3(x):
    top = x.astype(BF16).astype(F32)
    rest = x - top
    middle = rest.astype(BF16).astype(F32)
    return top, middle, rest - middle


def pack_kernel(
    first_ref, counts_ref, lodf_ref, base_ref, limits_ref, second_ref, out_ref, ids_ref
):
    width = lodf_ref.shape[0]
    firsts, cands = second_ref.shape
    peers = out_ref.shape[0]
    anchor = lax.axis_index("line") * width
    square = lodf_ref[:, pl.ds(pl.multiple_of(anchor, width), width)]
    row = iota((firsts, width), 0)
    lane = iota((firsts, width), 1)
    head = jnp.zeros((firsts, width), jnp.int32)
    lives = jnp.zeros((firsts, cands), jnp.int32)
    heads_row = jnp.zeros((1, width), F32)
    for j in range(firsts):
        local = first_ref[j] - anchor
        head = jnp.where(row == j, local, head)
        lives = jnp.where(iota((firsts, cands), 0) == j, counts_ref[j], lives)
        heads_row = jnp.where(iota((1, width), 1) == j, local.astype(F32), heads_row)
    hot = (lane == head).astype(BF16)
    first_row = jnp.dot(hot, square, preferred_element_type=F32)
    first_column = lax.dot_general(
        hot, square, (((1,), (1,)), ((), ())), preferred_element_type=F32
    )
    ids = jnp.where(iota((firsts, cands), 1) < lives, second_ref[...] - anchor, -1)
    ids_ref[...] = ids
    ones = jnp.ones((firsts, cands), BF16)
    line = iota((width, cands), 0)
    mult = jnp.zeros((firsts, width), F32)
    for j in range(firsts):
        named = (line == ids[j : j + 1]).astype(F32).astype(BF16)
        times = lax.dot_general(
            ones, named, (((1,), (1,)), ((), ())), preferred_element_type=F32
        )
        mult = jnp.where(row == j, times, mult)
    top, middle, low = split3(base_ref[...])
    limits = limits_ref[...].astype(F32)
    fill = jnp.zeros((firsts - 5, width), F32)
    block = jnp.concatenate(
        [first_row, first_column, mult, top, middle, low, heads_row, limits, fill],
        axis=0,
    )
    block = block.astype(BF16)
    for peer in range(peers):
        out_ref[peer] = block


def screen_kernel(
    cands,
    got_ref,
    lodf_ref,
    squares_ref,
    pressure_ref,
    grad_hbm,
    low_ref,
    high_ref,
    sum_ref,
    two_ref,
    mult_ref,
    lead_ref,
    heads_ref,
    at_head_ref,
    mix_ref,
    even_ref,
    odd_ref,
    grad_ref,
    grad_sem,
):
    width = lodf_ref.shape[0]
    tiles, firsts, _ = squares_ref.shape
    me = lax.axis_index("line")

    mine = got_ref[me].astype(F32)[3 * firsts :]
    base = mine[0:1] + mine[1:2] + mine[2:3]
    limit = 0.01 * mine[4:5]
    low_ref[...] = jnp.transpose(jnp.broadcast_to(-limit - base, (width, width)))
    high_ref[...] = jnp.transpose(jnp.broadcast_to(limit - base, (width, width)))
    sum_ref[...] = jnp.zeros_like(sum_ref)

    got = got_ref[...].astype(F32)
    shape = (tiles, firsts, width)
    flat = (tiles * firsts, width)
    p = got[:, :firsts].reshape(flat)
    q = got[:, firsts : 2 * firsts].reshape(flat)
    mult = got[:, 2 * firsts : 3 * firsts].reshape(flat)
    tail = got[:, 3 * firsts :]
    flows = jnp.broadcast_to(
        tail[:, 0:1] + tail[:, 1:2] + tail[:, 2:3], shape
    ).reshape(flat)
    own = iota(shape, 2) == iota(shape, 1)
    heads = jnp.sum(
        jnp.where(own, jnp.broadcast_to(tail[:, 3:4], shape), 0.0).reshape(flat),
        axis=1,
        keepdims=True,
    )
    lane = iota(flat, 1, F32)
    first_flow = jnp.sum(jnp.where(lane == heads, flows, 0.0), axis=1, keepdims=True)
    det = 1.0 - p * q
    one = (first_flow + p * flows) / det
    two_ref[...] = (flows + q * first_flow) / det
    mult_ref[...] = mult
    lead_ref[...] = 2.0 * mult * one
    heads_ref[...] = jnp.broadcast_to(heads, flat)

    pairs = tiles * firsts
    top = one.astype(BF16).astype(F32)
    slot = lax.rem(iota(flat, 0), firsts)
    for j in range(firsts):
        span = slice(j * width, (j + 1) * width)
        mix_ref[:pairs, span] = jnp.where(slot == j, top, 0.0).astype(BF16)
        mix_ref[pairs:, span] = jnp.where(slot == j, one - top, 0.0).astype(BF16)

    line_of = jnp.broadcast_to(heads, flat) + width * lax.div(
        iota(flat, 0), firsts
    ).astype(F32)
    line_row = jnp.transpose(line_of)[0:1]
    block = 4 * width
    at_head_ref[...] = jnp.zeros_like(at_head_ref)

    @pl.loop(0, tiles // 4, unroll=4)
    def _(step):
        start = pl.multiple_of(step * block, block)
        line = (iota((block, pairs), 0) + start).astype(F32)
        hot = (line == line_row).astype(F32).astype(BF16)
        at_head_ref[...] += jnp.dot(
            lodf_ref[:, pl.ds(start, block)], hot, preferred_element_type=F32
        )

    chunk = math.gcd(width, CHUNK)

    def tile_of(step):
        tile = me + step
        return jnp.where(tile >= tiles, tile - tiles, tile)

    def first_terms(step, out_ref):
        place = iota((width, pairs), 1) - tile_of(step) * firsts
        part = jnp.where((place >= 0) & (place < firsts), at_head_ref[...], 0.0)
        part = part.astype(BF16)
        out_ref[...] = jnp.dot(
            jnp.concatenate([part, part], axis=1),
            mix_ref[...],
            preferred_element_type=F32,
        )

    def one_tile(step, terms_ref, masked):
        tile = tile_of(step)
        rows = pl.ds(pl.multiple_of(tile * firsts, firsts), firsts)
        span = pl.ds(pl.multiple_of(tile * width, width), width)
        two = two_ref[rows, :]
        twice = 2.0 * two
        mult = mult_ref[rows, :]
        lead = lead_ref[rows, :]
        first = heads_ref[rows, :]
        squares = [jnp.zeros((8, width), F32)] * firsts
        lane = iota((chunk, width), 1, F32)
        for start in range(0, width, chunk):
            lines = slice(start, start + chunk)
            factors = lodf_ref[lines, span].astype(F32)
            low = low_ref[lines]
            high = high_ref[lines]
            total = sum_ref[lines]
            grad = jnp.zeros((chunk, width), F32)
            for j in range(firsts):
                pick = slice(j, j + 1)
                head = jnp.broadcast_to(first[pick], (chunk, width))
                change = (
                    terms_ref[lines, j * width : (j + 1) * width]
                    + factors * two[pick]
                )
                excess = change - jnp.minimum(jnp.maximum(change, low), high)
                if masked:
                    line = (iota((chunk, width), 0) + start).astype(F32)
                    excess = jnp.where((line == lane) | (line == head), 0.0, excess)
                squares[j] = squares[j] + jnp.sum(
                    (excess * excess).reshape(chunk // 8, 8, width), axis=0
                )
                total = total + excess * mult[pick]
                weighted = (excess * twice[pick]).astype(BF16).astype(F32)
                grad = grad + weighted * mult[pick]
                first_part = jnp.sum(excess * lead[pick], axis=1, keepdims=True)
                grad = grad + jnp.where(lane == head, first_part, 0.0)
            sum_ref[lines] = total
            grad_ref[lines, span] = (grad * (1.0 / cands)).astype(BF16)
        pltpu.make_async_copy(
            grad_ref.at[:, span], grad_hbm.at[:, span], grad_sem
        ).start()
        squares_ref[tile] = (
            jnp.concatenate(
                [jnp.sum(part, axis=0, keepdims=True) for part in squares], axis=0
            )
            * (1.0 / (tiles * width))
        ).astype(BF16)

    first_terms(0, even_ref)
    first_terms(1, odd_ref)
    one_tile(0, even_ref, True)

    @pl.loop(0, tiles // 2 - 1)
    def _(turn):
        step = 2 * turn + 1
        first_terms(step + 1, even_ref)
        one_tile(step, odd_ref, False)
        first_terms(step + 2, odd_ref)
        one_tile(step + 1, even_ref, False)

    one_tile(tiles - 1, odd_ref, False)

    pltpu.make_async_copy(grad_ref, grad_hbm, grad_sem).wait()
    pressure_ref[...] = jnp.sum(jnp.transpose(sum_ref[...]), axis=0, keepdims=True) * (
        2.0 / (tiles * firsts * cands)
    )


def penalty_kernel(sums_ref, ids_ref, out_ref):
    sums = jnp.sum(sums_ref[...].astype(F32), axis=0)
    ids = ids_ref[...]
    found = jnp.take_along_axis(sums, jnp.maximum(ids, 0), axis=1)
    out_ref[...] = jnp.where(ids >= 0, found, 0.0)


def per_device(lodf, limits, base_flow, first_ids, second_ids, counts):
    width, lines = lodf.shape
    firsts, cands = second_ids.shape
    tiles = lax.axis_size("line")
    vmem = pl.BlockSpec(memory_space=pltpu.VMEM)
    smem = pl.BlockSpec(memory_space=pltpu.SMEM)
    hbm = pl.BlockSpec(memory_space=pl.ANY)
    base = base_flow.reshape(1, width)
    packed, ids = pl.pallas_call(
        pack_kernel,
        out_shape=(
            pltpu.VMEM((tiles, 4 * firsts, width), BF16),
            pltpu.VMEM((firsts, cands), jnp.int32),
        ),
        in_specs=[smem, smem, vmem, vmem, vmem, vmem],
        out_specs=(vmem, vmem),
        name="pack_pairs",
    )(first_ids, counts, lodf, base, limits.reshape(1, width), second_ids)
    got = lax.all_to_all(packed, "line", split_axis=0, concat_axis=0, tiled=True)
    pairs = tiles * firsts
    squares, pressure, grad = pl.pallas_call(
        functools.partial(screen_kernel, cands),
        out_shape=(
            jax.ShapeDtypeStruct((tiles, firsts, width), BF16),
            jax.ShapeDtypeStruct((1, width), F32),
            jax.ShapeDtypeStruct((width, lines), BF16),
        ),
        in_specs=[vmem] * 2,
        out_specs=(vmem, vmem, hbm),
        scratch_shapes=[pltpu.VMEM((width, width), F32)] * 3
        + [pltpu.VMEM((pairs, width), F32)] * 4
        + [
            pltpu.VMEM((width, pairs), F32),
            pltpu.VMEM((2 * pairs, firsts * width), BF16),
            pltpu.VMEM((width, firsts * width), F32),
            pltpu.VMEM((width, firsts * width), F32),
            pltpu.VMEM((width, lines), BF16),
            pltpu.SemaphoreType.DMA,
        ],
        compiler_params=pltpu.CompilerParams(vmem_limit_bytes=32 * 1024 * 1024),
        name="screen_lines",
    )(got, lodf)
    sums = lax.all_to_all(squares, "line", split_axis=0, concat_axis=0, tiled=True)
    pair_penalty = pl.pallas_call(
        penalty_kernel,
        out_shape=jax.ShapeDtypeStruct((firsts, cands), F32),
        in_specs=[vmem, vmem],
        out_specs=vmem,
        compiler_params=pltpu.CompilerParams(vmem_limit_bytes=16 * 1024 * 1024),
        name="look_up",
    )(sums, ids)
    return (pair_penalty, pressure.reshape(width), grad)


def solution(mesh):
    return jax.shard_map(
        per_device,
        mesh=mesh,
        in_specs=(
            P("line", None),
            P("line"),
            P(("groups", "line")),
            P(("groups", "line")),
            P(("groups", "line"), None),
            P(("groups", "line")),
        ),
        out_specs=(P(("groups", "line"), None), P(("groups", "line")), P(("groups", "line"), None)),
        check_vma=False,
    )
```

```python
import functools
import math

import jax
import jax.numpy as jnp
from jax import lax
from jax.experimental import pallas as pl
from jax.experimental.pallas import tpu as pltpu
from jax.sharding import PartitionSpec as P

F32 = jnp.float32
BF16 = jnp.bfloat16
CHUNK = 32


def iota(shape, dim, dtype=jnp.int32):
    return lax.broadcasted_iota(jnp.int32, shape, dim).astype(dtype)


def split3(x):
    top = x.astype(BF16).astype(F32)
    rest = x - top
    middle = rest.astype(BF16).astype(F32)
    return top, middle, rest - middle


def pack_kernel(
    first_ref, counts_ref, lodf_ref, base_ref, limits_ref, second_ref, out_ref, ids_ref
):
    width = lodf_ref.shape[0]
    firsts, cands = second_ref.shape
    peers = out_ref.shape[0]
    anchor = lax.axis_index("line") * width
    square = lodf_ref[:, pl.ds(pl.multiple_of(anchor, width), width)]
    row = iota((firsts, width), 0)
    lane = iota((firsts, width), 1)
    head = jnp.zeros((firsts, width), jnp.int32)
    lives = jnp.zeros((firsts, cands), jnp.int32)
    heads_row = jnp.zeros((1, width), F32)
    for j in range(firsts):
        local = first_ref[j] - anchor
        head = jnp.where(row == j, local, head)
        lives = jnp.where(iota((firsts, cands), 0) == j, counts_ref[j], lives)
        heads_row = jnp.where(iota((1, width), 1) == j, local.astype(F32), heads_row)
    hot = (lane == head).astype(BF16)
    first_row = jnp.dot(hot, square, preferred_element_type=F32)
    first_column = lax.dot_general(
        hot, square, (((1,), (1,)), ((), ())), preferred_element_type=F32
    )
    ids = jnp.where(iota((firsts, cands), 1) < lives, second_ref[...] - anchor, -1)
    ids_ref[...] = ids
    ones = jnp.ones((firsts, cands), BF16)
    line = iota((width, cands), 0)
    mult = jnp.zeros((firsts, width), F32)
    for j in range(firsts):
        named = (line == ids[j : j + 1]).astype(F32).astype(BF16)
        times = lax.dot_general(
            ones, named, (((1,), (1,)), ((), ())), preferred_element_type=F32
        )
        mult = jnp.where(row == j, times, mult)
    top, middle, low = split3(base_ref[...])
    limits = limits_ref[...].astype(F32)
    fill = jnp.zeros((firsts - 5, width), F32)
    block = jnp.concatenate(
        [first_row, first_column, mult, top, middle, low, heads_row, limits, fill],
        axis=0,
    )
    block = block.astype(BF16)
    for peer in range(peers):
        out_ref[peer] = block


def screen_kernel(
    cands,
    got_ref,
    lodf_ref,
    squares_ref,
    pressure_ref,
    grad_ref,
    low_ref,
    high_ref,
    sum_ref,
    two_ref,
    mult_ref,
    lead_ref,
    heads_ref,
    at_head_ref,
    mix_ref,
    even_ref,
    odd_ref,
):
    width = lodf_ref.shape[0]
    tiles, firsts, _ = squares_ref.shape
    me = lax.axis_index("line")

    mine = got_ref[me].astype(F32)[3 * firsts :]
    base = mine[0:1] + mine[1:2] + mine[2:3]
    limit = 0.01 * mine[4:5]
    low_ref[...] = jnp.transpose(jnp.broadcast_to(-limit - base, (width, width)))
    high_ref[...] = jnp.transpose(jnp.broadcast_to(limit - base, (width, width)))
    sum_ref[...] = jnp.zeros_like(sum_ref)

    got = got_ref[...].astype(F32)
    shape = (tiles, firsts, width)
    flat = (tiles * firsts, width)
    p = got[:, :firsts].reshape(flat)
    q = got[:, firsts : 2 * firsts].reshape(flat)
    mult = got[:, 2 * firsts : 3 * firsts].reshape(flat)
    tail = got[:, 3 * firsts :]
    flows = jnp.broadcast_to(
        tail[:, 0:1] + tail[:, 1:2] + tail[:, 2:3], shape
    ).reshape(flat)
    own = iota(shape, 2) == iota(shape, 1)
    heads = jnp.sum(
        jnp.where(own, jnp.broadcast_to(tail[:, 3:4], shape), 0.0).reshape(flat),
        axis=1,
        keepdims=True,
    )
    lane = iota(flat, 1, F32)
    first_flow = jnp.sum(jnp.where(lane == heads, flows, 0.0), axis=1, keepdims=True)
    det = 1.0 - p * q
    one = (first_flow + p * flows) / det
    two_ref[...] = (flows + q * first_flow) / det
    mult_ref[...] = mult
    lead_ref[...] = 2.0 * mult * one
    heads_ref[...] = jnp.broadcast_to(heads, flat)

    pairs = tiles * firsts
    top = one.astype(BF16).astype(F32)
    slot = lax.rem(iota(flat, 0), firsts)
    for j in range(firsts):
        span = slice(j * width, (j + 1) * width)
        mix_ref[:pairs, span] = jnp.where(slot == j, top, 0.0).astype(BF16)
        mix_ref[pairs:, span] = jnp.where(slot == j, one - top, 0.0).astype(BF16)

    line_of = jnp.broadcast_to(heads, flat) + width * lax.div(
        iota(flat, 0), firsts
    ).astype(F32)
    line_row = jnp.transpose(line_of)[0:1]
    block = 4 * width
    at_head_ref[...] = jnp.zeros_like(at_head_ref)

    @pl.loop(0, tiles // 4, unroll=4)
    def _(step):
        start = pl.multiple_of(step * block, block)
        line = (iota((block, pairs), 0) + start).astype(F32)
        hot = (line == line_row).astype(F32).astype(BF16)
        at_head_ref[...] += jnp.dot(
            lodf_ref[:, pl.ds(start, block)], hot, preferred_element_type=F32
        )

    chunk = math.gcd(width, CHUNK)

    def tile_of(step):
        tile = me + step
        return jnp.where(tile >= tiles, tile - tiles, tile)

    def first_terms(step, out_ref):
        place = iota((width, pairs), 1) - tile_of(step) * firsts
        part = jnp.where((place >= 0) & (place < firsts), at_head_ref[...], 0.0)
        part = part.astype(BF16)
        out_ref[...] = jnp.dot(
            jnp.concatenate([part, part], axis=1),
            mix_ref[...],
            preferred_element_type=F32,
        )

    def one_tile(step, terms_ref, masked):
        tile = tile_of(step)
        rows = pl.ds(pl.multiple_of(tile * firsts, firsts), firsts)
        span = pl.ds(pl.multiple_of(tile * width, width), width)
        two = two_ref[rows, :]
        twice = 2.0 * two
        mult = mult_ref[rows, :]
        lead = lead_ref[rows, :]
        first = heads_ref[rows, :]
        squares = [jnp.zeros((8, width), F32)] * firsts
        lane = iota((chunk, width), 1, F32)
        for start in range(0, width, chunk):
            lines = slice(start, start + chunk)
            factors = lodf_ref[lines, span].astype(F32)
            low = low_ref[lines]
            high = high_ref[lines]
            total = sum_ref[lines]
            grad = jnp.zeros((chunk, width), F32)
            for j in range(firsts):
                pick = slice(j, j + 1)
                head = jnp.broadcast_to(first[pick], (chunk, width))
                change = (
                    terms_ref[lines, j * width : (j + 1) * width]
                    + factors * two[pick]
                )
                excess = change - jnp.minimum(jnp.maximum(change, low), high)
                if masked:
                    line = (iota((chunk, width), 0) + start).astype(F32)
                    excess = jnp.where((line == lane) | (line == head), 0.0, excess)
                squares[j] = squares[j] + jnp.sum(
                    (excess * excess).reshape(chunk // 8, 8, width), axis=0
                )
                total = total + excess * mult[pick]
                weighted = (excess * twice[pick]).astype(BF16).astype(F32)
                grad = grad + weighted * mult[pick]
                first_part = jnp.sum(excess * lead[pick], axis=1, keepdims=True)
                grad = grad + jnp.where(lane == head, first_part, 0.0)
            sum_ref[lines] = total
            grad_ref[lines, span] = (grad * (1.0 / cands)).astype(BF16)
        squares_ref[tile] = (
            jnp.concatenate(
                [jnp.sum(part, axis=0, keepdims=True) for part in squares], axis=0
            )
            * (1.0 / (tiles * width))
        ).astype(BF16)

    first_terms(0, even_ref)
    first_terms(1, odd_ref)
    one_tile(0, even_ref, True)

    @pl.loop(0, tiles // 2 - 1)
    def _(turn):
        step = 2 * turn + 1
        first_terms(step + 1, even_ref)
        one_tile(step, odd_ref, False)
        first_terms(step + 2, odd_ref)
        one_tile(step + 1, even_ref, False)

    one_tile(tiles - 1, odd_ref, False)

    pressure_ref[...] = jnp.sum(jnp.transpose(sum_ref[...]), axis=0, keepdims=True) * (
        2.0 / (tiles * firsts * cands)
    )


def penalty_kernel(sums_ref, ids_ref, out_ref):
    sums = jnp.sum(sums_ref[...].astype(F32), axis=0)
    ids = ids_ref[...]
    found = jnp.take_along_axis(sums, jnp.maximum(ids, 0), axis=1)
    out_ref[...] = jnp.where(ids >= 0, found, 0.0)


def per_device(lodf, limits, base_flow, first_ids, second_ids, counts):
    width, lines = lodf.shape
    firsts, cands = second_ids.shape
    tiles = lax.axis_size("line")
    vmem = pl.BlockSpec(memory_space=pltpu.VMEM)
    smem = pl.BlockSpec(memory_space=pltpu.SMEM)
    base = base_flow.reshape(1, width)
    packed, ids = pl.pallas_call(
        pack_kernel,
        out_shape=(
            pltpu.VMEM((tiles, 4 * firsts, width), BF16),
            pltpu.VMEM((firsts, cands), jnp.int32),
        ),
        in_specs=[smem, smem, vmem, vmem, vmem, vmem],
        out_specs=(vmem, vmem),
        name="pack_pairs",
    )(first_ids, counts, lodf, base, limits.reshape(1, width), second_ids)
    got = lax.all_to_all(packed, "line", split_axis=0, concat_axis=0, tiled=True)
    pairs = tiles * firsts
    squares, pressure, grad = pl.pallas_call(
        functools.partial(screen_kernel, cands),
        out_shape=(
            pltpu.VMEM((tiles, firsts, width), BF16),
            pltpu.VMEM((1, width), F32),
            pltpu.VMEM((width, lines), BF16),
        ),
        in_specs=[vmem] * 2,
        out_specs=(vmem,) * 3,
        scratch_shapes=[pltpu.VMEM((width, width), F32)] * 3
        + [pltpu.VMEM((pairs, width), F32)] * 4
        + [
            pltpu.VMEM((width, pairs), F32),
            pltpu.VMEM((2 * pairs, firsts * width), BF16),
            pltpu.VMEM((width, firsts * width), F32),
            pltpu.VMEM((width, firsts * width), F32),
        ],
        compiler_params=pltpu.CompilerParams(vmem_limit_bytes=32 * 1024 * 1024),
        name="screen_lines",
    )(got, lodf)
    sums = lax.all_to_all(squares, "line", split_axis=0, concat_axis=0, tiled=True)
    pair_penalty = pl.pallas_call(
        penalty_kernel,
        out_shape=jax.ShapeDtypeStruct((firsts, cands), F32),
        in_specs=[vmem, vmem],
        out_specs=vmem,
        compiler_params=pltpu.CompilerParams(vmem_limit_bytes=16 * 1024 * 1024),
        name="look_up",
    )(sums, ids)
    return (pair_penalty, pressure.reshape(width), grad)


def solution(mesh):
    return jax.shard_map(
        per_device,
        mesh=mesh,
        in_specs=(
            P("line", None),
            P("line"),
            P(("groups", "line")),
            P(("groups", "line")),
            P(("groups", "line"), None),
            P(("groups", "line")),
        ),
        out_specs=(P(("groups", "line"), None), P(("groups", "line")), P(("groups", "line"), None)),
        check_vma=False,
    )
```

```python
import functools
import math

import jax
import jax.numpy as jnp
from jax import lax
from jax.experimental import pallas as pl
from jax.experimental.pallas import tpu as pltpu
from jax.sharding import PartitionSpec as P

F32 = jnp.float32
BF16 = jnp.bfloat16
CHUNK = 32


def iota(shape, dim, dtype=jnp.int32):
    return lax.broadcasted_iota(jnp.int32, shape, dim).astype(dtype)


def split3(x):
    top = x.astype(BF16).astype(F32)
    rest = x - top
    middle = rest.astype(BF16).astype(F32)
    return top, middle, rest - middle


def pack_kernel(
    first_ref, counts_ref, lodf_ref, base_ref, limits_ref, second_ref, out_ref, ids_ref
):
    width = lodf_ref.shape[0]
    firsts, cands = second_ref.shape
    peers = out_ref.shape[0]
    anchor = lax.axis_index("line") * width
    square = lodf_ref[:, pl.ds(pl.multiple_of(anchor, width), width)]
    row = iota((firsts, width), 0)
    lane = iota((firsts, width), 1)
    head = jnp.zeros((firsts, width), jnp.int32)
    lives = jnp.zeros((firsts, cands), jnp.int32)
    heads_row = jnp.zeros((1, width), F32)
    for j in range(firsts):
        local = first_ref[j] - anchor
        head = jnp.where(row == j, local, head)
        lives = jnp.where(iota((firsts, cands), 0) == j, counts_ref[j], lives)
        heads_row = jnp.where(iota((1, width), 1) == j, local.astype(F32), heads_row)
    hot = (lane == head).astype(BF16)
    first_row = jnp.dot(hot, square, preferred_element_type=F32)
    first_column = lax.dot_general(
        hot, square, (((1,), (1,)), ((), ())), preferred_element_type=F32
    )
    ids = jnp.where(iota((firsts, cands), 1) < lives, second_ref[...] - anchor, -1)
    ids_ref[...] = ids
    ones = jnp.ones((firsts, cands), BF16)
    line = iota((width, cands), 0)
    mult = jnp.zeros((firsts, width), F32)
    for j in range(firsts):
        named = (line == ids[j : j + 1]).astype(F32).astype(BF16)
        times = lax.dot_general(
            ones, named, (((1,), (1,)), ((), ())), preferred_element_type=F32
        )
        mult = jnp.where(row == j, times, mult)
    top, middle, low = split3(base_ref[...])
    limits = limits_ref[...].astype(F32)
    fill = jnp.zeros((firsts - 5, width), F32)
    block = jnp.concatenate(
        [first_row, first_column, mult, top, middle, low, heads_row, limits, fill],
        axis=0,
    )
    block = block.astype(BF16)
    for peer in range(peers):
        out_ref[peer] = block


def screen_kernel(cands, for_pairs, got_ref, lodf_ref, *refs):
    if for_pairs:
        squares_ref, kept_ref, *refs, sem = refs
        keep = pltpu.make_async_copy(got_ref, kept_ref, sem)
        keep.start()
    else:
        pressure_ref, grad_hbm, *refs, grad_ref, grad_sem, sum_ref, mult_ref, lead_ref = refs
    low_ref, high_ref, two_ref, heads_ref, at_head_ref, mix_ref, even_ref, odd_ref = refs
    tiles = got_ref.shape[0]
    width = lodf_ref.shape[0]
    firsts = got_ref.shape[1] // 4
    me = lax.axis_index("line")

    mine = got_ref[me].astype(F32)[3 * firsts :]
    base = mine[0:1] + mine[1:2] + mine[2:3]
    limit = 0.01 * mine[4:5]
    low_ref[...] = jnp.transpose(jnp.broadcast_to(-limit - base, (width, width)))
    high_ref[...] = jnp.transpose(jnp.broadcast_to(limit - base, (width, width)))

    got = got_ref[...].astype(F32)
    shape = (tiles, firsts, width)
    flat = (tiles * firsts, width)
    p = got[:, :firsts].reshape(flat)
    q = got[:, firsts : 2 * firsts].reshape(flat)
    mult = got[:, 2 * firsts : 3 * firsts].reshape(flat)
    tail = got[:, 3 * firsts :]
    flows = jnp.broadcast_to(
        tail[:, 0:1] + tail[:, 1:2] + tail[:, 2:3], shape
    ).reshape(flat)
    own = iota(shape, 2) == iota(shape, 1)
    heads = jnp.sum(
        jnp.where(own, jnp.broadcast_to(tail[:, 3:4], shape), 0.0).reshape(flat),
        axis=1,
        keepdims=True,
    )
    lane = iota(flat, 1, F32)
    first_flow = jnp.sum(jnp.where(lane == heads, flows, 0.0), axis=1, keepdims=True)
    det = 1.0 - p * q
    one = (first_flow + p * flows) / det
    two_ref[...] = (flows + q * first_flow) / det
    if not for_pairs:
        mult_ref[...] = mult
        lead_ref[...] = 2.0 * mult * one
        sum_ref[...] = jnp.zeros_like(sum_ref)
    heads_ref[...] = jnp.broadcast_to(heads, flat)

    pairs = tiles * firsts
    top = one.astype(BF16).astype(F32)
    slot = lax.rem(iota(flat, 0), firsts)
    for j in range(firsts):
        span = slice(j * width, (j + 1) * width)
        mix_ref[:pairs, span] = jnp.where(slot == j, top, 0.0).astype(BF16)
        mix_ref[pairs:, span] = jnp.where(slot == j, one - top, 0.0).astype(BF16)

    line_of = jnp.broadcast_to(heads, flat) + width * lax.div(
        iota(flat, 0), firsts
    ).astype(F32)
    line_row = jnp.transpose(line_of)[0:1]
    block = 4 * width
    at_head_ref[...] = jnp.zeros_like(at_head_ref)

    @pl.loop(0, tiles // 4, unroll=4)
    def _(step):
        start = pl.multiple_of(step * block, block)
        line = (iota((block, pairs), 0) + start).astype(F32)
        hot = (line == line_row).astype(F32).astype(BF16)
        at_head_ref[...] += jnp.dot(
            lodf_ref[:, pl.ds(start, block)], hot, preferred_element_type=F32
        )

    chunk = math.gcd(width, CHUNK)

    def tile_of(step):
        tile = me + step
        return jnp.where(tile >= tiles, tile - tiles, tile)

    def first_terms(step, out_ref):
        place = iota((width, pairs), 1) - tile_of(step) * firsts
        part = jnp.where((place >= 0) & (place < firsts), at_head_ref[...], 0.0)
        part = part.astype(BF16)
        out_ref[...] = jnp.dot(
            jnp.concatenate([part, part], axis=1),
            mix_ref[...],
            preferred_element_type=F32,
        )

    def one_tile(step, terms_ref, masked):
        tile = tile_of(step)
        rows = pl.ds(pl.multiple_of(tile * firsts, firsts), firsts)
        span = pl.ds(pl.multiple_of(tile * width, width), width)
        two = two_ref[rows, :]
        first = heads_ref[rows, :]
        if not for_pairs:
            twice = 2.0 * two
            mult = mult_ref[rows, :]
            lead = lead_ref[rows, :]
        squares = [jnp.zeros((8, width), F32)] * firsts
        lane = iota((chunk, width), 1, F32)
        for start in range(0, width, chunk):
            lines = slice(start, start + chunk)
            factors = lodf_ref[lines, span].astype(F32)
            low = low_ref[lines]
            high = high_ref[lines]
            if not for_pairs:
                total = sum_ref[lines]
                grad = jnp.zeros((chunk, width), F32)
            for j in range(firsts):
                pick = slice(j, j + 1)
                head = jnp.broadcast_to(first[pick], (chunk, width))
                change = (
                    terms_ref[lines, j * width : (j + 1) * width]
                    + factors * two[pick]
                )
                excess = change - jnp.minimum(jnp.maximum(change, low), high)
                if masked:
                    line = (iota((chunk, width), 0) + start).astype(F32)
                    excess = jnp.where((line == lane) | (line == head), 0.0, excess)
                if for_pairs:
                    squares[j] = squares[j] + jnp.sum(
                        (excess * excess).reshape(chunk // 8, 8, width), axis=0
                    )
                    continue
                total = total + excess * mult[pick]
                weighted = (excess * twice[pick]).astype(BF16).astype(F32)
                grad = grad + weighted * mult[pick]
                first_part = jnp.sum(excess * lead[pick], axis=1, keepdims=True)
                grad = grad + jnp.where(lane == head, first_part, 0.0)
            if not for_pairs:
                sum_ref[lines] = total
                grad_ref[lines, span] = (grad * (1.0 / cands)).astype(BF16)
        if for_pairs:
            squares_ref[tile] = (
                jnp.concatenate(
                    [jnp.sum(part, axis=0, keepdims=True) for part in squares], axis=0
                )
                * (1.0 / (tiles * width))
            ).astype(BF16)
        else:
            pltpu.make_async_copy(
                grad_ref.at[:, span], grad_hbm.at[:, span], grad_sem
            ).start()

    first_terms(0, even_ref)
    first_terms(1, odd_ref)
    one_tile(0, even_ref, True)

    @pl.loop(0, tiles // 2 - 1)
    def _(turn):
        step = 2 * turn + 1
        first_terms(step + 1, even_ref)
        one_tile(step, odd_ref, False)
        first_terms(step + 2, odd_ref)
        one_tile(step + 1, even_ref, False)

    one_tile(tiles - 1, odd_ref, False)

    if for_pairs:
        keep.wait()
        return
    pressure_ref[...] = jnp.sum(jnp.transpose(sum_ref[...]), axis=0, keepdims=True) * (
        2.0 / (tiles * firsts * cands)
    )
    pltpu.make_async_copy(grad_ref, grad_hbm, grad_sem).wait()


def penalty_kernel(sums_ref, ids_ref, out_ref):
    sums = jnp.sum(sums_ref[...].astype(F32), axis=0)
    ids = ids_ref[...]
    found = jnp.take_along_axis(sums, jnp.maximum(ids, 0), axis=1)
    out_ref[...] = jnp.where(ids >= 0, found, 0.0)


def per_device(lodf, limits, base_flow, first_ids, second_ids, counts):
    width, lines = lodf.shape
    firsts, cands = second_ids.shape
    tiles = lax.axis_size("line")
    vmem = pl.BlockSpec(memory_space=pltpu.VMEM)
    smem = pl.BlockSpec(memory_space=pltpu.SMEM)
    hbm = pl.BlockSpec(memory_space=pl.ANY)
    base = base_flow.reshape(1, width)
    packed, ids = pl.pallas_call(
        pack_kernel,
        out_shape=(
            pltpu.VMEM((tiles, 4 * firsts, width), BF16),
            pltpu.VMEM((firsts, cands), jnp.int32),
        ),
        in_specs=[smem, smem, vmem, vmem, vmem, vmem],
        out_specs=(vmem, vmem),
        name="pack_pairs",
    )(first_ids, counts, lodf, base, limits.reshape(1, width), second_ids)
    got = lax.all_to_all(packed, "line", split_axis=0, concat_axis=0, tiled=True)
    pairs = tiles * firsts
    scratch = [
        pltpu.VMEM((width, width), F32),
        pltpu.VMEM((width, width), F32),
        pltpu.VMEM((pairs, width), F32),
        pltpu.VMEM((pairs, width), F32),
        pltpu.VMEM((width, pairs), F32),
        pltpu.VMEM((2 * pairs, firsts * width), BF16),
        pltpu.VMEM((width, firsts * width), F32),
        pltpu.VMEM((width, firsts * width), F32),
    ]
    params = pltpu.CompilerParams(vmem_limit_bytes=32 * 1024 * 1024)
    cost = pl.CostEstimate(
        flops=16 * width * width * pairs,
        bytes_accessed=4 * width * lines,
        transcendentals=0,
    )
    squares, kept = pl.pallas_call(
        functools.partial(screen_kernel, cands, True),
        out_shape=(
            pltpu.VMEM((tiles, firsts, width), BF16),
            jax.ShapeDtypeStruct(got.shape, BF16),
        ),
        in_specs=[vmem] * 2,
        out_specs=(vmem, hbm),
        scratch_shapes=scratch + [pltpu.SemaphoreType.DMA],
        compiler_params=params,
        cost_estimate=cost,
        name="screen_pairs",
    )(got, lodf)
    sums = lax.all_to_all(squares, "line", split_axis=0, concat_axis=0, tiled=True)
    pressure, grad = pl.pallas_call(
        functools.partial(screen_kernel, cands, False),
        out_shape=(
            jax.ShapeDtypeStruct((1, width), F32),
            jax.ShapeDtypeStruct((width, lines), BF16),
        ),
        in_specs=[vmem] * 2,
        out_specs=(vmem, hbm),
        scratch_shapes=scratch
        + [
            pltpu.VMEM((width, lines), BF16),
            pltpu.SemaphoreType.DMA,
            pltpu.VMEM((width, width), F32),
            pltpu.VMEM((pairs, width), F32),
            pltpu.VMEM((pairs, width), F32),
        ],
        compiler_params=params,
        cost_estimate=cost,
        name="screen_lines",
    )(kept, lodf)
    pair_penalty = pl.pallas_call(
        penalty_kernel,
        out_shape=jax.ShapeDtypeStruct((firsts, cands), F32),
        in_specs=[vmem, vmem],
        out_specs=vmem,
        compiler_params=pltpu.CompilerParams(vmem_limit_bytes=16 * 1024 * 1024),
        name="look_up",
    )(sums, ids)
    return (pair_penalty, pressure.reshape(width), grad)


def solution(mesh):
    return jax.shard_map(
        per_device,
        mesh=mesh,
        in_specs=(
            P("line", None),
            P("line"),
            P(("groups", "line")),
            P(("groups", "line")),
            P(("groups", "line"), None),
            P(("groups", "line")),
        ),
        out_specs=(P(("groups", "line"), None), P(("groups", "line")), P(("groups", "line"), None)),
        check_vma=False,
    )
```

```python
import functools
import math

import jax
import jax.numpy as jnp
from jax import lax
from jax.experimental import pallas as pl
from jax.experimental.pallas import tpu as pltpu
from jax.sharding import PartitionSpec as P

F32 = jnp.float32
BF16 = jnp.bfloat16
CHUNK = 32


def iota(shape, dim, dtype=jnp.int32):
    return lax.broadcasted_iota(jnp.int32, shape, dim).astype(dtype)


def split3(x):
    top = x.astype(BF16).astype(F32)
    rest = x - top
    middle = rest.astype(BF16).astype(F32)
    return top, middle, rest - middle


def pack_kernel(
    first_ref, counts_ref, lodf_ref, base_ref, limits_ref, second_ref, out_ref, ids_ref
):
    width = lodf_ref.shape[0]
    firsts, cands = second_ref.shape
    peers = out_ref.shape[0]
    anchor = lax.axis_index("line") * width
    square = lodf_ref[:, pl.ds(pl.multiple_of(anchor, width), width)]
    row = iota((firsts, width), 0)
    lane = iota((firsts, width), 1)
    head = jnp.zeros((firsts, width), jnp.int32)
    lives = jnp.zeros((firsts, cands), jnp.int32)
    heads_row = jnp.zeros((1, width), F32)
    for j in range(firsts):
        local = first_ref[j] - anchor
        head = jnp.where(row == j, local, head)
        lives = jnp.where(iota((firsts, cands), 0) == j, counts_ref[j], lives)
        heads_row = jnp.where(iota((1, width), 1) == j, local.astype(F32), heads_row)
    hot = (lane == head).astype(BF16)
    first_row = jnp.dot(hot, square, preferred_element_type=F32)
    first_column = lax.dot_general(
        hot, square, (((1,), (1,)), ((), ())), preferred_element_type=F32
    )
    ids = jnp.where(iota((firsts, cands), 1) < lives, second_ref[...] - anchor, -1)
    ids_ref[...] = ids
    ones = jnp.ones((firsts, cands), BF16)
    line = iota((width, cands), 0)
    mult = jnp.zeros((firsts, width), F32)
    for j in range(firsts):
        named = (line == ids[j : j + 1]).astype(F32).astype(BF16)
        times = lax.dot_general(
            ones, named, (((1,), (1,)), ((), ())), preferred_element_type=F32
        )
        mult = jnp.where(row == j, times, mult)
    top, middle, low = split3(base_ref[...])
    limits = limits_ref[...].astype(F32)
    fill = jnp.zeros((firsts - 5, width), F32)
    block = jnp.concatenate(
        [first_row, first_column, mult, top, middle, low, heads_row, limits, fill],
        axis=0,
    )
    block = block.astype(BF16)
    for peer in range(peers):
        out_ref[peer] = block


def screen_kernel(cands, for_pairs, got_ref, lodf_ref, *refs):
    if for_pairs:
        squares_ref, kept_ref, *refs, sem = refs
        keep = pltpu.make_async_copy(got_ref, kept_ref, sem)
        keep.start()
    else:
        pressure_ref, grad_hbm, *refs, grad_ref, grad_sem, sum_ref, mult_ref, lead_ref = refs
    low_ref, high_ref, two_ref, heads_ref, at_head_ref, mix_ref, even_ref, odd_ref = refs
    tiles = got_ref.shape[0]
    width = lodf_ref.shape[0]
    firsts = got_ref.shape[1] // 4
    me = lax.axis_index("line")

    mine = got_ref[me].astype(F32)[3 * firsts :]
    base = mine[0:1] + mine[1:2] + mine[2:3]
    limit = 0.01 * mine[4:5]
    low_ref[...] = jnp.transpose(jnp.broadcast_to(-limit - base, (width, width)))
    high_ref[...] = jnp.transpose(jnp.broadcast_to(limit - base, (width, width)))

    got = got_ref[...].astype(F32)
    shape = (tiles, firsts, width)
    flat = (tiles * firsts, width)
    p = got[:, :firsts].reshape(flat)
    q = got[:, firsts : 2 * firsts].reshape(flat)
    mult = got[:, 2 * firsts : 3 * firsts].reshape(flat)
    tail = got[:, 3 * firsts :]
    flows = jnp.broadcast_to(
        tail[:, 0:1] + tail[:, 1:2] + tail[:, 2:3], shape
    ).reshape(flat)
    own = iota(shape, 2) == iota(shape, 1)
    heads = jnp.sum(
        jnp.where(own, jnp.broadcast_to(tail[:, 3:4], shape), 0.0).reshape(flat),
        axis=1,
        keepdims=True,
    )
    lane = iota(flat, 1, F32)
    first_flow = jnp.sum(jnp.where(lane == heads, flows, 0.0), axis=1, keepdims=True)
    det = 1.0 - p * q
    one = (first_flow + p * flows) / det
    two_ref[...] = (flows + q * first_flow) / det
    if not for_pairs:
        mult_ref[...] = mult
        lead_ref[...] = 2.0 * mult * one
        sum_ref[...] = jnp.zeros_like(sum_ref)
    heads_ref[...] = jnp.broadcast_to(heads, flat)

    pairs = tiles * firsts
    top = one.astype(BF16).astype(F32)
    slot = lax.rem(iota(flat, 0), firsts)
    for j in range(firsts):
        span = slice(j * width, (j + 1) * width)
        mix_ref[:pairs, span] = jnp.where(slot == j, top, 0.0).astype(BF16)
        mix_ref[pairs:, span] = jnp.where(slot == j, one - top, 0.0).astype(BF16)

    line_of = jnp.broadcast_to(heads, flat) + width * lax.div(
        iota(flat, 0), firsts
    ).astype(F32)
    line_row = jnp.transpose(line_of)[0:1]
    block = 4 * width
    at_head_ref[...] = jnp.zeros_like(at_head_ref)

    @pl.loop(0, tiles // 4, unroll=4)
    def _(step):
        start = pl.multiple_of(step * block, block)
        here = line_row - start.astype(F32)
        hot = (iota((block, pairs), 0, F32) == here).astype(F32).astype(BF16)
        at_head_ref[...] += jnp.dot(
            lodf_ref[:, pl.ds(start, block)], hot, preferred_element_type=F32
        )

    chunk = math.gcd(width, 2 * CHUNK if for_pairs else CHUNK)

    def tile_of(step):
        tile = me + step
        return jnp.where(tile >= tiles, tile - tiles, tile)

    def first_terms(couple, out_ref):
        parts = []
        for step in (2 * couple, 2 * couple + 1):
            place = iota((width, pairs), 1) - tile_of(step) * firsts
            part = jnp.where((place >= 0) & (place < firsts), at_head_ref[...], 0.0)
            parts.append(part.astype(BF16))
        part = jnp.concatenate(parts, axis=0)
        out_ref[...] = jnp.dot(
            jnp.concatenate([part, part], axis=1),
            mix_ref[...],
            preferred_element_type=F32,
        )

    def two_tiles(couple, terms_ref, masked):
        one_tile(2 * couple, terms_ref, 0, masked)
        one_tile(2 * couple + 1, terms_ref, width, False)

    def one_tile(step, terms_ref, offset, masked):
        tile = tile_of(step)
        rows = pl.ds(pl.multiple_of(tile * firsts, firsts), firsts)
        span = pl.ds(pl.multiple_of(tile * width, width), width)
        two = two_ref[rows, :]
        first = heads_ref[rows, :]
        if not for_pairs:
            twice = 2.0 * two
            mult = mult_ref[rows, :]
            lead = lead_ref[rows, :]
        squares = [jnp.zeros((8, width), F32)] * firsts
        lane = iota((chunk, width), 1, F32)
        for start in range(0, width, chunk):
            lines = slice(start, start + chunk)
            factors = lodf_ref[lines, span].astype(F32)
            low = low_ref[lines]
            high = high_ref[lines]
            if not for_pairs:
                total = sum_ref[lines]
                grad = jnp.zeros((chunk, width), F32)
            for j in range(firsts):
                pick = slice(j, j + 1)
                head = jnp.broadcast_to(first[pick], (chunk, width))
                change = (
                    terms_ref[
                        offset + start : offset + start + chunk,
                        j * width : (j + 1) * width,
                    ]
                    + factors * two[pick]
                )
                excess = change - jnp.minimum(jnp.maximum(change, low), high)
                if masked:
                    line = (iota((chunk, width), 0) + start).astype(F32)
                    excess = jnp.where((line == lane) | (line == head), 0.0, excess)
                if for_pairs:
                    squares[j] = squares[j] + jnp.sum(
                        (excess * excess).reshape(chunk // 8, 8, width), axis=0
                    )
                    continue
                total = total + excess * mult[pick]
                weighted = (excess * twice[pick]).astype(BF16).astype(F32)
                grad = grad + weighted * mult[pick]
                first_part = jnp.sum(excess * lead[pick], axis=1, keepdims=True)
                grad = grad + jnp.where(lane == head, first_part, 0.0)
            if not for_pairs:
                sum_ref[lines] = total
                grad_ref[lines, span] = (grad * (1.0 / cands)).astype(BF16)
        if for_pairs:
            squares_ref[tile] = (
                jnp.concatenate(
                    [jnp.sum(part, axis=0, keepdims=True) for part in squares], axis=0
                )
                * (1.0 / (tiles * width))
            ).astype(BF16)
        else:
            pltpu.make_async_copy(
                grad_ref.at[:, span], grad_hbm.at[:, span], grad_sem
            ).start()

    first_terms(0, even_ref)
    first_terms(1, odd_ref)
    two_tiles(0, even_ref, True)

    @pl.loop(0, tiles // 4 - 1)
    def _(turn):
        couple = 2 * turn + 1
        first_terms(couple + 1, even_ref)
        two_tiles(couple, odd_ref, False)
        first_terms(couple + 2, odd_ref)
        two_tiles(couple + 1, even_ref, False)

    two_tiles(tiles // 2 - 1, odd_ref, False)

    if for_pairs:
        keep.wait()
        return
    pressure_ref[...] = jnp.sum(jnp.transpose(sum_ref[...]), axis=0, keepdims=True) * (
        2.0 / (tiles * firsts * cands)
    )
    pltpu.make_async_copy(grad_ref, grad_hbm, grad_sem).wait()


def penalty_kernel(sums_ref, ids_ref, out_ref):
    sums = jnp.sum(sums_ref[...].astype(F32), axis=0)
    ids = ids_ref[...]
    found = jnp.take_along_axis(sums, jnp.maximum(ids, 0), axis=1)
    out_ref[...] = jnp.where(ids >= 0, found, 0.0)


def per_device(lodf, limits, base_flow, first_ids, second_ids, counts):
    width, lines = lodf.shape
    firsts, cands = second_ids.shape
    tiles = lax.axis_size("line")
    vmem = pl.BlockSpec(memory_space=pltpu.VMEM)
    smem = pl.BlockSpec(memory_space=pltpu.SMEM)
    hbm = pl.BlockSpec(memory_space=pl.ANY)
    base = base_flow.reshape(1, width)
    packed, ids = pl.pallas_call(
        pack_kernel,
        out_shape=(
            pltpu.VMEM((tiles, 4 * firsts, width), BF16),
            pltpu.VMEM((firsts, cands), jnp.int32),
        ),
        in_specs=[smem, smem, vmem, vmem, vmem, vmem],
        out_specs=(vmem, vmem),
        name="pack_pairs",
    )(first_ids, counts, lodf, base, limits.reshape(1, width), second_ids)
    got = lax.all_to_all(packed, "line", split_axis=0, concat_axis=0, tiled=True)
    pairs = tiles * firsts
    scratch = [
        pltpu.VMEM((width, width), F32),
        pltpu.VMEM((width, width), F32),
        pltpu.VMEM((pairs, width), F32),
        pltpu.VMEM((pairs, width), F32),
        pltpu.VMEM((width, pairs), F32),
        pltpu.VMEM((2 * pairs, firsts * width), BF16),
        pltpu.VMEM((2 * width, firsts * width), F32),
        pltpu.VMEM((2 * width, firsts * width), F32),
    ]
    params = pltpu.CompilerParams(vmem_limit_bytes=32 * 1024 * 1024)
    cost = pl.CostEstimate(
        flops=16 * width * width * pairs,
        bytes_accessed=4 * width * lines,
        transcendentals=0,
    )
    squares, kept = pl.pallas_call(
        functools.partial(screen_kernel, cands, True),
        out_shape=(
            pltpu.VMEM((tiles, firsts, width), BF16),
            jax.ShapeDtypeStruct(got.shape, BF16),
        ),
        in_specs=[vmem] * 2,
        out_specs=(vmem, hbm),
        scratch_shapes=scratch + [pltpu.SemaphoreType.DMA],
        compiler_params=params,
        cost_estimate=cost,
        name="screen_pairs",
    )(got, lodf)
    sums = lax.all_to_all(squares, "line", split_axis=0, concat_axis=0, tiled=True)
    pressure, grad = pl.pallas_call(
        functools.partial(screen_kernel, cands, False),
        out_shape=(
            jax.ShapeDtypeStruct((1, width), F32),
            jax.ShapeDtypeStruct((width, lines), BF16),
        ),
        in_specs=[vmem] * 2,
        out_specs=(vmem, hbm),
        scratch_shapes=scratch
        + [
            pltpu.VMEM((width, lines), BF16),
            pltpu.SemaphoreType.DMA,
            pltpu.VMEM((width, width), F32),
            pltpu.VMEM((pairs, width), F32),
            pltpu.VMEM((pairs, width), F32),
        ],
        compiler_params=params,
        cost_estimate=cost,
        name="screen_lines",
    )(kept, lodf)
    pair_penalty = pl.pallas_call(
        penalty_kernel,
        out_shape=jax.ShapeDtypeStruct((firsts, cands), F32),
        in_specs=[vmem, vmem],
        out_specs=vmem,
        compiler_params=pltpu.CompilerParams(vmem_limit_bytes=16 * 1024 * 1024),
        name="look_up",
    )(sums, ids)
    return (pair_penalty, pressure.reshape(width), grad)


def solution(mesh):
    return jax.shard_map(
        per_device,
        mesh=mesh,
        in_specs=(
            P("line", None),
            P("line"),
            P(("groups", "line")),
            P(("groups", "line")),
            P(("groups", "line"), None),
            P(("groups", "line")),
        ),
        out_specs=(P(("groups", "line"), None), P(("groups", "line")), P(("groups", "line"), None)),
        check_vma=False,
    )
```

```python
import functools
import math

import jax
import jax.numpy as jnp
from jax import lax
from jax.experimental import pallas as pl
from jax.experimental.pallas import tpu as pltpu
from jax.sharding import PartitionSpec as P

F32 = jnp.float32
BF16 = jnp.bfloat16
CHUNK = 32


def iota(shape, dim, dtype=jnp.int32):
    return lax.broadcasted_iota(jnp.int32, shape, dim).astype(dtype)


def split3(x):
    top = x.astype(BF16).astype(F32)
    rest = x - top
    middle = rest.astype(BF16).astype(F32)
    return top, middle, rest - middle


def pack_kernel(
    first_ref, counts_ref, lodf_ref, base_ref, limits_ref, second_ref, out_ref, ids_ref
):
    width = lodf_ref.shape[0]
    firsts, cands = second_ref.shape
    peers = out_ref.shape[0]
    anchor = lax.axis_index("line") * width
    square = lodf_ref[:, pl.ds(pl.multiple_of(anchor, width), width)]
    row = iota((firsts, width), 0)
    lane = iota((firsts, width), 1)
    head = jnp.zeros((firsts, width), jnp.int32)
    lives = jnp.zeros((firsts, cands), jnp.int32)
    heads_row = jnp.full((1, width), -1.0, F32)
    place = iota((1, width), 1)
    for j in range(firsts):
        local = first_ref[j] - anchor
        head = jnp.where(row == j, local, head)
        lives = jnp.where(iota((firsts, cands), 0) == j, counts_ref[j], lives)
        heads_row = jnp.where(
            (place == j) | (place == j + firsts), local.astype(F32), heads_row
        )
    hot = (lane == head).astype(BF16)
    first_row = jnp.dot(hot, square, preferred_element_type=F32)
    first_column = lax.dot_general(
        hot, square, (((1,), (1,)), ((), ())), preferred_element_type=F32
    )
    ids = jnp.where(iota((firsts, cands), 1) < lives, second_ref[...] - anchor, -1)
    ids_ref[...] = ids
    ones = jnp.ones((firsts, cands), BF16)
    line = iota((width, cands), 0)
    mult = jnp.zeros((firsts, width), F32)
    for j in range(firsts):
        named = (line == ids[j : j + 1]).astype(F32).astype(BF16)
        times = lax.dot_general(
            ones, named, (((1,), (1,)), ((), ())), preferred_element_type=F32
        )
        mult = jnp.where(row == j, times, mult)
    top, middle, low = split3(base_ref[...])
    limits = limits_ref[...].astype(F32)
    fill = jnp.zeros((firsts - 5, width), F32)
    block = jnp.concatenate(
        [first_row, first_column, mult, top, middle, low, heads_row, limits, fill],
        axis=0,
    )
    block = block.astype(BF16)
    for peer in range(peers):
        out_ref[peer] = block


def screen_kernel(cands, for_pairs, got_ref, lodf_ref, *refs):
    if for_pairs:
        squares_ref, kept_ref, *refs, sem = refs
        keep = pltpu.make_async_copy(got_ref, kept_ref, sem)
        keep.start()
    else:
        pressure_ref, grad_hbm, *refs, grad_ref, grad_sem, sum_ref, mult_ref, lead_ref = refs
    low_ref, high_ref, two_ref, heads_ref, at_head_ref, mix_ref, even_ref, odd_ref = refs
    tiles = got_ref.shape[0]
    width = lodf_ref.shape[0]
    firsts = got_ref.shape[1] // 4
    me = lax.axis_index("line")

    mine = got_ref[me].astype(F32)[3 * firsts :]
    base = mine[0:1] + mine[1:2] + mine[2:3]
    limit = 0.01 * mine[4:5]
    low_ref[...] = jnp.transpose(jnp.broadcast_to(-limit - base, (width, width)))
    high_ref[...] = jnp.transpose(jnp.broadcast_to(limit - base, (width, width)))

    got = got_ref[...].astype(F32)
    shape = (tiles, firsts, width)
    flat = (tiles * firsts, width)
    p = got[:, :firsts].reshape(flat)
    q = got[:, firsts : 2 * firsts].reshape(flat)
    mult = got[:, 2 * firsts : 3 * firsts].reshape(flat)
    tail = got[:, 3 * firsts :]
    flows = jnp.broadcast_to(
        tail[:, 0:1] + tail[:, 1:2] + tail[:, 2:3], shape
    ).reshape(flat)
    own = iota(shape, 2) == iota(shape, 1)
    heads = jnp.sum(
        jnp.where(own, jnp.broadcast_to(tail[:, 3:4], shape), 0.0).reshape(flat),
        axis=1,
        keepdims=True,
    )
    lane = iota(flat, 1, F32)
    first_flow = jnp.sum(jnp.where(lane == heads, flows, 0.0), axis=1, keepdims=True)
    det = 1.0 - p * q
    one = (first_flow + p * flows) / det
    two_ref[...] = (flows + q * first_flow) / det
    if not for_pairs:
        mult_ref[...] = mult
        lead_ref[...] = 2.0 * mult * one
        sum_ref[...] = jnp.zeros_like(sum_ref)
    heads_ref[...] = jnp.broadcast_to(heads, flat)

    pairs = tiles * firsts
    top = one.astype(BF16).astype(F32)
    slot = lax.rem(iota(flat, 0), firsts)
    for j in range(firsts):
        parts = [
            jnp.where(slot == j, part, 0.0).reshape(shape) for part in (top, one - top)
        ]
        mix_ref[:, :, j * width : (j + 1) * width] = jnp.concatenate(
            parts, axis=1
        ).astype(BF16)

    line = iota((width, width), 0, F32)

    @pl.loop(0, tiles, unroll=4)
    def _(tile):
        row = got_ref[tile].astype(F32)[3 * firsts + 3 : 3 * firsts + 4]
        hot = (line == row).astype(F32).astype(BF16)
        span = pl.ds(pl.multiple_of(tile * width, width), width)
        at_head_ref[tile] = jnp.dot(
            lodf_ref[:, span], hot, preferred_element_type=F32
        ).astype(BF16)

    chunk = math.gcd(width, 2 * CHUNK if for_pairs else CHUNK)

    def tile_of(step):
        tile = me + step
        return jnp.where(tile >= tiles, tile - tiles, tile)

    def first_terms(couple, out_ref):
        for half in range(2):
            tile = tile_of(2 * couple + half)
            out_ref[half * width : (half + 1) * width, :] = jnp.dot(
                at_head_ref[tile][:, : 2 * firsts],
                mix_ref[tile],
                preferred_element_type=F32,
            )

    def two_tiles(couple, terms_ref, masked):
        one_tile(2 * couple, terms_ref, 0, masked)
        one_tile(2 * couple + 1, terms_ref, width, False)

    def one_tile(step, terms_ref, offset, masked):
        tile = tile_of(step)
        rows = pl.ds(pl.multiple_of(tile * firsts, firsts), firsts)
        span = pl.ds(pl.multiple_of(tile * width, width), width)
        two = two_ref[rows, :]
        first = heads_ref[rows, :]
        if not for_pairs:
            twice = 2.0 * two
            mult = mult_ref[rows, :]
            lead = lead_ref[rows, :]
        squares = [jnp.zeros((8, width), F32)] * firsts
        lane = iota((chunk, width), 1, F32)
        for start in range(0, width, chunk):
            lines = slice(start, start + chunk)
            factors = lodf_ref[lines, span].astype(F32)
            low = low_ref[lines]
            high = high_ref[lines]
            if not for_pairs:
                total = sum_ref[lines]
                grad = jnp.zeros((chunk, width), F32)
            for j in range(firsts):
                pick = slice(j, j + 1)
                head = jnp.broadcast_to(first[pick], (chunk, width))
                change = (
                    terms_ref[
                        offset + start : offset + start + chunk,
                        j * width : (j + 1) * width,
                    ]
                    + factors * two[pick]
                )
                excess = change - jnp.minimum(jnp.maximum(change, low), high)
                if masked:
                    line = (iota((chunk, width), 0) + start).astype(F32)
                    excess = jnp.where((line == lane) | (line == head), 0.0, excess)
                if for_pairs:
                    squares[j] = squares[j] + jnp.sum(
                        (excess * excess).reshape(chunk // 8, 8, width), axis=0
                    )
                    continue
                total = total + excess * mult[pick]
                weighted = (excess * twice[pick]).astype(BF16).astype(F32)
                grad = grad + weighted * mult[pick]
                first_part = jnp.sum(excess * lead[pick], axis=1, keepdims=True)
                grad = grad + jnp.where(lane == head, first_part, 0.0)
            if not for_pairs:
                sum_ref[lines] = total
                grad_ref[lines, span] = (grad * (1.0 / cands)).astype(BF16)
        if for_pairs:
            squares_ref[tile] = (
                jnp.concatenate(
                    [jnp.sum(part, axis=0, keepdims=True) for part in squares], axis=0
                )
                * (1.0 / (tiles * width))
            ).astype(BF16)
        else:
            pltpu.make_async_copy(
                grad_ref.at[:, span], grad_hbm.at[:, span], grad_sem
            ).start()

    first_terms(0, even_ref)
    first_terms(1, odd_ref)
    two_tiles(0, even_ref, True)

    @pl.loop(0, tiles // 4 - 1)
    def _(turn):
        couple = 2 * turn + 1
        first_terms(couple + 1, even_ref)
        two_tiles(couple, odd_ref, False)
        first_terms(couple + 2, odd_ref)
        two_tiles(couple + 1, even_ref, False)

    two_tiles(tiles // 2 - 1, odd_ref, False)

    if for_pairs:
        keep.wait()
        return
    pressure_ref[...] = jnp.sum(jnp.transpose(sum_ref[...]), axis=0, keepdims=True) * (
        2.0 / (tiles * firsts * cands)
    )
    pltpu.make_async_copy(grad_ref, grad_hbm, grad_sem).wait()


def penalty_kernel(sums_ref, ids_ref, out_ref):
    sums = jnp.sum(sums_ref[...].astype(F32), axis=0)
    ids = ids_ref[...]
    found = jnp.take_along_axis(sums, jnp.maximum(ids, 0), axis=1)
    out_ref[...] = jnp.where(ids >= 0, found, 0.0)


def per_device(lodf, limits, base_flow, first_ids, second_ids, counts):
    width, lines = lodf.shape
    firsts, cands = second_ids.shape
    tiles = lax.axis_size("line")
    vmem = pl.BlockSpec(memory_space=pltpu.VMEM)
    smem = pl.BlockSpec(memory_space=pltpu.SMEM)
    hbm = pl.BlockSpec(memory_space=pl.ANY)
    base = base_flow.reshape(1, width)
    packed, ids = pl.pallas_call(
        pack_kernel,
        out_shape=(
            pltpu.VMEM((tiles, 4 * firsts, width), BF16),
            pltpu.VMEM((firsts, cands), jnp.int32),
        ),
        in_specs=[smem, smem, vmem, vmem, vmem, vmem],
        out_specs=(vmem, vmem),
        name="pack_pairs",
    )(first_ids, counts, lodf, base, limits.reshape(1, width), second_ids)
    got = lax.all_to_all(packed, "line", split_axis=0, concat_axis=0, tiled=True)
    pairs = tiles * firsts
    scratch = [
        pltpu.VMEM((width, width), F32),
        pltpu.VMEM((width, width), F32),
        pltpu.VMEM((pairs, width), F32),
        pltpu.VMEM((pairs, width), F32),
        pltpu.VMEM((tiles, width, width), BF16),
        pltpu.VMEM((tiles, 2 * firsts, firsts * width), BF16),
        pltpu.VMEM((2 * width, firsts * width), F32),
        pltpu.VMEM((2 * width, firsts * width), F32),
    ]
    params = pltpu.CompilerParams(vmem_limit_bytes=32 * 1024 * 1024)
    cost = pl.CostEstimate(
        flops=16 * width * width * pairs,
        bytes_accessed=4 * width * lines,
        transcendentals=0,
    )
    squares, kept = pl.pallas_call(
        functools.partial(screen_kernel, cands, True),
        out_shape=(
            pltpu.VMEM((tiles, firsts, width), BF16),
            jax.ShapeDtypeStruct(got.shape, BF16),
        ),
        in_specs=[vmem] * 2,
        out_specs=(vmem, hbm),
        scratch_shapes=scratch + [pltpu.SemaphoreType.DMA],
        compiler_params=params,
        cost_estimate=cost,
        name="screen_pairs",
    )(got, lodf)
    sums = lax.all_to_all(squares, "line", split_axis=0, concat_axis=0, tiled=True)
    pressure, grad = pl.pallas_call(
        functools.partial(screen_kernel, cands, False),
        out_shape=(
            jax.ShapeDtypeStruct((1, width), F32),
            jax.ShapeDtypeStruct((width, lines), BF16),
        ),
        in_specs=[vmem] * 2,
        out_specs=(vmem, hbm),
        scratch_shapes=scratch
        + [
            pltpu.VMEM((width, lines), BF16),
            pltpu.SemaphoreType.DMA,
            pltpu.VMEM((width, width), F32),
            pltpu.VMEM((pairs, width), F32),
            pltpu.VMEM((pairs, width), F32),
        ],
        compiler_params=params,
        cost_estimate=cost,
        name="screen_lines",
    )(kept, lodf)
    pair_penalty = pl.pallas_call(
        penalty_kernel,
        out_shape=jax.ShapeDtypeStruct((firsts, cands), F32),
        in_specs=[vmem, vmem],
        out_specs=vmem,
        compiler_params=pltpu.CompilerParams(vmem_limit_bytes=16 * 1024 * 1024),
        name="look_up",
    )(sums, ids)
    return (pair_penalty, pressure.reshape(width), grad)


def solution(mesh):
    return jax.shard_map(
        per_device,
        mesh=mesh,
        in_specs=(
            P("line", None),
            P("line"),
            P(("groups", "line")),
            P(("groups", "line")),
            P(("groups", "line"), None),
            P(("groups", "line")),
        ),
        out_specs=(P(("groups", "line"), None), P(("groups", "line")), P(("groups", "line"), None)),
        check_vma=False,
    )
```

```python
import functools
import math

import jax
import jax.numpy as jnp
from jax import lax
from jax.experimental import pallas as pl
from jax.experimental.pallas import tpu as pltpu
from jax.sharding import PartitionSpec as P

F32 = jnp.float32
BF16 = jnp.bfloat16
CHUNK = 32


def iota(shape, dim, dtype=jnp.int32):
    return lax.broadcasted_iota(jnp.int32, shape, dim).astype(dtype)


def split3(x):
    top = x.astype(BF16).astype(F32)
    rest = x - top
    middle = rest.astype(BF16).astype(F32)
    return top, middle, rest - middle


def pack_kernel(
    first_ref, counts_ref, lodf_ref, base_ref, limits_ref, second_ref, out_ref, ids_ref
):
    width = lodf_ref.shape[0]
    firsts, cands = second_ref.shape
    peers = out_ref.shape[0]
    anchor = lax.axis_index("line") * width
    square = lodf_ref[:, pl.ds(pl.multiple_of(anchor, width), width)]
    row = iota((firsts, width), 0)
    lane = iota((firsts, width), 1)
    head = jnp.zeros((firsts, width), jnp.int32)
    lives = jnp.zeros((firsts, cands), jnp.int32)
    heads_row = jnp.zeros((1, width), F32)
    for j in range(firsts):
        local = first_ref[j] - anchor
        head = jnp.where(row == j, local, head)
        lives = jnp.where(iota((firsts, cands), 0) == j, counts_ref[j], lives)
        heads_row = jnp.where(iota((1, width), 1) == j, local.astype(F32), heads_row)
    hot = (lane == head).astype(BF16)
    first_row = jnp.dot(hot, square, preferred_element_type=F32)
    first_column = lax.dot_general(
        hot, square, (((1,), (1,)), ((), ())), preferred_element_type=F32
    )
    ids = jnp.where(iota((firsts, cands), 1) < lives, second_ref[...] - anchor, -1)
    ids_ref[...] = ids
    ones = jnp.ones((firsts, cands), BF16)
    line = iota((width, cands), 0)
    mult = jnp.zeros((firsts, width), F32)
    for j in range(firsts):
        named = (line == ids[j : j + 1]).astype(F32).astype(BF16)
        times = lax.dot_general(
            ones, named, (((1,), (1,)), ((), ())), preferred_element_type=F32
        )
        mult = jnp.where(row == j, times, mult)
    top, middle, low = split3(base_ref[...])
    limits = limits_ref[...].astype(F32)
    fill = jnp.zeros((firsts - 5, width), F32)
    block = jnp.concatenate(
        [first_row, first_column, mult, top, middle, low, heads_row, limits, fill],
        axis=0,
    )
    block = block.astype(BF16)
    for peer in range(peers):
        out_ref[peer] = block


def screen_kernel(cands, for_pairs, got_ref, lodf_ref, *refs):
    if for_pairs:
        squares_ref, kept_ref, *refs, sem = refs
        keep = pltpu.make_async_copy(got_ref, kept_ref, sem)
        keep.start()
    else:
        pressure_ref, grad_hbm, *refs, grad_ref, grad_sem, sum_ref, mult_ref, lead_ref = refs
    low_ref, high_ref, two_ref, heads_ref, at_head_ref, mix_ref, even_ref, odd_ref = refs
    tiles = got_ref.shape[0]
    width = lodf_ref.shape[0]
    firsts = got_ref.shape[1] // 4
    me = lax.axis_index("line")

    mine = got_ref[me].astype(F32)[3 * firsts :]
    base = mine[0:1] + mine[1:2] + mine[2:3]
    limit = 0.01 * mine[4:5]
    low_ref[...] = jnp.transpose(jnp.broadcast_to(-limit - base, (width, width)))
    high_ref[...] = jnp.transpose(jnp.broadcast_to(limit - base, (width, width)))

    got = got_ref[...].astype(F32)
    shape = (tiles, firsts, width)
    flat = (tiles * firsts, width)
    p = got[:, :firsts].reshape(flat)
    q = got[:, firsts : 2 * firsts].reshape(flat)
    mult = got[:, 2 * firsts : 3 * firsts].reshape(flat)
    tail = got[:, 3 * firsts :]
    flows = jnp.broadcast_to(
        tail[:, 0:1] + tail[:, 1:2] + tail[:, 2:3], shape
    ).reshape(flat)
    own = iota(shape, 2) == iota(shape, 1)
    heads = jnp.sum(
        jnp.where(own, jnp.broadcast_to(tail[:, 3:4], shape), 0.0).reshape(flat),
        axis=1,
        keepdims=True,
    )
    lane = iota(flat, 1, F32)
    first_flow = jnp.sum(jnp.where(lane == heads, flows, 0.0), axis=1, keepdims=True)
    det = 1.0 - p * q
    one = (first_flow + p * flows) / det
    two_ref[...] = (flows + q * first_flow) / det
    if not for_pairs:
        mult_ref[...] = mult
        lead_ref[...] = 2.0 * mult * one
        sum_ref[...] = jnp.zeros_like(sum_ref)
    heads_ref[...] = jnp.broadcast_to(heads, flat)

    pairs = tiles * firsts
    top = one.astype(BF16).astype(F32)
    slot = lax.rem(iota(flat, 0), firsts)
    for j in range(firsts):
        span = slice(j * width, (j + 1) * width)
        mix_ref[:pairs, span] = jnp.where(slot == j, top, 0.0).astype(BF16)
        mix_ref[pairs:, span] = jnp.where(slot == j, one - top, 0.0).astype(BF16)

    line_of = jnp.broadcast_to(heads, flat) + width * lax.div(
        iota(flat, 0), firsts
    ).astype(F32)
    line_row = jnp.transpose(line_of)[0:1]
    block = 4 * width
    at_head_ref[...] = jnp.zeros_like(at_head_ref)

    @pl.loop(0, tiles // 4, unroll=4)
    def _(step):
        start = pl.multiple_of(step * block, block)
        here = line_row - start.astype(F32)
        hot = (iota((block, pairs), 0, F32) == here).astype(F32).astype(BF16)
        at_head_ref[...] += jnp.dot(
            lodf_ref[:, pl.ds(start, block)], hot, preferred_element_type=F32
        )

    chunk = math.gcd(width, 2 * CHUNK if for_pairs else CHUNK)

    def tile_of(step):
        tile = me + step
        return jnp.where(tile >= tiles, tile - tiles, tile)

    stack = math.gcd(tiles // 2, 4 if for_pairs else 2)

    def first_terms(group, out_ref):
        parts = []
        for place in range(stack):
            tile = tile_of(stack * group + place)
            place = iota((width, pairs), 1) - tile * firsts
            part = jnp.where((place >= 0) & (place < firsts), at_head_ref[...], 0.0)
            parts.append(part.astype(BF16))
        part = jnp.concatenate(parts, axis=0)
        out_ref[...] = jnp.dot(
            jnp.concatenate([part, part], axis=1),
            mix_ref[...],
            preferred_element_type=F32,
        )

    def some_tiles(group, terms_ref, masked):
        for place in range(stack):
            one_tile(
                stack * group + place, terms_ref, place * width, masked and place == 0
            )

    def one_tile(step, terms_ref, offset, masked):
        tile = tile_of(step)
        rows = pl.ds(pl.multiple_of(tile * firsts, firsts), firsts)
        span = pl.ds(pl.multiple_of(tile * width, width), width)
        two = two_ref[rows, :]
        first = heads_ref[rows, :]
        if not for_pairs:
            twice = 2.0 * two
            mult = mult_ref[rows, :]
            lead = lead_ref[rows, :]
        squares = [jnp.zeros((8, width), F32)] * firsts
        lane = iota((chunk, width), 1, F32)
        for start in range(0, width, chunk):
            lines = slice(start, start + chunk)
            factors = lodf_ref[lines, span].astype(F32)
            low = low_ref[lines]
            high = high_ref[lines]
            if not for_pairs:
                total = sum_ref[lines]
                grad = jnp.zeros((chunk, width), F32)
            for j in range(firsts):
                pick = slice(j, j + 1)
                head = jnp.broadcast_to(first[pick], (chunk, width))
                change = (
                    terms_ref[
                        offset + start : offset + start + chunk,
                        j * width : (j + 1) * width,
                    ]
                    + factors * two[pick]
                )
                excess = change - jnp.minimum(jnp.maximum(change, low), high)
                if masked:
                    line = (iota((chunk, width), 0) + start).astype(F32)
                    excess = jnp.where((line == lane) | (line == head), 0.0, excess)
                if for_pairs:
                    squares[j] = squares[j] + jnp.sum(
                        (excess * excess).reshape(chunk // 8, 8, width), axis=0
                    )
                    continue
                total = total + excess * mult[pick]
                weighted = (excess * twice[pick]).astype(BF16).astype(F32)
                grad = grad + weighted * mult[pick]
                first_part = jnp.sum(excess * lead[pick], axis=1, keepdims=True)
                grad = grad + jnp.where(lane == head, first_part, 0.0)
            if not for_pairs:
                sum_ref[lines] = total
                grad_ref[lines, span] = (grad * (1.0 / cands)).astype(BF16)
        if for_pairs:
            squares_ref[tile] = (
                jnp.concatenate(
                    [jnp.sum(part, axis=0, keepdims=True) for part in squares], axis=0
                )
                * (1.0 / (tiles * width))
            ).astype(BF16)
        else:
            pltpu.make_async_copy(
                grad_ref.at[:, span], grad_hbm.at[:, span], grad_sem
            ).start()

    first_terms(0, even_ref)
    first_terms(1, odd_ref)
    some_tiles(0, even_ref, True)

    @pl.loop(0, tiles // (2 * stack) - 1)
    def _(turn):
        group = 2 * turn + 1
        first_terms(group + 1, even_ref)
        some_tiles(group, odd_ref, False)
        first_terms(group + 2, odd_ref)
        some_tiles(group + 1, even_ref, False)

    some_tiles(tiles // stack - 1, odd_ref, False)

    if for_pairs:
        keep.wait()
        return
    pressure_ref[...] = jnp.sum(jnp.transpose(sum_ref[...]), axis=0, keepdims=True) * (
        2.0 / (tiles * firsts * cands)
    )
    pltpu.make_async_copy(grad_ref, grad_hbm, grad_sem).wait()


def penalty_kernel(sums_ref, ids_ref, out_ref):
    sums = jnp.sum(sums_ref[...].astype(F32), axis=0)
    ids = ids_ref[...]
    found = jnp.take_along_axis(sums, jnp.maximum(ids, 0), axis=1)
    out_ref[...] = jnp.where(ids >= 0, found, 0.0)


def per_device(lodf, limits, base_flow, first_ids, second_ids, counts):
    width, lines = lodf.shape
    firsts, cands = second_ids.shape
    tiles = lax.axis_size("line")
    vmem = pl.BlockSpec(memory_space=pltpu.VMEM)
    smem = pl.BlockSpec(memory_space=pltpu.SMEM)
    hbm = pl.BlockSpec(memory_space=pl.ANY)
    base = base_flow.reshape(1, width)
    packed, ids = pl.pallas_call(
        pack_kernel,
        out_shape=(
            pltpu.VMEM((tiles, 4 * firsts, width), BF16),
            pltpu.VMEM((firsts, cands), jnp.int32),
        ),
        in_specs=[smem, smem, vmem, vmem, vmem, vmem],
        out_specs=(vmem, vmem),
        name="pack_pairs",
    )(first_ids, counts, lodf, base, limits.reshape(1, width), second_ids)
    got = lax.all_to_all(packed, "line", split_axis=0, concat_axis=0, tiled=True)
    pairs = tiles * firsts
    scratch = [
        pltpu.VMEM((width, width), F32),
        pltpu.VMEM((width, width), F32),
        pltpu.VMEM((pairs, width), F32),
        pltpu.VMEM((pairs, width), F32),
        pltpu.VMEM((width, pairs), F32),
        pltpu.VMEM((2 * pairs, firsts * width), BF16),
    ]
    terms = [
        [pltpu.VMEM((stack * width, firsts * width), F32)] * 2
        for stack in (math.gcd(tiles // 2, 4), math.gcd(tiles // 2, 2))
    ]
    params = pltpu.CompilerParams(vmem_limit_bytes=32 * 1024 * 1024)
    cost = pl.CostEstimate(
        flops=16 * width * width * pairs,
        bytes_accessed=4 * width * lines,
        transcendentals=0,
    )
    squares, kept = pl.pallas_call(
        functools.partial(screen_kernel, cands, True),
        out_shape=(
            pltpu.VMEM((tiles, firsts, width), BF16),
            jax.ShapeDtypeStruct(got.shape, BF16),
        ),
        in_specs=[vmem] * 2,
        out_specs=(vmem, hbm),
        scratch_shapes=scratch + terms[0] + [pltpu.SemaphoreType.DMA],
        compiler_params=params,
        cost_estimate=cost,
        name="screen_pairs",
    )(got, lodf)
    sums = lax.all_to_all(squares, "line", split_axis=0, concat_axis=0, tiled=True)
    pressure, grad = pl.pallas_call(
        functools.partial(screen_kernel, cands, False),
        out_shape=(
            jax.ShapeDtypeStruct((1, width), F32),
            jax.ShapeDtypeStruct((width, lines), BF16),
        ),
        in_specs=[vmem] * 2,
        out_specs=(vmem, hbm),
        scratch_shapes=scratch
        + terms[1]
        + [
            pltpu.VMEM((width, lines), BF16),
            pltpu.SemaphoreType.DMA,
            pltpu.VMEM((width, width), F32),
            pltpu.VMEM((pairs, width), F32),
            pltpu.VMEM((pairs, width), F32),
        ],
        compiler_params=params,
        cost_estimate=cost,
        name="screen_lines",
    )(kept, lodf)
    pair_penalty = pl.pallas_call(
        penalty_kernel,
        out_shape=jax.ShapeDtypeStruct((firsts, cands), F32),
        in_specs=[vmem, vmem],
        out_specs=vmem,
        compiler_params=pltpu.CompilerParams(vmem_limit_bytes=16 * 1024 * 1024),
        name="look_up",
    )(sums, ids)
    return (pair_penalty, pressure.reshape(width), grad)


def solution(mesh):
    return jax.shard_map(
        per_device,
        mesh=mesh,
        in_specs=(
            P("line", None),
            P("line"),
            P(("groups", "line")),
            P(("groups", "line")),
            P(("groups", "line"), None),
            P(("groups", "line")),
        ),
        out_specs=(P(("groups", "line"), None), P(("groups", "line")), P(("groups", "line"), None)),
        check_vma=False,
    )
```

```python
import functools
import math

import jax
import jax.numpy as jnp
from jax import lax
from jax.experimental import pallas as pl
from jax.experimental.pallas import tpu as pltpu
from jax.sharding import PartitionSpec as P

F32 = jnp.float32
BF16 = jnp.bfloat16
CHUNK = 32


def iota(shape, dim, dtype=jnp.int32):
    return lax.broadcasted_iota(jnp.int32, shape, dim).astype(dtype)


def split3(x):
    top = x.astype(BF16).astype(F32)
    rest = x - top
    middle = rest.astype(BF16).astype(F32)
    return top, middle, rest - middle


def pack_kernel(
    first_ref, counts_ref, lodf_ref, base_ref, limits_ref, second_ref, out_ref, ids_ref
):
    width = lodf_ref.shape[0]
    firsts, cands = second_ref.shape
    peers = out_ref.shape[0]
    anchor = lax.axis_index("line") * width
    square = lodf_ref[:, pl.ds(pl.multiple_of(anchor, width), width)]
    row = iota((firsts, width), 0)
    lane = iota((firsts, width), 1)
    head = jnp.zeros((firsts, width), jnp.int32)
    lives = jnp.zeros((firsts, cands), jnp.int32)
    heads_row = jnp.zeros((1, width), F32)
    for j in range(firsts):
        local = first_ref[j] - anchor
        head = jnp.where(row == j, local, head)
        lives = jnp.where(iota((firsts, cands), 0) == j, counts_ref[j], lives)
        heads_row = jnp.where(iota((1, width), 1) == j, local.astype(F32), heads_row)
    hot = (lane == head).astype(BF16)
    first_row = jnp.dot(hot, square, preferred_element_type=F32)
    first_column = lax.dot_general(
        hot, square, (((1,), (1,)), ((), ())), preferred_element_type=F32
    )
    ids = jnp.where(iota((firsts, cands), 1) < lives, second_ref[...] - anchor, -1)
    ids_ref[...] = ids
    ones = jnp.ones((firsts, cands), BF16)
    line = iota((width, cands), 0)
    mult = jnp.zeros((firsts, width), F32)
    for j in range(firsts):
        named = (line == ids[j : j + 1]).astype(F32).astype(BF16)
        times = lax.dot_general(
            ones, named, (((1,), (1,)), ((), ())), preferred_element_type=F32
        )
        mult = jnp.where(row == j, times, mult)
    top, middle, low = split3(base_ref[...])
    limits = limits_ref[...].astype(F32)
    fill = jnp.zeros((firsts - 5, width), F32)
    block = jnp.concatenate(
        [first_row, first_column, mult, top, middle, low, heads_row, limits, fill],
        axis=0,
    )
    block = block.astype(BF16)
    for peer in range(peers):
        out_ref[peer] = block


def screen_kernel(cands, for_pairs, got_ref, lodf_ref, *refs):
    if for_pairs:
        squares_ref, kept_ref, *refs, sem = refs
        keep = pltpu.make_async_copy(got_ref, kept_ref, sem)
        keep.start()
    else:
        pressure_ref, grad_hbm, *refs, grad_ref, grad_sem, sum_ref, mult_ref, lead_ref = refs
    low_ref, high_ref, two_ref, heads_ref, at_head_ref, mix_ref, even_ref, odd_ref = refs
    tiles = got_ref.shape[0]
    width = lodf_ref.shape[0]
    firsts = got_ref.shape[1] // 4
    me = lax.axis_index("line")

    mine = got_ref[me].astype(F32)[3 * firsts :]
    base = mine[0:1] + mine[1:2] + mine[2:3]
    limit = 0.01 * mine[4:5]
    low_ref[...] = jnp.transpose(jnp.broadcast_to(-limit - base, (width, width)))
    high_ref[...] = jnp.transpose(jnp.broadcast_to(limit - base, (width, width)))

    got = got_ref[...].astype(F32)
    shape = (tiles, firsts, width)
    flat = (tiles * firsts, width)
    p = got[:, :firsts].reshape(flat)
    q = got[:, firsts : 2 * firsts].reshape(flat)
    mult = got[:, 2 * firsts : 3 * firsts].reshape(flat)
    tail = got[:, 3 * firsts :]
    flows = jnp.broadcast_to(
        tail[:, 0:1] + tail[:, 1:2] + tail[:, 2:3], shape
    ).reshape(flat)
    own = iota(shape, 2) == iota(shape, 1)
    heads = jnp.sum(
        jnp.where(own, jnp.broadcast_to(tail[:, 3:4], shape), 0.0).reshape(flat),
        axis=1,
        keepdims=True,
    )
    lane = iota(flat, 1, F32)
    first_flow = jnp.sum(jnp.where(lane == heads, flows, 0.0), axis=1, keepdims=True)
    det = 1.0 - p * q
    one = (first_flow + p * flows) / det
    two_ref[...] = (flows + q * first_flow) / det
    if not for_pairs:
        mult_ref[...] = mult
        lead_ref[...] = 2.0 * mult * one
        sum_ref[...] = jnp.zeros_like(sum_ref)
    heads_ref[...] = jnp.broadcast_to(heads, flat)

    pairs = tiles * firsts
    top = one.astype(BF16).astype(F32)
    slot = lax.rem(iota(flat, 0), firsts)
    for j in range(firsts):
        span = slice(j * width, (j + 1) * width)
        mix_ref[:pairs, span] = jnp.where(slot == j, top, 0.0).astype(BF16)
        mix_ref[pairs:, span] = jnp.where(slot == j, one - top, 0.0).astype(BF16)

    line_of = jnp.broadcast_to(heads, flat) + width * lax.div(
        iota(flat, 0), firsts
    ).astype(F32)
    line_row = jnp.transpose(line_of)[0:1]
    block = 4 * width
    at_head_ref[...] = jnp.zeros_like(at_head_ref)

    @pl.loop(0, tiles // 4, unroll=4)
    def _(step):
        start = pl.multiple_of(step * block, block)
        here = line_row - start.astype(F32)
        hot = (iota((block, pairs), 0, F32) == here).astype(F32).astype(BF16)
        at_head_ref[...] += jnp.dot(
            lodf_ref[:, pl.ds(start, block)], hot, preferred_element_type=F32
        )

    chunk = math.gcd(width, 2 * CHUNK if for_pairs else CHUNK)

    def tile_of(step):
        tile = me + step
        return jnp.where(tile >= tiles, tile - tiles, tile)

    stack = math.gcd(tiles // 2, 4)

    def first_terms(group, out_ref):
        parts = []
        for place in range(stack):
            tile = tile_of(stack * group + place)
            place = iota((width, pairs), 1) - tile * firsts
            part = jnp.where((place >= 0) & (place < firsts), at_head_ref[...], 0.0)
            parts.append(part.astype(BF16))
        part = jnp.concatenate(parts, axis=0)
        out_ref[...] = jnp.dot(
            jnp.concatenate([part, part], axis=1),
            mix_ref[...],
            preferred_element_type=F32,
        )

    def some_tiles(group, terms_ref, masked):
        for place in range(stack):
            one_tile(
                stack * group + place, terms_ref, place * width, masked and place == 0
            )

    def one_tile(step, terms_ref, offset, masked):
        tile = tile_of(step)
        rows = pl.ds(pl.multiple_of(tile * firsts, firsts), firsts)
        span = pl.ds(pl.multiple_of(tile * width, width), width)
        two = two_ref[rows, :]
        first = heads_ref[rows, :]
        if not for_pairs:
            twice = 2.0 * two
            mult = mult_ref[rows, :]
            lead = lead_ref[rows, :]
        squares = [jnp.zeros((8, width), F32)] * firsts
        lane = iota((chunk, width), 1, F32)
        for start in range(0, width, chunk):
            lines = slice(start, start + chunk)
            factors = lodf_ref[lines, span].astype(F32)
            low = low_ref[lines]
            high = high_ref[lines]
            if not for_pairs:
                total = sum_ref[lines]
                grad = jnp.zeros((chunk, width), F32)
            for j in range(firsts):
                pick = slice(j, j + 1)
                head = jnp.broadcast_to(first[pick], (chunk, width))
                change = (
                    terms_ref[
                        offset + start : offset + start + chunk,
                        j * width : (j + 1) * width,
                    ]
                    + factors * two[pick]
                )
                excess = change - jnp.minimum(jnp.maximum(change, low), high)
                if masked:
                    line = (iota((chunk, width), 0) + start).astype(F32)
                    excess = jnp.where((line == lane) | (line == head), 0.0, excess)
                if for_pairs:
                    squares[j] = squares[j] + jnp.sum(
                        (excess * excess).reshape(chunk // 8, 8, width), axis=0
                    )
                    continue
                total = total + excess * mult[pick]
                weighted = (excess * twice[pick]).astype(BF16).astype(F32)
                grad = grad + weighted * mult[pick]
                first_part = jnp.sum(excess * lead[pick], axis=1, keepdims=True)
                grad = grad + jnp.where(lane == head, first_part, 0.0)
            if not for_pairs:
                sum_ref[lines] = total
                grad_ref[lines, span] = (grad * (1.0 / cands)).astype(BF16)
        if for_pairs:
            squares_ref[tile] = (
                jnp.concatenate(
                    [jnp.sum(part, axis=0, keepdims=True) for part in squares], axis=0
                )
                * (1.0 / (tiles * width))
            ).astype(BF16)
        else:
            pltpu.make_async_copy(
                grad_ref.at[:, span], grad_hbm.at[:, span], grad_sem
            ).start()

    first_terms(0, even_ref)
    first_terms(1, odd_ref)
    some_tiles(0, even_ref, True)

    @pl.loop(0, tiles // (2 * stack) - 1)
    def _(turn):
        group = 2 * turn + 1
        first_terms(group + 1, even_ref)
        some_tiles(group, odd_ref, False)
        first_terms(group + 2, odd_ref)
        some_tiles(group + 1, even_ref, False)

    some_tiles(tiles // stack - 1, odd_ref, False)

    if for_pairs:
        keep.wait()
        return
    pressure_ref[...] = jnp.sum(jnp.transpose(sum_ref[...]), axis=0, keepdims=True) * (
        2.0 / (tiles * firsts * cands)
    )
    pltpu.make_async_copy(grad_ref, grad_hbm, grad_sem).wait()


def penalty_kernel(sums_ref, ids_ref, out_ref):
    sums = jnp.sum(sums_ref[...].astype(F32), axis=0)
    ids = ids_ref[...]
    found = jnp.take_along_axis(sums, jnp.maximum(ids, 0), axis=1)
    out_ref[...] = jnp.where(ids >= 0, found, 0.0)


def per_device(lodf, limits, base_flow, first_ids, second_ids, counts):
    width, lines = lodf.shape
    firsts, cands = second_ids.shape
    tiles = lax.axis_size("line")
    vmem = pl.BlockSpec(memory_space=pltpu.VMEM)
    smem = pl.BlockSpec(memory_space=pltpu.SMEM)
    hbm = pl.BlockSpec(memory_space=pl.ANY)
    base = base_flow.reshape(1, width)
    packed, ids = pl.pallas_call(
        pack_kernel,
        out_shape=(
            pltpu.VMEM((tiles, 4 * firsts, width), BF16),
            pltpu.VMEM((firsts, cands), jnp.int32),
        ),
        in_specs=[smem, smem, vmem, vmem, vmem, vmem],
        out_specs=(vmem, vmem),
        name="pack_pairs",
    )(first_ids, counts, lodf, base, limits.reshape(1, width), second_ids)
    got = lax.all_to_all(packed, "line", split_axis=0, concat_axis=0, tiled=True)
    pairs = tiles * firsts
    scratch = [
        pltpu.VMEM((width, width), F32),
        pltpu.VMEM((width, width), F32),
        pltpu.VMEM((pairs, width), F32),
        pltpu.VMEM((pairs, width), F32),
        pltpu.VMEM((width, pairs), F32),
        pltpu.VMEM((2 * pairs, firsts * width), BF16),
    ]
    scratch += [pltpu.VMEM((math.gcd(tiles // 2, 4) * width, firsts * width), F32)] * 2
    params = pltpu.CompilerParams(vmem_limit_bytes=32 * 1024 * 1024)
    cost = pl.CostEstimate(
        flops=16 * width * width * pairs,
        bytes_accessed=4 * width * lines,
        transcendentals=0,
    )
    squares, kept = pl.pallas_call(
        functools.partial(screen_kernel, cands, True),
        out_shape=(
            pltpu.VMEM((tiles, firsts, width), BF16),
            jax.ShapeDtypeStruct(got.shape, BF16),
        ),
        in_specs=[vmem] * 2,
        out_specs=(vmem, hbm),
        scratch_shapes=scratch + [pltpu.SemaphoreType.DMA],
        compiler_params=params,
        cost_estimate=cost,
        name="screen_pairs",
    )(got, lodf)
    sums = lax.all_to_all(squares, "line", split_axis=0, concat_axis=0, tiled=True)
    pressure, grad = pl.pallas_call(
        functools.partial(screen_kernel, cands, False),
        out_shape=(
            jax.ShapeDtypeStruct((1, width), F32),
            jax.ShapeDtypeStruct((width, lines), BF16),
        ),
        in_specs=[vmem] * 2,
        out_specs=(vmem, hbm),
        scratch_shapes=scratch
        + [
            pltpu.VMEM((width, lines), BF16),
            pltpu.SemaphoreType.DMA,
            pltpu.VMEM((width, width), F32),
            pltpu.VMEM((pairs, width), F32),
            pltpu.VMEM((pairs, width), F32),
        ],
        compiler_params=params,
        cost_estimate=cost,
        name="screen_lines",
    )(kept, lodf)
    pair_penalty = pl.pallas_call(
        penalty_kernel,
        out_shape=jax.ShapeDtypeStruct((firsts, cands), F32),
        in_specs=[vmem, vmem],
        out_specs=vmem,
        compiler_params=pltpu.CompilerParams(vmem_limit_bytes=16 * 1024 * 1024),
        name="look_up",
    )(sums, ids)
    return (pair_penalty, pressure.reshape(width), grad)


def solution(mesh):
    return jax.shard_map(
        per_device,
        mesh=mesh,
        in_specs=(
            P("line", None),
            P("line"),
            P(("groups", "line")),
            P(("groups", "line")),
            P(("groups", "line"), None),
            P(("groups", "line")),
        ),
        out_specs=(P(("groups", "line"), None), P(("groups", "line")), P(("groups", "line"), None)),
        check_vma=False,
    )
```
